32 devices in a mesh: section: 4 (over y, x), dp: 8 (over z, core).
Axes of the slice: x: 2, y: 2, z: 4, core: 2. Of those that a mesh axis runs over, the one named last changes fastest.
Arguments:
- content_in: bfloat16 [2048, 768], P('dp'), may hold values from -6 to 6
- query_in: bfloat16 [2048, 768], P('dp'), may hold values from -6 to 6
- memory: bfloat16 [2, 1024, 768], P(None, 'dp'), may hold values from -6 to 6
- doc_lengths: int32 [16], P('dp'), may hold values from 64 to 128, as said below
- perm_rank: int32 [16, 128], P('dp'), may hold values from 0 to 127, each once within a row
- segment_ids: int32 [16, 128], P('dp'), may hold values from 0 to 3, never falling along the last dimension, each value on 1 to 64 neighbouring positions
- w_query: bfloat16 [2, 768, 768], replicated, may hold values from -0.21875 to 0.21875
- w_keyval: bfloat16 [2, 768, 1536], replicated, may hold values from -0.21875 to 0.21875
- w_out: bfloat16 [2, 768, 768], replicated, may hold values from -0.875 to 0.875
- w_rel: bfloat16 [2, 768, 768], replicated, may hold values from -0.21875 to 0.21875
- head_bias: float32 [2, 3, 768], replicated, may hold values from -3 to 3
- seg_embed: float32 [2, 2, 768], replicated, may hold values from -6 to 6
- attn_gain: float32 [2, 768], replicated, may hold values from 0.25 to 1.75
- attn_shift: float32 [2, 768], replicated, may hold values from -2 to 2
- ffn_in: bfloat16 [2, 768, 3072], replicated, may hold values from -0.21875 to 0.21875
- ffn_in_bias: float32 [2, 3072], replicated, may hold values from -2 to 2
- ffn_out: bfloat16 [2, 3072, 768], replicated, may hold values from -0.109375 to 0.109375
- ffn_out_bias: float32 [2, 768], replicated, may hold values from -2 to 2
- ffn_gain: float32 [2, 768], replicated, may hold values from 0.25 to 1.75
- ffn_shift: float32 [2, 768], replicated, may hold values from -2 to 2
- cot_content: bfloat16 [2048, 768], P('dp'), may hold values from -6 to 6
- cot_query: bfloat16 [2048, 768], P('dp'), may hold values from -6 to 6
Outputs:
- out_content: bfloat16 [2048, 768], P('dp', 'section')
- out_query: bfloat16 [2048, 768], P('dp', 'section')
- grad_content: float32 [2048, 768], P('dp', 'section')
- grad_query: float32 [2048, 768], P('dp', 'section')
- grad_memory: float32 [2, 1024, 768], P(None, 'dp', 'section')
- grad_w_query: float32 [2, 768, 768], P(None, 'section', 'dp')
- grad_w_keyval: float32 [2, 768, 1536], P(None, 'section', 'dp')
- grad_w_out: float32 [2, 768, 768], P(None, 'section', 'dp')
- grad_w_rel: float32 [2, 768, 768], P(None, 'section', 'dp')
- grad_head_bias: float32 [2, 3, 768], P(None, None, 'section')
- grad_seg_embed: float32 [2, 2, 768], P(None, None, 'section')
- grad_attn_gain: float32 [2, 768], P(None, 'section')
- grad_attn_shift: float32 [2, 768], P(None, 'section')
- grad_ffn_in: float32 [2, 768, 3072], P(None, 'section', 'dp')
- grad_ffn_in_bias: float32 [2, 3072], P(None, 'section')
- grad_ffn_out: float32 [2, 3072, 768], P(None, 'section', 'dp')
- grad_ffn_out_bias: float32 [2, 768], P(None, 'section')
- grad_ffn_gain: float32 [2, 768], P(None, 'section')
- grad_ffn_shift: float32 [2, 768], P(None, 'section')
The draws below stay inside these ranges and needn't reach their ends.
Inputs may be any that keep to these rules, and one draw needn't show every extreme that they name: `doc_lengths`: some sequence has exactly 64 rows and some exactly 128. `perm_rank`: each sequence's row is a permutation of 0 to 127. `segment_ids`: never falling along a sequence; each segment 1 to 64 rows long.
All inputs are finite; a program needn't handle non-finite values.
Results may differ from the reference program's by a relative error of at most 0.03.
Values may be sent and summed in bfloat16 or wider, within the bound.
No kernel may reach another device: no remote copies, remote signals or barrier semaphores. Data moves between devices by JAX's collectives and lax.ppermute only.
A program may use at most 320 MiB of HBM per device.

```python
import math
import jax
import jax.numpy as jnp
import numpy as np
from jax import lax

D = 768
HEADS = 12
HEAD = 64
FF = 3072
S = 128
M = 64
LAYERS = 2
LEAST = 64
SEQS = 16
TOKENS = 2048
MEMS = 1024


def draw_doc_lengths(key, part):
    key = jax.random.fold_in(key, 11)
    first_key, second_key = jax.random.split(key)
    lengths = jax.random.randint(first_key, (SEQS,), LEAST, S + 1)
    chosen = jax.random.randint(second_key, (), 0, SEQS)
    lengths = lengths.at[chosen].set(S)
    lengths = lengths.at[(chosen + 1) % SEQS].set(LEAST)
    return lengths.astype(jnp.int32)


def block_scale(own_key, extent, cuts, smallest, high):
    factor_of = 1.0
    for position, blocks in cuts:
        steps = jax.random.uniform(jax.random.fold_in(jax.random.fold_in(own_key, 6), position), (blocks,), jnp.float32, smallest / len(cuts), high / len(cuts))
        factor_of = factor_of * jnp.repeat(jnp.exp(steps), extent[position] // blocks).reshape((-1,) + (1,) * (len(extent) - 1 - position))
    return factor_of


def profile(count, total, reach, lean):
    portions = [(1 << 20) // math.isqrt(grade ** lean) + 1 for grade in range(2, count + 1)]
    rest, counts = total - reach - (count - 1), [1] * (count - 1)
    while rest > 0:
        candidates = [i for i in range(count - 1) if counts[i] < reach]
        whole, left = sum([portions[i] for i in candidates]), rest
        for i in candidates:
            addition = min(reach - counts[i], max(1, left * portions[i] // whole), rest)
            counts[i] = counts[i] + addition
            rest = rest - addition
    return np.array([reach] + counts)


def uneven_parts(key, count, total, most, lean):
    if count == 2:
        one = jax.random.randint(key, (), max(1, total - most), min(most, total - 1) + 1)
        return jnp.stack([one, total - one])
    tallies = jnp.asarray(profile(count, total, most, lean), jnp.int32)
    pairs = (count - 1) // 2
    donor, receiver = tallies[1:1 + 2 * pairs:2], tallies[2:2 + 2 * pairs:2]
    room = jnp.minimum(donor - 1, most - receiver)
    passed = jax.random.randint(jax.random.fold_in(key, 1), (pairs,), 0, 1 << 20) % (room + 1)
    tallies = tallies.at[1:1 + 2 * pairs:2].set(donor - passed).at[2:2 + 2 * pairs:2].set(receiver + passed)
    return tallies[jax.random.permutation(jax.random.fold_in(key, 2), count)]


def gaussian(own_key, shape, deviation, limit, pieces=(), kind=jnp.bfloat16):
    array = jax.random.normal(own_key, shape, jnp.float32) * deviation
    if len(pieces) > 0:
        array = block_scale(own_key, shape, pieces, -0.22, 0.18) * array
    return jnp.clip(array, min=-limit, max=limit).astype(kind)


def setup_inputs(seed: int = 0) -> dict:
    keys = jax.random.split(jax.random.key(seed), 23)
    content_in = gaussian(keys[0], (TOKENS, D), 1.0, 6.0, ((0, 8),))
    query_in = gaussian(keys[1], (TOKENS, D), 1.0, 6.0, ((0, 8),))
    memory = gaussian(keys[2], (LAYERS, MEMS, D), 1.0, 6.0, ((1, 8),))
    doc_lengths = draw_doc_lengths(jax.random.fold_in(keys[22], 71), 0)
    perm_rank = jax.vmap(lambda own: jax.random.permutation(own, S))(jax.random.split(keys[4], SEQS)).reshape((SEQS, S)).astype(jnp.int32)
    segment_ids = jax.vmap(lambda own: jnp.searchsorted(jnp.cumsum(uneven_parts(own, 4, S, S // 2, 2)), jnp.arange(S), side="right"))(jax.random.split(keys[5], SEQS)).reshape((SEQS, S)).astype(jnp.int32)
    w_query = gaussian(keys[6], (LAYERS, D, D), D ** -0.5, 0.21875)
    w_keyval = gaussian(keys[7], (LAYERS, D, 2 * D), D ** -0.5, 0.21875)
    w_out = gaussian(keys[8], (LAYERS, D, D), (max(D // 16, 1)) ** -0.5, 0.875)
    w_rel = gaussian(keys[9], (LAYERS, D, D), D ** -0.5, 0.21875)
    head_bias = gaussian(keys[10], (LAYERS, 3, D), 0.5, 3.0, (), jnp.float32)
    seg_embed = gaussian(keys[11], (LAYERS, 2, D), 1.0, 6.0, (), jnp.float32)
    attn_gain = jnp.clip(1.0 + 0.15 * jax.random.normal(keys[12], (LAYERS, D), jnp.float32), 0.25, 1.75)
    attn_shift = gaussian(keys[13], (LAYERS, D), 0.3, 2.0, (), jnp.float32)
    ffn_in = gaussian(keys[14], (LAYERS, D, FF), D ** -0.5, 0.21875)
    ffn_in_bias = gaussian(keys[15], (LAYERS, FF), 0.3, 2.0, (), jnp.float32)
    ffn_out = gaussian(keys[16], (LAYERS, FF, D), FF ** -0.5, 0.109375)
    ffn_out_bias = gaussian(keys[17], (LAYERS, D), 0.3, 2.0, (), jnp.float32)
    ffn_gain = jnp.clip(1.0 + 0.15 * jax.random.normal(keys[18], (LAYERS, D), jnp.float32), 0.25, 1.75)
    ffn_shift = gaussian(keys[19], (LAYERS, D), 0.3, 2.0, (), jnp.float32)
    cot_content = gaussian(keys[20], (TOKENS, D), 1.0, 6.0, ((0, 8),))
    cot_query = gaussian(keys[21], (TOKENS, D), 1.0, 6.0, ((0, 8),))
    return {"content_in": content_in, "query_in": query_in, "memory": memory, "doc_lengths": doc_lengths, "perm_rank": perm_rank, "segment_ids": segment_ids, "w_query": w_query, "w_keyval": w_keyval, "w_out": w_out, "w_rel": w_rel, "head_bias": head_bias, "seg_embed": seg_embed, "attn_gain": attn_gain, "attn_shift": attn_shift, "ffn_in": ffn_in, "ffn_in_bias": ffn_in_bias, "ffn_out": ffn_out, "ffn_out_bias": ffn_out_bias, "ffn_gain": ffn_gain, "ffn_shift": ffn_shift, "cot_content": cot_content, "cot_query": cot_query}


NEGATIVE = -1e+30
EPSILON = 1e-05
HIGHEST = lax.Precision.HIGHEST

@jax.custom_vjp
def low(v):
    return lax.optimization_barrier(v.astype(jnp.bfloat16)).astype(jnp.float32)

@jax.custom_vjp
def low_back(v):
    return v

def low_keep(v):
    return (low(v), None)

def low_pass(kept, grad):
    return (grad,)

def back_keep(v):
    return (v, None)

def back_low(kept, grad):
    return (low(grad),)
low.defvjp(low_keep, low_pass)
low_back.defvjp(back_keep, back_low)

def send(values):
    return low_back(low(values))

def layer_norm(values, norm_gain, norm_shift):
    centre = values - lax.optimization_barrier(jnp.mean(values, axis=-1, keepdims=True))
    spread = lax.optimization_barrier(jnp.mean(centre * centre, axis=-1, keepdims=True))
    return centre * lax.rsqrt(spread + EPSILON) * norm_gain + norm_shift

def position_table():
    distance = (M + S - 1 - jnp.arange(M + 2 * S - 1)).astype(jnp.float32)
    inverse = jnp.exp(jnp.arange(0, D, 2).astype(jnp.float32) * (-math.log(10000.0) / D))
    angles = distance[:, None] * inverse[None, :]
    return jnp.concatenate([jnp.sin(angles), jnp.cos(angles)], axis=1)

def skew_scores(wide_scores):
    head_count, query_count, table_count = wide_scores.shape
    flattened = wide_scores.reshape(head_count, query_count * table_count)
    taken = flattened[:, query_count - 1:query_count - 1 + query_count * (table_count - 1)]
    return taken.reshape(head_count, query_count, table_count - 1)[:, :, :table_count - query_count + 1]

def attend_sequence(content, query_rows, memory_rows, length, rank_row, segment, weights):
    w_query, w_keyval, w_out, w_rel, head_bias, seg_embed, norm_gain, norm_shift = weights
    score_scale = HEAD ** (-0.5)
    joined = jnp.concatenate([memory_rows, content], axis=0)
    keyval = low(low_back(jnp.dot(joined, w_keyval, precision=HIGHEST)))
    keys_all = keyval[:, :D].reshape(M + S, HEADS, HEAD)
    values_all = keyval[:, D:].reshape(M + S, HEADS, HEAD)
    pos_table = low(position_table())
    relative = low(low_back(jnp.dot(pos_table, w_rel, precision=HIGHEST))).reshape(M + 2 * S - 1, HEADS, HEAD)
    key_place = jnp.arange(M + S)
    key_live = (key_place < M) | (key_place - M < length)
    key_rank = jnp.concatenate([jnp.full((M,), -1, jnp.int32), rank_row.astype(jnp.int32)])
    key_segment = jnp.concatenate([jnp.zeros((M,), jnp.int32), segment.astype(jnp.int32)])
    differs = (segment[:, None] != key_segment[None, :]).astype(jnp.float32)
    see_content = key_live[None, :] & (key_rank[None, :] <= rank_row[:, None])
    see_query = key_live[None, :] & (key_rank[None, :] < rank_row[:, None])
    seg_table = seg_embed.reshape(2, HEADS, HEAD)

    def stream(inputs, visible):
        projected = low_back(jnp.dot(inputs, w_query, precision=HIGHEST))
        with_content = low((projected + head_bias[0]) * score_scale).reshape(S, HEADS, HEAD)
        with_position = low((projected + head_bias[1]) * score_scale).reshape(S, HEADS, HEAD)
        with_segment = ((projected + head_bias[2]) * score_scale).reshape(S, HEADS, HEAD)
        seg_terms = jnp.einsum('she,khe->hsk', with_segment, seg_table, precision=HIGHEST)
        content_part = jnp.einsum('she,khe->hsk', with_content, keys_all, precision=HIGHEST)
        wide_scores = jnp.einsum('she,rhe->hsr', with_position, relative, precision=HIGHEST)
        raw_scores = content_part + skew_scores(wide_scores) + seg_terms[:, :, 0:1] + differs[None] * (seg_terms[:, :, 1:2] - seg_terms[:, :, 0:1])
        scores = low_back(jnp.where(visible[None], raw_scores, NEGATIVE))
        highest = lax.optimization_barrier(jnp.max(scores, axis=-1, keepdims=True))
        exponent = jnp.exp(scores - highest)
        probability = exponent / lax.optimization_barrier(jnp.sum(exponent, axis=-1, keepdims=True))
        mixed = jnp.einsum('hsk,khe->she', low(probability), values_all, precision=HIGHEST).reshape(S, D)
        attended = low(low_back(mixed))
        summed = low_back(jnp.dot(attended, w_out, precision=HIGHEST)) + inputs
        return layer_norm(summed, norm_gain, norm_shift)
    return (stream(content, see_content), stream(query_rows, see_query))

def feed_forward(rows_in, w_in, bias_in, w_back, bias_out, norm_gain, norm_shift):
    hidden_pre = low_back(jnp.dot(rows_in, w_in, precision=HIGHEST) + bias_in)
    activated = low(jax.nn.gelu(hidden_pre, approximate=True))
    summed = low_back(jnp.dot(activated, w_back, precision=HIGHEST)) + bias_out + rows_in
    return layer_norm(summed, norm_gain, norm_shift)

def reference(content_in, query_in, memory, doc_lengths, perm_rank, segment_ids, w_query, w_keyval, w_out, w_rel, head_bias, seg_embed, attn_gain, attn_shift, ffn_in, ffn_in_bias, ffn_out, ffn_out_bias, ffn_gain, ffn_shift, cot_content, cot_query):
    floats = tuple((argument.astype(jnp.float32) for argument in (content_in, query_in, memory, w_query, w_keyval, w_out, w_rel, head_bias, seg_embed, attn_gain, attn_shift, ffn_in, ffn_in_bias, ffn_out, ffn_out_bias, ffn_gain, ffn_shift)))

    def forward(content_arg, query_arg, memory_arg, wq_arg, wkv_arg, wo_arg, wr_arg, hb_arg, se_arg, ag_arg, as_arg, fi_arg, fib_arg, fo_arg, fob_arg, fg_arg, fs_arg):
        content = content_arg.reshape(SEQS, S, D)
        query_rows = query_arg.reshape(SEQS, S, D)
        for layer_index in range(LAYERS):
            weights = (wq_arg[layer_index], wkv_arg[layer_index], wo_arg[layer_index], wr_arg[layer_index], hb_arg[layer_index], se_arg[layer_index], ag_arg[layer_index], as_arg[layer_index])
            memory_rows = memory_arg[layer_index].reshape(SEQS, M, D)

            def per_sequence(packed, weights=weights):
                return attend_sequence(packed[0], packed[1], packed[2], packed[3], packed[4], packed[5], weights)
            content, query_rows = lax.map(jax.checkpoint(per_sequence), (content, query_rows, memory_rows, doc_lengths, perm_rank, segment_ids))
            content = send(content)
            query_rows = send(query_rows)
            stacked = jnp.concatenate([content, query_rows], axis=0).reshape(2 * SEQS * S, D)
            ffn_rows = feed_forward(stacked, fi_arg[layer_index], fib_arg[layer_index], fo_arg[layer_index], fob_arg[layer_index], fg_arg[layer_index], fs_arg[layer_index])
            ffn_rows = send(ffn_rows).reshape(2, SEQS, S, D)
            content = ffn_rows[0]
            query_rows = ffn_rows[1]
        return (content.reshape(TOKENS, D), query_rows.reshape(TOKENS, D))
    outputs, pullback = jax.vjp(forward, *floats)
    gradients = pullback((cot_content.astype(jnp.float32), cot_query.astype(jnp.float32)))
    return (outputs[0].astype(jnp.bfloat16), outputs[1].astype(jnp.bfloat16), gradients[0], gradients[1], gradients[2], gradients[3], gradients[4], gradients[5], gradients[6], gradients[7], gradients[8], gradients[9], gradients[10], gradients[11], gradients[12], gradients[13], gradients[14], gradients[15], gradients[16])
```

```python
import functools
import math

import jax
import jax.numpy as jnp
import numpy as np
from jax import lax
from jax.experimental import pallas as pl
from jax.experimental.pallas import tpu as pltpu
from jax.sharding import PartitionSpec as P

D = 768
HEADS = 12
HEAD = 64
FF = 3072
S = 128
M = 64
LAYERS = 2
HALF = S // 2
KEYS = M + S
TABLE = M + 2 * S - 1
WIDE = 256
PAIRS = HEADS // 2
SHARE = D // 4
SCALE = HEAD**-0.5
NEGATIVE = -1e30
EPSILON = 1e-05
HIGHEST = lax.Precision.HIGHEST
BF = jnp.bfloat16
F32 = jnp.float32
GELU_C = math.sqrt(2.0 / math.pi)
MEG = 1 << 20

ROW_KV = 2 * HALF
ROW_REL = ROW_KV + KEYS
ROW_VEC = ROW_REL + WIDE // 2
ROWS_FIRST = ROW_VEC + 16
ROWS_SECOND = 2 * HALF
ROWS_ATTN = 240


def position_table():
    distance = (M + S - 1 - np.arange(TABLE)).astype(np.float32)
    inverse = np.exp(np.arange(0, D, 2).astype(np.float32) * np.float32(-math.log(10000.0) / D))
    angles = distance[:, None] * inverse[None, :].astype(np.float32)
    table = np.concatenate([np.sin(angles), np.cos(angles)], axis=1)
    table = np.concatenate([table, np.zeros((1, D), np.float32)], axis=0)
    return jnp.asarray(table, jnp.float32).astype(BF)


def dot_nn(a, b, precision=None):
    return lax.dot_general(
        a, b, (((1,), (0,)), ((), ())), precision=precision, preferred_element_type=F32
    )


def dot_nt(a, b):
    return lax.dot_general(a, b, (((1,), (1,)), ((), ())), preferred_element_type=F32)


def dot_tn(a, b):
    return lax.dot_general(a, b, (((0,), (0,)), ((), ())), preferred_element_type=F32)


def norm_parts(values):
    centre = values - jnp.mean(values, axis=-1, keepdims=True)
    spread = jnp.mean(centre * centre, axis=-1, keepdims=True)
    root = lax.rsqrt(spread + EPSILON)
    return centre * root, root


def norm_back(values, gain, grad):
    normal, root = norm_parts(values)
    scaled = grad * gain
    grad_gain = jnp.sum(grad * normal, axis=0, keepdims=True)
    grad_shift = jnp.sum(grad, axis=0, keepdims=True)
    first = jnp.mean(scaled, axis=-1, keepdims=True)
    second = jnp.mean(scaled * normal, axis=-1, keepdims=True)
    return root * (scaled - first - normal * second), grad_gain, grad_shift


def gelu(v):
    return 0.5 * v * (1.0 + jnp.tanh(GELU_C * (v + 0.044715 * (v * v * v))))


def gelu_both(v):
    square = v * v
    bend = jnp.tanh(GELU_C * (v + 0.044715 * (square * v)))
    half = 0.5 * (1.0 + bend)
    slope = half + 0.5 * v * (1.0 - bend * bend) * (GELU_C * (1.0 + 3 * 0.044715 * square))
    return v * half, slope


def low_lanes():
    return lax.broadcasted_iota(jnp.int32, (1, 2 * HEAD), 1) < HEAD


def two_heads(pair):
    low = low_lanes()
    zero = jnp.zeros_like(pair)
    return jnp.concatenate([jnp.where(low, pair, zero), jnp.where(low, zero, pair)], axis=0)


def one_pair(stacked):
    half = stacked.shape[0] // 2
    return jnp.where(low_lanes(), stacked[:half], stacked[half:])


def lane_sums(values):
    low = low_lanes()
    zero = jnp.zeros_like(values)
    first = jnp.sum(jnp.where(low, values, zero), axis=-1, keepdims=True)
    second = jnp.sum(jnp.where(low, zero, values), axis=-1, keepdims=True)
    return jnp.concatenate([first, second], axis=0)


def attn_forward_kernel(
    first_layer,
    at_ref,
    one_ref,
    two_ref,
    memory_ref,
    wq_ref,
    wkv_ref,
    wo_ref,
    wr_ref,
    bias_ref,
    seg_ref,
    gain_ref,
    shift_ref,
    table_ref,
    seen_ref,
    differs_ref,
    attended_ref,
    y_ref,
    summed_ref,
    qc_ref,
    qp_ref,
    qs_ref,
    kv_ref,
    rel_ref,
    prob_ref,
    joined_ref,
):
    section = at_ref[0]
    seq, half = section // 2, section % 2
    if first_layer:
        own = pl.ds(pl.multiple_of(section * HALF, HALF), HALF)
        x = jnp.concatenate([one_ref[own, :], two_ref[own, :]], axis=0)
        joined_ref[M:, :] = one_ref[pl.ds(pl.multiple_of(seq * S, S), S), :]
    else:
        x = one_ref[...]
        joined_ref[pl.ds(pl.multiple_of(M + HALF * half, HALF), HALF), :] = one_ref[:HALF, :]
        joined_ref[pl.ds(pl.multiple_of(M + HALF * (1 - half), HALF), HALF), :] = two_ref[...]
    joined_ref[:M, :] = memory_ref[pl.ds(pl.multiple_of(seq * M, M), M), :]
    projected = dot_nn(x, wq_ref[...])
    qc_ref[...] = ((projected + bias_ref[0:1, :]) * SCALE).astype(BF)
    qp_ref[...] = ((projected + bias_ref[1:2, :]) * SCALE).astype(BF)
    qs_ref[...] = (projected + bias_ref[2:3, :]) * SCALE
    kv_ref[...] = dot_nn(joined_ref[...], wkv_ref[...]).astype(BF)
    rows = table_ref[pl.ds(pl.multiple_of(HALF * (1 - half), HALF), WIDE), :]
    rel_ref[...] = dot_nn(rows, wr_ref[...]).astype(BF)
    seen = jnp.concatenate([seen_ref[...]] * 2, axis=0) > 0.0
    differs = jnp.concatenate([differs_ref[...]] * 2, axis=0)
    for p in range(PAIRS):
        at = slice(2 * HEAD * p, 2 * HEAD * (p + 1))
        later = slice(D + 2 * HEAD * p, D + 2 * HEAD * (p + 1))
        content = dot_nt(two_heads(qc_ref[:, at]), kv_ref[:, at])
        wide = dot_nt(two_heads(qp_ref[:, at]), rel_ref[:, at])
        skewed = jnp.concatenate(
            [
                pltpu.roll(
                    wide[HALF * b : HALF * (b + 1)], WIDE - HALF + 1, 1, stride=1, stride_axis=0
                )
                for b in range(4)
            ],
            axis=0,
        )[:, :KEYS]
        segment = qs_ref[:, at]
        same = lane_sums(segment * seg_ref[0:1, at])
        other = lane_sums(segment * seg_ref[1:2, at])
        raw = content + skewed + same + differs * (other - same)
        scores = jnp.where(seen, raw, NEGATIVE)
        highest = jnp.max(scores, axis=-1, keepdims=True)
        exponent = jnp.exp(scores - highest)
        prob = exponent / jnp.sum(exponent, axis=-1, keepdims=True)
        prob_ref[p] = prob
        mixed = dot_nn(prob.astype(BF), kv_ref[:, later])
        attended_ref[:, at] = one_pair(mixed).astype(BF)
    summed = dot_nn(attended_ref[...], wo_ref[...]) + x.astype(F32)
    summed_ref[...] = summed
    y_ref[...] = (norm_parts(summed)[0] * gain_ref[...] + shift_ref[...]).astype(BF)


def whole(shape):
    return pl.BlockSpec(shape, lambda i: (0,) * len(shape))


def of_layer(layer, shape):
    return pl.BlockSpec((None,) + shape, lambda i: (layer,) + (0,) * len(shape))


SCALAR = pl.BlockSpec(memory_space=pltpu.SMEM)


def params(limit=56 * MEG):
    return pltpu.CompilerParams(vmem_limit_bytes=limit)


def cost(flops, read):
    return pl.CostEstimate(flops=flops, bytes_accessed=read, transcendentals=0)


def attn_forward(layer, at, one, two, memory, weights, table, seen, differs):
    wq, wkv, wo, wr, bias, seg, gain, shift = weights
    shapes = [
        ((2 * HALF, D), BF),
        ((2 * HALF, D), BF),
        ((2 * HALF, D), F32),
        ((2 * HALF, D), BF),
        ((2 * HALF, D), BF),
        ((2 * HALF, D), F32),
        ((KEYS, 2 * D), BF),
        ((WIDE, D), BF),
        ((PAIRS, 4 * HALF, KEYS), F32),
    ]
    return pl.pallas_call(
        functools.partial(attn_forward_kernel, layer == 0),
        grid=(1,),
        in_specs=[
            SCALAR,
            whole(one.shape),
            whole(two.shape),
            of_layer(layer, memory.shape[1:]),
            of_layer(layer, (D, D)),
            of_layer(layer, (D, 2 * D)),
            of_layer(layer, (D, D)),
            of_layer(layer, (D, D)),
            of_layer(layer, (3, D)),
            of_layer(layer, (2, D)),
            of_layer(layer, (1, D)),
            of_layer(layer, (1, D)),
            whole(table.shape),
            whole(seen.shape),
            whole(differs.shape),
        ],
        out_specs=[whole(s) for s, _ in shapes],
        out_shape=[jax.ShapeDtypeStruct(s, t) for s, t in shapes],
        scratch_shapes=[pltpu.VMEM((KEYS, D), BF)],
        compiler_params=params(),
        cost_estimate=cost(1_200_000_000, 8_000_000),
        name="attn_forward",
    )(at, one, two, memory, wq, wkv, wo, wr, bias, seg, gain, shift, table, seen, differs)


FF_STEPS = 4
FF_BLOCK = FF // FF_STEPS


def ffn_forward_kernel(
    y_ref, win_ref, bin_ref, wout_ref, bout_ref, gain_ref, shift_ref,
    x_ref, pre_ref, sum_ref, total_ref,
):
    step = pl.program_id(0)
    y = y_ref[...]
    pre = dot_nn(y, win_ref[...]) + bin_ref[...]
    pre_ref[...] = pre
    part = dot_nn(gelu(pre).astype(BF), wout_ref[...])

    @pl.when(step == 0)
    def _():
        total_ref[...] = part

    @pl.when(step > 0)
    def _():
        total_ref[...] += part

    @pl.when(step == FF_STEPS - 1)
    def _():
        summed = total_ref[...] + bout_ref[...] + y.astype(F32)
        sum_ref[...] = summed
        x_ref[...] = (norm_parts(summed)[0] * gain_ref[...] + shift_ref[...]).astype(BF)


def ffn_forward(layer, y, weights):
    win, b_in, wout, b_out, gain, shift = weights
    rows = y.shape[0]
    return pl.pallas_call(
        ffn_forward_kernel,
        grid=(FF_STEPS,),
        in_specs=[
            whole(y.shape),
            pl.BlockSpec((None, D, FF_BLOCK), lambda i: (layer, 0, i)),
            pl.BlockSpec((None, 1, FF_BLOCK), lambda i: (layer, 0, i)),
            pl.BlockSpec((None, FF_BLOCK, D), lambda i: (layer, i, 0)),
            of_layer(layer, (1, D)),
            of_layer(layer, (1, D)),
            of_layer(layer, (1, D)),
        ],
        out_specs=[
            whole((rows, D)),
            pl.BlockSpec((rows, FF_BLOCK), lambda i: (0, i)),
            whole((rows, D)),
        ],
        out_shape=[
            jax.ShapeDtypeStruct((rows, D), BF),
            jax.ShapeDtypeStruct((rows, FF), F32),
            jax.ShapeDtypeStruct((rows, D), F32),
        ],
        scratch_shapes=[pltpu.VMEM((rows, D), F32)],
        compiler_params=params(),
        cost_estimate=cost(1_200_000_000, 12_000_000),
        name="ffn_forward",
    )(y, win, b_in, wout, b_out, gain, shift)


def ffn_backward_kernel(
    grad_ref, sum_ref, pre_ref, win_ref, wout_ref, gain_ref,
    gy_ref, low_ref, vec_ref, gsum_ref, total_ref,
):
    step = pl.program_id(0)

    @pl.when(step == 0)
    def _():
        gsum, ggain, gshift = norm_back(sum_ref[...], gain_ref[...], grad_ref[...].astype(F32))
        gsum_ref[...] = gsum
        low_ref[...] = gsum.astype(BF)
        gbias = jnp.sum(gsum, axis=0, keepdims=True)
        vec_ref[...] = jnp.concatenate([ggain, gshift, gbias, jnp.zeros((5, D), F32)], axis=0)

    slope = gelu_both(pre_ref[...])[1]
    gpre = (dot_nt(low_ref[...], wout_ref[...]) * slope).astype(BF)
    part = dot_nt(gpre, win_ref[...])

    @pl.when(step == 0)
    def _():
        total_ref[...] = part

    @pl.when(step > 0)
    def _():
        total_ref[...] += part

    @pl.when(step == FF_STEPS - 1)
    def _():
        gy_ref[...] = (total_ref[...] + gsum_ref[...]).astype(BF)


def ffn_backward(layer, grad, summed, pre, weights):
    win, b_in, wout, b_out, gain, shift = weights
    rows = grad.shape[0]
    return pl.pallas_call(
        ffn_backward_kernel,
        grid=(FF_STEPS,),
        in_specs=[
            whole((rows, D)),
            whole((rows, D)),
            pl.BlockSpec((rows, FF_BLOCK), lambda i: (0, i)),
            pl.BlockSpec((None, D, FF_BLOCK), lambda i: (layer, 0, i)),
            pl.BlockSpec((None, FF_BLOCK, D), lambda i: (layer, i, 0)),
            of_layer(layer, (1, D)),
        ],
        out_specs=[whole((rows, D)), whole((rows, D)), whole((8, D))],
        out_shape=[
            jax.ShapeDtypeStruct((rows, D), BF),
            jax.ShapeDtypeStruct((rows, D), BF),
            jax.ShapeDtypeStruct((8, D), F32),
        ],
        scratch_shapes=[pltpu.VMEM((rows, D), F32), pltpu.VMEM((rows, D), F32)],
        compiler_params=params(),
        cost_estimate=cost(1_200_000_000, 12_000_000),
        name="ffn_backward",
    )(grad, summed, pre, win, wout, gain)


def attn_backward_kernel(
    first_layer,
    at_ref,
    grad_ref,
    summed_ref,
    wq_ref,
    wkv_ref,
    wo_ref,
    seg_ref,
    gain_ref,
    qc_ref,
    qp_ref,
    qs_ref,
    kv_ref,
    rel_ref,
    prob_ref,
    differs_ref,
    ffn_vec_ref,
    out_ref,
    gx_ref,
    send_ref,
    first0_ref,
    first1_ref,
    first2_ref,
    first3_ref,
    second0_ref,
    second1_ref,
    second2_ref,
    second3_ref,
    vec_ref,
    proj_ref,
    gkv_ref,
    grel_ref,
    joined_ref,
    first_ref,
    second_ref,
):
    section = at_ref[0]
    half = section % 2
    gsum, ggain, gshift = norm_back(summed_ref[...], gain_ref[...], grad_ref[...].astype(F32))
    low = gsum.astype(BF)
    vec_ref[0:1, :] = ggain
    vec_ref[1:2, :] = gshift
    vec_ref[7:8, :] = jnp.zeros((1, D), F32)
    vec_ref[8:16, :] = ffn_vec_ref[...]
    g_attended = dot_nt(low, wo_ref[...]).astype(BF)
    differs = jnp.concatenate([differs_ref[...]] * 2, axis=0)
    row = lax.broadcasted_iota(jnp.int32, (4 * HALF, 4 * HALF), 0)
    column = lax.broadcasted_iota(jnp.int32, (4 * HALF, 4 * HALF), 1)
    flip = ((row // HALF == column // HALF) & (row % HALF + column % HALF == HALF - 1)).astype(BF)
    lowest = low_lanes()
    for p in range(PAIRS):
        at = slice(2 * HEAD * p, 2 * HEAD * (p + 1))
        later = slice(D + 2 * HEAD * p, D + 2 * HEAD * (p + 1))
        prob = prob_ref[p]
        ga = two_heads(g_attended[:, at])
        gprob = dot_nt(ga, kv_ref[:, later])
        gkv_ref[:, later] = dot_tn(prob.astype(BF), ga).astype(BF)
        weighted = prob * gprob
        centre = jnp.sum(weighted, axis=-1, keepdims=True)
        gscores = (weighted - prob * centre).astype(BF)
        wide_low = gscores.astype(F32)
        other_part = wide_low * differs
        other = jnp.sum(other_part, axis=-1, keepdims=True)
        same = jnp.sum(wide_low - other_part, axis=-1, keepdims=True)
        gqc = one_pair(dot_nn(gscores, kv_ref[:, at]))
        gkv_ref[:, at] = dot_tn(gscores, two_heads(qc_ref[:, at])).astype(BF)
        flipped = dot_nn(flip, gscores)
        padded = jnp.concatenate(
            [flipped, jnp.zeros((4 * HALF, WIDE - KEYS), F32)], axis=1
        )
        turned = jnp.concatenate(
            [
                pltpu.roll(padded[HALF * b : HALF * (b + 1)], 0, 1, stride=1, stride_axis=0)
                for b in range(4)
            ],
            axis=0,
        )
        gwide = dot_nn(flip, turned.astype(BF)).astype(BF)
        gqp = one_pair(dot_nn(gwide, rel_ref[:, at]))
        grel_ref[:, at] = dot_tn(gwide, two_heads(qp_ref[:, at])).astype(BF)
        rows = 2 * HALF
        same_pair = jnp.where(lowest, same[:rows], same[rows:])
        other_pair = jnp.where(lowest, other[:rows], other[rows:])
        gqs = same_pair * seg_ref[0:1, at] + other_pair * seg_ref[1:2, at]
        segment = qs_ref[:, at]
        vec_ref[2:3, at] = jnp.sum(gqc, axis=0, keepdims=True) * SCALE
        vec_ref[3:4, at] = jnp.sum(gqp, axis=0, keepdims=True) * SCALE
        vec_ref[4:5, at] = jnp.sum(gqs, axis=0, keepdims=True) * SCALE
        vec_ref[5:6, at] = jnp.sum(same_pair * segment, axis=0, keepdims=True)
        vec_ref[6:7, at] = jnp.sum(other_pair * segment, axis=0, keepdims=True)
        proj_ref[:, at] = ((gqc + gqp + gqs) * SCALE).astype(BF)
    vectors = vec_ref[...].astype(BF)
    proj = proj_ref[...]
    for d in range(4):
        at = slice(SHARE * d, SHARE * (d + 1))
        first_ref[d, :ROW_KV, :SHARE] = low[:, at]
        first_ref[d, :ROW_KV, SHARE:] = proj[:, at]
        first_ref[d, ROW_KV:ROW_REL, :] = gkv_ref[:, 2 * SHARE * d : 2 * SHARE * (d + 1)]
        first_ref[d, ROW_REL:ROW_VEC, :SHARE] = grel_ref[: WIDE // 2, at]
        first_ref[d, ROW_REL:ROW_VEC, SHARE:] = grel_ref[WIDE // 2 :, at]
        first_ref[d, ROW_VEC:, :SHARE] = vectors[:, at]
        first_ref[d, ROW_VEC:, SHARE:] = vectors[:, at]
    first0_ref[...] = first_ref[section]
    for k, ref in ((1, first1_ref), (2, first2_ref), (3, first3_ref)):
        ref[...] = first_ref[section ^ k]
    gx = dot_nt(proj, wq_ref[...]) + gsum
    joined_ref[...] = dot_nt(gkv_ref[...], wkv_ref[...])
    own = joined_ref[pl.ds(pl.multiple_of(M + HALF * half, HALF), HALF), :]
    partner = joined_ref[pl.ds(pl.multiple_of(M + HALF * (1 - half), HALF), HALF), :].astype(BF)
    memory = joined_ref[:M, :].astype(BF)
    gx = jnp.concatenate([gx[:HALF] + own, gx[HALF:]], axis=0)
    gx_ref[...] = gx
    send_ref[...] = partner
    carried = gx.astype(BF) if first_layer else out_ref[...]
    for d in range(4):
        at = slice(SHARE * d, SHARE * (d + 1))
        second_ref[d, :HALF, :SHARE] = carried[:HALF, at]
        second_ref[d, :HALF, SHARE:] = carried[HALF:, at]
        second_ref[d, HALF:, :SHARE] = partner[:, at]
        second_ref[d, HALF:, SHARE:] = memory[:, at]
    second0_ref[...] = second_ref[section]
    for k, ref in ((1, second1_ref), (2, second2_ref), (3, second3_ref)):
        ref[...] = second_ref[section ^ k]


def attn_backward(layer, at, grad, saved, weights, differs, ffn_vec, out):
    wq, wkv, wo, wr, bias, seg, gain, shift = weights
    attended, y, summed, qc, qp, qs, kv, rel, prob = saved
    shapes = (
        [((2 * HALF, D), F32), ((HALF, D), BF)]
        + [((ROWS_FIRST, 2 * SHARE), BF)] * 4
        + [((ROWS_SECOND, 2 * SHARE), BF)] * 4
    )
    return pl.pallas_call(
        functools.partial(attn_backward_kernel, layer == 0),
        grid=(1,),
        in_specs=[
            SCALAR,
            whole(grad.shape),
            whole(summed.shape),
            of_layer(layer, (D, D)),
            of_layer(layer, (D, 2 * D)),
            of_layer(layer, (D, D)),
            of_layer(layer, (2, D)),
            of_layer(layer, (1, D)),
            whole(qc.shape),
            whole(qp.shape),
            whole(qs.shape),
            whole(kv.shape),
            whole(rel.shape),
            whole(prob.shape),
            whole(differs.shape),
            whole(ffn_vec.shape),
            whole(out.shape),
        ],
        out_specs=[whole(s) for s, _ in shapes],
        out_shape=[jax.ShapeDtypeStruct(s, t) for s, t in shapes],
        scratch_shapes=[
            pltpu.VMEM((16, D), F32),
            pltpu.VMEM((2 * HALF, D), BF),
            pltpu.VMEM((KEYS, 2 * D), BF),
            pltpu.VMEM((WIDE, D), BF),
            pltpu.VMEM((KEYS, D), F32),
            pltpu.VMEM((4, ROWS_FIRST, 2 * SHARE), BF),
            pltpu.VMEM((4, ROWS_SECOND, 2 * SHARE), BF),
        ],
        compiler_params=params(),
        cost_estimate=cost(1_500_000_000, 8_000_000),
        name="attn_backward",
    )(
        at, grad, summed, wq, wkv, wo, seg, gain, qc, qp, qs, kv, rel, prob, differs, ffn_vec, out
    )


def ffn_weights_kernel(
    blocks, at_ref, y0, y1, y2, y3, g0, g1, g2, g3, win_ref, bin_ref, wout_ref, *outs
):
    step = pl.program_id(0)
    y = jnp.concatenate([r[...] for r in (y0, y1, y2, y3)], axis=0)
    low = jnp.concatenate([r[...] for r in (g0, g1, g2, g3)], axis=0)
    pre = dot_nn(y, win_ref[...]) + bin_ref[...]
    active, slope = gelu_both(pre)
    gpre = (dot_nt(low, wout_ref[...]) * slope).astype(BF)
    outs[-1][...] = jnp.sum(gpre.astype(F32), axis=0, keepdims=True)
    grad_in = dot_tn(y, gpre).astype(BF)
    grad_out = dot_tn(low, active.astype(BF)).astype(BF)
    if blocks:
        piece_ref = outs[0]
        rows = D // 8
        for s in range(4):
            piece_ref[step * 4 + s, :SHARE, :] = grad_in[SHARE * s : SHARE * (s + 1), :]
        for d in range(8):
            start = pl.multiple_of(SHARE + step * rows, rows)
            piece_ref[d, pl.ds(start, rows), :] = grad_out[rows * d : rows * (d + 1), :]
    else:
        outs[0][...] = grad_in
        outs[1][...] = grad_out


def ffn_weights(layer, at, y_all, low_all, weights, blocks):
    win, b_in, wout, b_out, gain, shift = weights
    rows = y_all[0].shape[0]
    width = FF // 8
    if blocks:
        outs = [(8, 2 * SHARE, width)]
        specs = [pl.BlockSpec(outs[0], lambda i, s: (0, 0, 0))]
    else:
        outs = [(D, 2 * width), (D, 2 * width)]
        specs = [pl.BlockSpec((D, width), lambda i, s: (0, i))] * 2
    piece = pl.BlockSpec((rows, D), lambda i, s: (0, 0))
    return pl.pallas_call(
        functools.partial(ffn_weights_kernel, blocks),
        grid_spec=pltpu.PrefetchScalarGridSpec(
            num_scalar_prefetch=1,
            grid=(2,),
            in_specs=[piece] * 8
            + [
                pl.BlockSpec((None, D, width), lambda i, s: (layer, 0, 2 * s[0] + i)),
                pl.BlockSpec((None, 1, width), lambda i, s: (layer, 0, 2 * s[0] + i)),
                pl.BlockSpec((None, width, D), lambda i, s: (layer, 2 * s[0] + i, 0)),
            ],
            out_specs=specs + [pl.BlockSpec((1, width), lambda i, s: (0, i))],
        ),
        out_shape=[jax.ShapeDtypeStruct(s, BF) for s in outs]
        + [jax.ShapeDtypeStruct((1, 2 * width), F32)],
        compiler_params=params(),
        cost_estimate=cost(3_000_000_000, 5_000_000),
        name="ffn_weights",
    )(at, *y_all, *low_all, win, b_in, wout)


def attn_weights_kernel(first_layer, blocks, at_ref, *refs):
    count = 2 if first_layer else 4
    inputs, refs = refs[:count], refs[count:]
    memory_ref, table_ref = refs[:2]
    attended = refs[2:6]
    messages = refs[6:10]
    outs, scratch = refs[10:-2], refs[-2:]
    x_ref, joined_ref = scratch
    section = at_ref[0]
    half = section % 2
    for k in range(4):
        source = section ^ k
        if first_layer:
            rows = pl.ds(pl.multiple_of(source * HALF, HALF), HALF)
            x_ref[2 * HALF * k : 2 * HALF * k + HALF, :] = inputs[0][rows, :]
            x_ref[2 * HALF * k + HALF : 2 * HALF * (k + 1), :] = inputs[1][rows, :]
        else:
            x_ref[2 * HALF * k : 2 * HALF * (k + 1), :] = inputs[k][...]
    for pair in range(2):
        seq = (section ^ (2 * pair)) // 2
        joined_ref[pair, :M, :] = memory_ref[pl.ds(pl.multiple_of(seq * M, M), M), :]
        for k in (2 * pair, 2 * pair + 1):
            place = half ^ (k & 1)
            rows = pl.ds(pl.multiple_of(M + HALF * place, HALF), HALF)
            joined_ref[pair, rows, :] = x_ref[2 * HALF * k : 2 * HALF * k + HALF, :]
    x = x_ref[...]
    low = jnp.concatenate([r[:ROW_KV, :SHARE] for r in messages], axis=0)
    proj = jnp.concatenate([r[:ROW_KV, SHARE:] for r in messages], axis=0)
    grad_q = dot_tn(proj, x).astype(BF)
    grad_o = dot_tn(low, jnp.concatenate([r[...] for r in attended], axis=0)).astype(BF)
    grad_kv = None
    for pair in range(2):
        one, two = messages[2 * pair], messages[2 * pair + 1]
        both = (
            one[ROW_KV:ROW_REL, :].astype(F32) + two[ROW_KV:ROW_REL, :].astype(F32)
        ).astype(BF)
        part = dot_tn(both, joined_ref[pair])
        grad_kv = part if grad_kv is None else grad_kv + part
    grad_kv = grad_kv.astype(BF)
    grad_rel = None
    for k in range(2):
        place = half ^ k
        total = messages[k][ROW_REL:ROW_VEC, :].astype(F32) + messages[k + 2][
            ROW_REL:ROW_VEC, :
        ].astype(F32)
        total = jnp.concatenate([total[:, :SHARE], total[:, SHARE:]], axis=0).astype(BF)
        rows = table_ref[pl.ds(pl.multiple_of(HALF * (1 - place), HALF), WIDE), :]
        part = dot_tn(total, rows)
        grad_rel = part if grad_rel is None else grad_rel + part
    grad_rel = grad_rel.astype(BF)
    vectors = None
    for r in messages:
        part = r[ROW_VEC:, :SHARE].astype(F32)
        vectors = part if vectors is None else vectors + part
    outs[-1][...] = vectors
    if blocks:
        piece_ref = outs[0]
        rows = SHARE // 2
        small = rows // 2
        for h in range(2):
            for s in range(4):
                d = 4 * h + s
                at = slice(SHARE * s, SHARE * (s + 1))
                piece_ref[d, :rows, :SHARE] = grad_q[rows * h : rows * (h + 1), at]
                piece_ref[d, :rows, SHARE:] = grad_o[rows * h : rows * (h + 1), at]
                start = 2 * rows * h
                piece_ref[d, rows : 2 * rows, :SHARE] = grad_kv[start : start + rows, at]
                piece_ref[d, rows : 2 * rows, SHARE:] = grad_kv[start + rows : start + 2 * rows, at]
                start = rows * h
                piece_ref[d, 2 * rows :, :SHARE] = grad_rel[start : start + small, at]
                piece_ref[d, 2 * rows :, SHARE:] = grad_rel[start + small : start + rows, at]
    else:
        outs[0][...] = grad_q
        outs[1][...] = grad_kv
        outs[2][...] = grad_o
        outs[3][...] = grad_rel


def attn_weights(layer, at, inputs, memory, table, attended, messages, blocks):
    if blocks:
        outs = [(8, ROWS_ATTN, 2 * SHARE)]
    else:
        outs = [(SHARE, D), (2 * SHARE, D), (SHARE, D), (SHARE, D)]
    return pl.pallas_call(
        functools.partial(attn_weights_kernel, layer == 0, blocks),
        grid=(1,),
        in_specs=[SCALAR]
        + [whole(a.shape) for a in inputs]
        + [of_layer(layer, memory.shape[1:]), whole(table.shape)]
        + [whole(a.shape) for a in attended]
        + [whole(a.shape) for a in messages],
        out_specs=[whole(s) for s in outs] + [whole((16, SHARE))],
        out_shape=[jax.ShapeDtypeStruct(s, BF) for s in outs]
        + [jax.ShapeDtypeStruct((16, SHARE), F32)],
        scratch_shapes=[pltpu.VMEM((8 * HALF, D), BF), pltpu.VMEM((2, KEYS, D), BF)],
        compiler_params=params(),
        cost_estimate=cost(1_000_000_000, 5_000_000),
        name="attn_weights",
    )(at, *inputs, memory, table, *attended, *messages)


def gather_kernel(at_ref, *refs):
    section = at_ref[0]
    late, early = refs[:4], refs[4:8]
    outc_ref, outq_ref, gradc_ref, gradq_ref, mem_ref = refs[8:]
    for k in range(4):
        rows = pl.ds(pl.multiple_of((section ^ k) * HALF, HALF), HALF)
        outc_ref[rows, :] = late[k][:HALF, :SHARE]
        outq_ref[rows, :] = late[k][:HALF, SHARE:]
        gradc_ref[rows, :] = early[k][:HALF, :SHARE].astype(F32) + early[k ^ 1][
            HALF:, :SHARE
        ].astype(F32)
        gradq_ref[rows, :] = early[k][:HALF, SHARE:].astype(F32)
    for pair in range(2):
        rows = pl.ds(pl.multiple_of((section ^ (2 * pair)) // 2 * M, M), M)
        for layer, refs4 in ((0, early), (1, late)):
            mem_ref[layer, rows, :] = refs4[2 * pair][HALF:, SHARE:].astype(F32) + refs4[
                2 * pair + 1
            ][HALF:, SHARE:].astype(F32)


def gather_rows(at, late, early):
    rows = 4 * HALF
    shapes = [
        ((rows, SHARE), BF),
        ((rows, SHARE), BF),
        ((rows, SHARE), F32),
        ((rows, SHARE), F32),
        ((LAYERS, 2 * M, SHARE), F32),
    ]
    return pl.pallas_call(
        gather_kernel,
        grid=(1,),
        in_specs=[SCALAR] + [whole(a.shape) for a in (*late, *early)],
        out_specs=[whole(s) for s, _ in shapes],
        out_shape=[jax.ShapeDtypeStruct(s, t) for s, t in shapes],
        compiler_params=params(),
        cost_estimate=cost(1_000_000, 2_000_000),
        name="gather_rows",
    )(at, *late, *early)


def swapped(x, axis, k):
    return lax.ppermute(x, axis, [(i, i ^ k) for i in range(lax.axis_size(axis))])


def from_all(x):
    return [x] + [swapped(x, "section", k) for k in (1, 2, 3)]


def added(a, b):
    return (a.astype(F32) + b.astype(F32)).astype(BF)


def reduce_scattered(pieces):
    count = pieces.shape[0]
    if count != 8:
        return lax.psum_scatter(pieces, "dp", scatter_dimension=0, tiled=False)
    index = lax.axis_index("dp")
    core, chip = index % 2, index // 2
    split = pieces.reshape((count // 2, 2) + pieces.shape[1:])
    kept = lax.dynamic_index_in_dim(split, core, 1, keepdims=False)
    given = lax.dynamic_index_in_dim(split, 1 - core, 1, keepdims=False)
    mine = added(kept, swapped(given, "dp", 1))
    chips = count // 2

    def at(place):
        return lax.dynamic_index_in_dim(mine, jnp.clip(place, 0, chips - 1), 0, keepdims=False)

    right = left = None
    for step in range(1, chips):
        to_right, to_left = at(chip + chips - step), at(chip - chips + step)
        if right is not None:
            to_right, to_left = added(to_right, right), added(to_left, left)
        right = lax.ppermute(to_right, "dp", [(i, i + 2) for i in range(count - 2)])
        left = lax.ppermute(to_left, "dp", [(i + 2, i) for i in range(count - 2)])
    return (at(chip).astype(F32) + right.astype(F32) + left.astype(F32)).astype(BF)


def to_owner(piece):
    sections, count = lax.axis_size("section"), lax.axis_size("dp")
    m = count // sections
    pairs = []
    for s in range(sections):
        for d in range(count):
            h, t = d // sections, d % sections
            pairs.append((s * count + d, t * count + m * s + h))
    return lax.ppermute(piece, ("section", "dp"), pairs)


def summed_over_dp(x):
    step = 1
    while step < lax.axis_size("dp"):
        x = x + swapped(x, "dp", step)
        step *= 2
    return x


def on_device(
    content_in,
    query_in,
    memory,
    doc_lengths,
    perm_rank,
    segment_ids,
    w_query,
    w_keyval,
    w_out,
    w_rel,
    head_bias,
    seg_embed,
    attn_gain,
    attn_shift,
    ffn_in,
    ffn_in_bias,
    ffn_out,
    ffn_out_bias,
    ffn_gain,
    ffn_shift,
    cot_content,
    cot_query,
):
    dp = lax.axis_size("dp")
    blocks = dp == 8
    section = lax.axis_index("section")
    at = section.astype(jnp.int32).reshape(1)
    seq, half = section // 2, section % 2

    def lifted(v):
        return v.reshape(LAYERS, 1, -1)

    attn = (
        w_query, w_keyval, w_out, w_rel, head_bias, seg_embed, lifted(attn_gain), lifted(attn_shift)
    )
    ffn = (
        ffn_in, lifted(ffn_in_bias), ffn_out, lifted(ffn_out_bias), lifted(ffn_gain),
        lifted(ffn_shift),
    )
    table = position_table()

    ranks = lax.dynamic_index_in_dim(perm_rank, seq, 0, keepdims=False)
    segments = lax.dynamic_index_in_dim(segment_ids, seq, 0, keepdims=False)
    length = lax.dynamic_index_in_dim(doc_lengths, seq, 0, keepdims=False)
    key_rank = jnp.concatenate(
        [jnp.full((M,), -1, jnp.int32), jnp.where(jnp.arange(S) < length, ranks, 2 * S)]
    )
    own_rank = lax.dynamic_slice_in_dim(ranks, half * HALF, HALF, 0)
    reach = jnp.concatenate([own_rank, own_rank - 1])
    seen = (key_rank[None, :] <= reach[:, None]).astype(F32)
    own_segment = lax.dynamic_slice_in_dim(segments, half * HALF, HALF, 0)
    key_segment = jnp.concatenate([jnp.zeros((M,), jnp.int32), segments])
    differs = (jnp.concatenate([own_segment] * 2)[:, None] != key_segment[None, :]).astype(F32)

    def own_rows(one, two):
        return jnp.concatenate(
            [lax.dynamic_slice_in_dim(a, section * HALF, HALF, 0) for a in (one, two)], axis=0
        )

    saved0 = attn_forward(0, at, content_in, query_in, memory, attn, table, seen, differs)
    x1, pre0, sum0 = ffn_forward(0, saved0[1], ffn)
    other = swapped(x1[:HALF], "section", 1)
    saved1 = attn_forward(1, at, x1, other, memory, attn, table, seen, differs)
    x2, pre1, sum1 = ffn_forward(1, saved1[1], ffn)
    attended0, y0 = from_all(saved0[0]), from_all(saved0[1])
    x1_all = from_all(x1)
    attended1, y1 = from_all(saved1[0]), from_all(saved1[1])

    gy1, low1, vec1 = ffn_backward(1, own_rows(cot_content, cot_query), sum1, pre1, ffn)
    low1_all = from_all(low1)
    back1 = attn_backward(1, at, gy1, saved1, attn, differs, vec1, x2)
    received = swapped(back1[1], "section", 1)
    gx1 = back1[0]
    gx1 = jnp.concatenate([gx1[:HALF] + received.astype(F32), gx1[HALF:]], axis=0).astype(BF)
    gy0, low0, vec0 = ffn_backward(0, gx1, sum0, pre0, ffn)
    low0_all = from_all(low0)
    back0 = attn_backward(0, at, gy0, saved0, attn, differs, vec0, x2)

    def messages(parts):
        return [parts[0]] + [swapped(parts[k], "section", k) for k in (1, 2, 3)]

    def spread(arrays):
        m = dp // 4
        parts = []
        for a, by_columns in arrays:
            if by_columns:
                cut = a.reshape(4, SHARE, m, -1).transpose(2, 0, 1, 3)
            else:
                cut = a.reshape(m, -1, 4, SHARE).transpose(0, 2, 1, 3)
            parts.append(cut.reshape(dp, -1))
        return parts

    def ffn_grads(layer, y_all, low_all):
        *grads, bias = ffn_weights(layer, at, y_all, low_all, ffn, blocks)
        if blocks:
            total = reduce_scattered(grads[0])
            inner, outer = total[:SHARE], total[SHARE:]
            outer = jnp.concatenate([outer[: D // 8], outer[D // 8 :]], axis=1)
        else:
            parts = spread([(grads[0], True)]) + [grads[1].reshape(dp, -1)]
            width = parts[0].shape[1]
            total = reduce_scattered(jnp.concatenate(parts, axis=1).reshape(dp, -1, 128))
            total = total.reshape(-1)
            inner = total[:width].reshape(SHARE, -1)
            outer = total[width:].reshape(D // dp, FF // 4)
        return to_owner(inner).astype(F32), outer.astype(F32).T, bias

    def attn_grads(layer, inputs, attended, parts):
        *grads, vectors = attn_weights(
            layer, at, inputs, memory, table, attended, parts, blocks
        )
        if blocks:
            total = to_owner(reduce_scattered(grads[0])).astype(F32)
            rows = SHARE // 2
            q, o = total[:rows, :SHARE], total[:rows, SHARE:]
            kv = jnp.concatenate(
                [total[rows : 2 * rows, :SHARE], total[rows : 2 * rows, SHARE:]], axis=0
            )
            r = jnp.concatenate([total[2 * rows :, :SHARE], total[2 * rows :, SHARE:]], axis=0)
        else:
            parts = spread([(g, False) for g in grads])
            total = reduce_scattered(jnp.concatenate(parts, axis=1).reshape(dp, -1, 128))
            total = to_owner(total).astype(F32).reshape(-1)
            cuts, start = [], 0
            for part in parts:
                cuts.append(total[start : start + part.shape[1]].reshape(-1, SHARE))
                start += part.shape[1]
            q, kv, o, r = cuts
        return q.T, kv.T, o.T, r.T, vectors

    fin1, fout1, fbias1 = ffn_grads(1, y1, low1_all)
    wq1, wkv1, wo1, wr1, vectors1 = attn_grads(1, x1_all, attended1, messages(back1[2:6]))
    fin0, fout0, fbias0 = ffn_grads(0, y0, low0_all)
    wq0, wkv0, wo0, wr0, vectors0 = attn_grads(
        0, (content_in, query_in), attended0, messages(back0[2:6])
    )
    late, early = messages(back1[6:10]), messages(back0[6:10])
    out_content, out_query, grad_content, grad_query, grad_memory = gather_rows(at, late, early)
    small = jnp.concatenate(
        [vectors0, vectors1, fbias0.reshape(4, SHARE), fbias1.reshape(4, SHARE)], axis=0
    )
    small = summed_over_dp(small)
    vectors = small[:32].reshape(LAYERS, 16, SHARE)
    return (
        out_content,
        out_query,
        grad_content,
        grad_query,
        grad_memory,
        jnp.stack([wq0, wq1]),
        jnp.stack([wkv0, wkv1]),
        jnp.stack([wo0, wo1]),
        jnp.stack([wr0, wr1]),
        vectors[:, 2:5],
        vectors[:, 5:7],
        vectors[:, 0],
        vectors[:, 1],
        jnp.stack([fin0, fin1]),
        small[32:].reshape(LAYERS, FF // 4),
        jnp.stack([fout0, fout1]),
        vectors[:, 10],
        vectors[:, 8],
        vectors[:, 9],
    )


def solution(mesh):
    in_specs = (
        P("dp", None),
        P("dp", None),
        P(None, "dp", None),
        P("dp"),
        P("dp", None),
        P("dp", None),
    ) + (P(),) * 14 + (P("dp", None), P("dp", None))
    weight, vector = P(None, "section", "dp"), P(None, "section")
    out_specs = (
        P("dp", "section"),
        P("dp", "section"),
        P("dp", "section"),
        P("dp", "section"),
        P(None, "dp", "section"),
        weight,
        weight,
        weight,
        weight,
        P(None, None, "section"),
        P(None, None, "section"),
        vector,
        vector,
        weight,
        vector,
        weight,
        vector,
        vector,
        vector,
    )
    return jax.shard_map(
        on_device, mesh=mesh, in_specs=in_specs, out_specs=out_specs, check_vma=False
    )
```

```python
import functools
import math

import jax
import jax.numpy as jnp
import numpy as np
from jax import lax
from jax.experimental import pallas as pl
from jax.experimental.pallas import tpu as pltpu
from jax.sharding import PartitionSpec as P

D = 768
HEADS = 12
HEAD = 64
FF = 3072
S = 128
M = 64
LAYERS = 2
HALF = S // 2
KEYS = M + S
TABLE = M + 2 * S - 1
WIDE = 256
ROWS = 2 * HALF
PAIRS = HEADS // 2
SHARE = D // 4
SCALE = HEAD**-0.5
NEGATIVE = -1e30
EPSILON = 1e-05
SECTION, DP = "section", "dp"
BF = jnp.bfloat16
F32 = jnp.float32
GELU_C = math.sqrt(2.0 / math.pi)
MEG = 1 << 20

FIRST = (SHARE, 7 * 128)
SECOND = (SHARE, 2 * WIDE)
ROWS_ATTN = 240
ROWS_VEC = 16
ROWS_FFN = FF // 16


def position_table():
    distance = (M + S - 1 - np.arange(TABLE)).astype(np.float32)
    inverse = np.exp(np.arange(0, D, 2).astype(np.float32) * np.float32(-math.log(10000.0) / D))
    angles = distance[:, None] * inverse[None, :].astype(np.float32)
    table = np.concatenate([np.sin(angles), np.cos(angles)], axis=1)
    table = np.concatenate([table, np.zeros((1, D), np.float32)], axis=0)
    return jnp.asarray(table, jnp.float32).astype(BF)


def dot_nn(a, b):
    return lax.dot_general(a, b, (((1,), (0,)), ((), ())), preferred_element_type=F32)


def dot_nt(a, b):
    return lax.dot_general(a, b, (((1,), (1,)), ((), ())), preferred_element_type=F32)


def norm_parts(values):
    centre = values - jnp.mean(values, axis=-1, keepdims=True)
    spread = jnp.mean(centre * centre, axis=-1, keepdims=True)
    root = lax.rsqrt(spread + EPSILON)
    return centre * root, root


def norm_back(values, gain, grad):
    normal, root = norm_parts(values)
    scaled = grad * gain
    grad_gain = jnp.sum(grad * normal, axis=0, keepdims=True)
    grad_shift = jnp.sum(grad, axis=0, keepdims=True)
    first = jnp.mean(scaled, axis=-1, keepdims=True)
    second = jnp.mean(scaled * normal, axis=-1, keepdims=True)
    return root * (scaled - first - normal * second), grad_gain, grad_shift


def gelu(v):
    return 0.5 * v * (1.0 + jnp.tanh(GELU_C * (v + 0.044715 * (v * v * v))))


def gelu_both(v):
    square = v * v
    bend = jnp.tanh(GELU_C * (v + 0.044715 * (square * v)))
    half = 0.5 * (1.0 + bend)
    slope = half + 0.5 * v * (1.0 - bend * bend) * (GELU_C * (1.0 + 3 * 0.044715 * square))
    return v * half, slope


def low_lanes():
    return lax.broadcasted_iota(jnp.int32, (1, 2 * HEAD), 1) < HEAD


def two_heads(pair):
    low = low_lanes()
    zero = jnp.zeros_like(pair)
    return jnp.concatenate([jnp.where(low, pair, zero), jnp.where(low, zero, pair)], axis=0)


def one_pair(stacked):
    half = stacked.shape[0] // 2
    return jnp.where(low_lanes(), stacked[:half], stacked[half:])


def in_two(values):
    high = values.astype(BF)
    return jnp.concatenate([high, (values - high.astype(F32)).astype(BF)], axis=1)


def skewed_scores(wide):
    parts = [
        pltpu.roll(wide[HALF * b : HALF * (b + 1)], WIDE - HALF + 1, 1, stride=1, stride_axis=0)
        for b in range(4)
    ]
    return jnp.concatenate(parts, axis=0)[:, :KEYS]


def unskewed_scores(scores):
    rows, wide = 4 * HALF, WIDE // 2
    shift = HALF - 1 - lax.broadcasted_iota(jnp.int32, (rows, wide), 0) % HALF
    lane = lax.broadcasted_iota(jnp.int32, (rows, wide), 1)
    source = (lane - shift) & (wide - 1)
    wrapped = lane < shift
    rest = jnp.concatenate([scores[:, wide:], jnp.zeros((rows, WIDE - KEYS), F32)], axis=1)
    first, second = (
        jnp.take_along_axis(a, source, axis=1, mode=lax.GatherScatterMode.PROMISE_IN_BOUNDS)
        for a in (scores[:, :wide], rest)
    )
    return jnp.concatenate(
        [jnp.where(wrapped, 0.0, first), jnp.where(wrapped, first, second)], axis=1
    )


def sight(at_ref, lengths_ref, ranks_ref, segments_ref):
    seq, half = at_ref[0] // 2, at_ref[0] % 2
    ranks = ranks_ref[pl.ds(seq, 1), :]
    segments = segments_ref[pl.ds(seq, 1), :]
    place = lax.broadcasted_iota(jnp.int32, (1, S), 1)
    live = jnp.where(place < lengths_ref[seq], ranks, 2 * S)
    key_rank = jnp.concatenate([jnp.full((1, M), -1, jnp.int32), live], axis=1)
    key_segment = jnp.concatenate([jnp.zeros((1, M), jnp.int32), segments], axis=1)
    row = lax.broadcasted_iota(jnp.int32, (HALF, S), 0) + half * HALF
    column = lax.broadcasted_iota(jnp.int32, (HALF, S), 1)

    def upright(values):
        wide = jnp.where(row == column, values.astype(F32), 0.0)
        return jnp.sum(wide, axis=-1, keepdims=True).astype(jnp.int32)

    own_rank, own_segment = upright(ranks), upright(segments)
    reach = jnp.concatenate([own_rank, own_rank - 1], axis=0)
    hidden = jnp.where(key_rank <= reach, 0.0, 1.0)
    differs = jnp.where(jnp.concatenate([own_segment] * 2, axis=0) != key_segment, 1.0, 0.0)
    return [jnp.concatenate([a] * 2, axis=0) > 0.0 for a in (hidden, differs)]


class Mover:
    def __init__(self, semaphores):
        self.semaphores, self.count, self.open = semaphores, 0, []

    def __call__(self, source, target):
        copy = pltpu.make_async_copy(source, target, self.semaphores.at[self.count])
        self.count += 1
        copy.start()
        self.open.append(copy)
        return copy

    def wait(self, *copies):
        for copy in copies:
            if any(copy is other for other in self.open):
                self.open = [other for other in self.open if other is not copy]
                copy.wait()

    def finish(self):
        self.wait(*list(self.open))


class Bag:
    def __init__(self, names, values):
        self.__dict__.update(zip(names, values))


class Place:
    def __init__(self, seen, space):
        self.spec, self.space = pl.BlockSpec(memory_space=seen), space

    def operand(self, array):
        if self.space is None:
            return array
        return pltpu.with_memory_space_constraint(array, self.space)

    def result(self, shape, kind):
        return jax.ShapeDtypeStruct(shape, kind) if self.space is None else self.space(shape, kind)


SCALARS = Place(pltpu.SMEM, None)
SMALL = Place(pltpu.VMEM, pltpu.HBM)
FAR = Place(pl.ANY, pltpu.HBM)
NEAR = Place(pltpu.VMEM, pltpu.VMEM)
TOKEN = pl.BlockSpec(memory_space=pl.ANY)
SPARE = 4 * MEG


def padded_bytes(shape, kind):
    *front, rows, columns = shape
    return math.prod(front) * -(-rows // 16) * 16 * -(-columns // 128) * 128 * jnp.dtype(kind).itemsize


def params(limit=8 * MEG):
    return pltpu.CompilerParams(vmem_limit_bytes=limit)


def cost(flops, moved):
    return pl.CostEstimate(flops=flops, bytes_accessed=moved, transcendentals=0)


ORDER = []


def run(kernel, name, ins, outs, scratch, copies=1, flops=1_000_000, moved=1_000_000, after=()):
    after = ORDER[-1:] + list(after)
    arrays, counts, specs, held_bytes = [], [], [], 0
    for value, place in ins.values():
        many = isinstance(value, (list, tuple))
        counts.append(len(value) if many else 0)
        for a in value if many else [value]:
            arrays.append(place.operand(a))
            specs.append(place.spec)
            held_bytes += padded_bytes(a.shape, a.dtype) if place is SMALL else 0
    shapes, out_specs = [], []
    for shape, kind, place in outs.values():
        many = isinstance(shape, list)
        counts.append(len(shape) if many else 0)
        for one in shape if many else [shape]:
            shapes.append(place.result(one, kind))
            out_specs.append(place.spec)
            held_bytes += 2 * padded_bytes(one, kind) if place is SMALL else 0
    held_bytes += sum(padded_bytes(*s) for s in scratch.values())

    def grouped(refs, counts):
        refs = list(refs)
        taken = []
        for count in counts:
            taken.append([refs.pop(0) for _ in range(count)] if count else refs.pop(0))
        return taken

    def body(*refs):
        refs = refs[: len(arrays)] + refs[len(arrays) + len(after) :]
        split = len(arrays) + len(shapes)
        go = Mover(refs[-1])
        kernel(
            Bag([*ins, *outs], grouped(refs[:split], counts)), Bag(scratch, refs[split:-1]), go
        )
        go.finish()

    results = pl.pallas_call(
        body,
        in_specs=specs + [TOKEN] * len(after),
        out_specs=out_specs,
        out_shape=shapes,
        scratch_shapes=[pltpu.VMEM(*s) for s in scratch.values()]
        + [pltpu.SemaphoreType.DMA((copies,))],
        compiler_params=params(held_bytes + SPARE),
        cost_estimate=cost(flops, moved),
        name=name,
    )(*arrays, *after)
    ORDER.append(results[0])
    return Bag(outs, grouped(results, counts[len(ins) :]))


def aligned(start, multiple, size=None):
    return pl.ds(pl.multiple_of(start, multiple), size or multiple)


SAVED = dict(
    summed=((ROWS, D), F32),
    qc=((ROWS, D), BF),
    qp=((ROWS, D), BF),
    qs=((ROWS, D), F32),
    kv=((KEYS, 2 * D), BF),
    rel=((WIDE, D), BF),
    mix=((ROWS, D), F32),
    prob=((PAIRS, 2 * ROWS, KEYS), F32),
)
FF_STEPS = 4
FF_BLOCK = FF // FF_STEPS


def attn_forward_body(layer, r, h, saved, w, go, ready):
    mine = slice(layer, layer + 1)
    go.wait(*ready)
    projected = dot_nn(h.x[...], w.wq[...])
    saved.qc[...] = ((projected + r.bias[0, mine, :]) * SCALE).astype(BF)
    saved.qp[...] = ((projected + r.bias[1, mine, :]) * SCALE).astype(BF)
    saved.qs[...] = (projected + r.bias[2, mine, :]) * SCALE
    saved.kv[...] = dot_nn(h.joined[...], w.wkv[...]).astype(BF)
    half = r.at[0] % 2
    rows = h.table[...] if layer == 0 else r.table[aligned(HALF * (1 - half), HALF, WIDE), :]
    saved.rel[...] = dot_nn(rows, w.wr[...]).astype(BF)
    hidden, differs = sight(r.at, r.lengths, r.ranks, r.segments)
    ones = jnp.ones((WIDE, KEYS), BF)
    beside = jnp.ones((KEYS, 2 * HEAD), BF)
    for p in range(PAIRS):
        at = slice(2 * HEAD * p, 2 * HEAD * (p + 1))
        later = slice(D + 2 * HEAD * p, D + 2 * HEAD * (p + 1))
        content = dot_nt(two_heads(saved.qc[:, at]), saved.kv[:, at])
        wide = dot_nt(two_heads(saved.qp[:, at]), saved.rel[:, at])
        segment = saved.qs[:, at]
        same = dot_nn(in_two(two_heads(segment * r.seg[layer, 0:1, at])), ones)
        other = dot_nn(in_two(two_heads(segment * r.seg[layer, 1:2, at])), ones)
        raw = content + skewed_scores(wide) + jnp.where(differs, other, same)
        scores = jnp.where(hidden, NEGATIVE, raw)
        exponent = jnp.exp(scores - jnp.max(scores, axis=-1, keepdims=True))
        values = jnp.concatenate([saved.kv[:, later], beside], axis=1)
        mixed = dot_nn(exponent.astype(BF), values)
        share = 1.0 / mixed[:, 2 * HEAD :]
        saved.prob[p] = exponent * jnp.concatenate([share, share[:, : KEYS - 2 * HEAD]], axis=1)
        attended = one_pair(mixed[:, : 2 * HEAD] * share)
        saved.mix[:, at] = attended
        h.att[:, at] = attended.astype(BF)
    summed = dot_nn(h.att[...], w.wo[...]) + h.x[...].astype(F32)
    saved.summed[...] = summed
    h.y[...] = (norm_parts(summed)[0] * r.again[mine, :] + r.ashift[mine, :]).astype(BF)


def ffn_forward_body(layer, r, h, w, go, ready=()):
    mine = slice(layer, layer + 1)
    y = h.y[...]
    go.wait(*ready)
    total = None
    for c in range(FF_STEPS):
        at = slice(FF_BLOCK * c, FF_BLOCK * (c + 1))
        pre = dot_nn(y, w.win[:, at]) + r.fbin[mine, at]
        h.pre[:, at] = pre
        part = dot_nn(gelu(pre).astype(BF), w.wout[at, :])
        total = part if total is None else total + part
    summed = total + r.fbout[mine, :] + y.astype(F32)
    h.fsum[...] = summed
    return (norm_parts(summed)[0] * r.fgain[mine, :] + r.fshift[mine, :]).astype(BF)


def ffn_backward_body(layer, grad, r, h, w):
    gsum, ggain, gshift = norm_back(h.fsum[...], r.fgain[layer : layer + 1, :], grad)
    low = gsum.astype(BF)
    gbias = jnp.sum(gsum, axis=0, keepdims=True)
    vectors = [ggain, gshift, gbias]
    total = gsum
    for c in range(FF_STEPS):
        at = slice(FF_BLOCK * c, FF_BLOCK * (c + 1))
        slope = gelu_both(h.pre[:, at])[1]
        gpre = (dot_nt(low, w.wout[at, :]) * slope).astype(BF)
        vectors.append(jnp.sum(gpre.astype(F32), axis=0, keepdims=True))
        total = total + dot_nt(gpre, w.win[:, at])
    vectors = jnp.concatenate(vectors + [jnp.zeros((1, D), F32)], axis=0)
    return total.astype(BF), low, vectors


def near_weights(layer, r):
    names = [n for n in WEIGHTS if n in r.__dict__]
    return Bag(names, [r.__dict__[n].at[layer] for n in names])


WEIGHTS = dict(
    wq=((D, D), BF), wkv=((D, 2 * D), BF), wr=((D, D), BF), wo=((D, D), BF), win=((D, FF), BF),
    wout=((FF, D), BF),
)
FORWARD_SCRATCH = dict(
    x=((ROWS, D), BF),
    joined=((KEYS, D), BF),
    att=((ROWS, D), BF),
    y=((ROWS, D), BF),
    pre=((ROWS, FF), F32),
    fsum=((ROWS, D), F32),
)


def forward_first_kernel(r, h, go):
    section = r.at[0]
    seq, half = section // 2, section % 2
    own = aligned(section * HALF, HALF)
    ready = [
        go(r.content.at[own], h.x.at[pl.ds(0, HALF)]),
        go(r.query.at[own], h.x.at[pl.ds(HALF, HALF)]),
        go(r.memory.at[0, aligned(seq * M, M)], h.joined.at[pl.ds(0, M)]),
        go(r.content.at[aligned(seq * S, S)], h.joined.at[pl.ds(M, S)]),
        go(r.table.at[aligned(HALF * (1 - half), HALF, WIDE)], h.table),
        go(r.wq.at[0], h.wq),
        go(r.wkv.at[0], h.wkv),
        go(r.wr.at[0], h.wr),
        go(r.wo.at[0], h.wo),
    ]
    later = [go(r.win.at[0], h.win), go(r.wout.at[0], h.wout)]
    attn_forward_body(0, r, h, h, h, go, ready)
    for n in SAVED:
        go(h.__dict__[n], r.__dict__[n])
    r.acts[:ROWS, :] = h.att[...]
    x = ffn_forward_body(0, r, h, h, go, later)
    go(h.pre, r.pre0)
    go(h.fsum, r.fsum0)
    r.acts[ROWS:, :] = x
    r.half[...] = x[:HALF]


def forward_second_kernel(r, h, go):
    section = r.at[0]
    seq, half = section // 2, section % 2
    own = aligned(section * HALF, HALF)
    w = near_weights(1, r)
    ready = [
        go(r.memory.at[1, aligned(seq * M, M)], h.joined.at[pl.ds(0, M)]),
        go(r.cotc.at[own], h.grad.at[pl.ds(0, HALF)]),
        go(r.cotq.at[own], h.grad.at[pl.ds(HALF, HALF)]),
    ]
    h.x[...] = r.acts0[ROWS:, :]
    h.joined[aligned(M + HALF * half, HALF), :] = r.acts0[ROWS : ROWS + HALF, :]
    h.joined[aligned(M + HALF * (1 - half), HALF), :] = r.other[...]
    attn_forward_body(1, r, h, r, w, go, ready)
    r.acts[:ROWS, :] = h.att[...]
    r.out[...] = ffn_forward_body(1, r, h, w, go)
    gy, low, vectors = ffn_backward_body(1, h.grad[...].astype(F32), r, h, w)
    r.acts[ROWS:, :] = low
    r.gy[...] = gy
    r.fvec[...] = vectors


def ffn_backward_kernel(r, h, go):
    go(r.fsum0, h.fsum)
    go(r.pre0, h.pre)
    w = near_weights(0, r)
    gx = r.gx
    grad = jnp.concatenate([gx[:HALF, :] + r.other[...].astype(F32), gx[HALF:, :]], axis=0)
    go.finish()
    gy, low, vectors = ffn_backward_body(0, grad.astype(BF).astype(F32), r, h, w)
    r.low[...] = low
    r.gy[...] = gy
    r.fvec[...] = vectors


def attn_backward_kernel(layer, r, h, go):
    section = r.at[0]
    half = section % 2
    mine = slice(layer, layer + 1)
    w = near_weights(layer, r)
    if layer == 0:
        for n in SAVED:
            go(r.__dict__[n], h.__dict__[n])
        go.finish()
    k = h if layer == 0 else r
    gsum, ggain, gshift = norm_back(k.summed[...], r.again[mine, :], r.gy[...].astype(F32))
    low = gsum.astype(BF)
    h.vec[0:1, :] = ggain
    h.vec[1:2, :] = gshift
    h.vec[7:15, :] = r.fvec[...]
    h.vec[15:16, :] = jnp.zeros((1, D), F32)
    g_attended = dot_nt(low, w.wo[...]).astype(BF)
    differs = sight(r.at, r.lengths, r.ranks, r.segments)[1]
    lowest = low_lanes()
    ones = jnp.ones((WIDE, KEYS), BF)
    for p in range(PAIRS):
        at = slice(2 * HEAD * p, 2 * HEAD * (p + 1))
        later = slice(D + 2 * HEAD * p, D + 2 * HEAD * (p + 1))
        prob = k.prob[p]
        ga = two_heads(g_attended[:, at])
        gprob = dot_nt(ga, k.kv[:, later])
        h.gkv[later, :] = dot_nn(ga.T, prob.astype(BF)).astype(BF)
        centre = dot_nn(in_two(two_heads(g_attended[:, at].astype(F32) * k.mix[:, at])), ones)
        gscores = (prob * (gprob - centre)).astype(BF)
        gqc = one_pair(dot_nn(gscores, k.kv[:, at]))
        h.gkv[at, :] = dot_nn(two_heads(k.qc[:, at]).T, gscores).astype(BF)
        gwhole = gscores.astype(F32)
        gwide = unskewed_scores(gwhole).astype(BF)
        gqp = one_pair(dot_nn(gwide, k.rel[:, at]))
        h.grel[at, :] = dot_nn(two_heads(k.qp[:, at]).T, gwide).astype(BF)
        other_part = jnp.where(differs, gwhole, 0.0)
        other = jnp.sum(other_part, axis=-1, keepdims=True)
        same = jnp.sum(gwhole - other_part, axis=-1, keepdims=True)
        same_pair = jnp.where(lowest, same[:ROWS], same[ROWS:])
        other_pair = jnp.where(lowest, other[:ROWS], other[ROWS:])
        gqs = same_pair * r.seg[layer, 0:1, at] + other_pair * r.seg[layer, 1:2, at]
        segment = k.qs[:, at]
        h.vec[2:3, at] = jnp.sum(gqc, axis=0, keepdims=True) * SCALE
        h.vec[3:4, at] = jnp.sum(gqp, axis=0, keepdims=True) * SCALE
        h.vec[4:5, at] = jnp.sum(gqs, axis=0, keepdims=True) * SCALE
        h.vec[5:6, at] = jnp.sum(same_pair * segment, axis=0, keepdims=True)
        h.vec[6:7, at] = jnp.sum(other_pair * segment, axis=0, keepdims=True)
        h.turned[at, :ROWS] = low[:, at].T
        h.turned[at, ROWS:] = ((gqc + gqp + gqs) * SCALE).astype(BF).T
    few = KEYS - 128
    for n, message in enumerate(r.first):
        d = section ^ n
        rows = aligned(SHARE * d, SHARE)
        message[:SHARE, :256] = h.turned[rows, :]
        message[:SHARE, 256:512] = h.grel[rows, :]
        for j in range(2):
            rows = aligned(SHARE * (2 * d + j), SHARE)
            message[:SHARE, 512 + 128 * j : 640 + 128 * j] = h.gkv[rows, :128]
            message[:SHARE, 768 + few * j : 768 + few * (j + 1)] = h.gkv[rows, 128:]
    joined = dot_nn(w.wkv[...], h.gkv[...])
    one, two = joined[:, M : M + HALF], joined[:, M + HALF :]
    first_half = jnp.zeros((1, 1), jnp.int32) + half == 0
    own, partner = jnp.where(first_half, one, two), jnp.where(first_half, two, one)
    gx = dot_nn(w.wq[...], h.turned[:, ROWS:]) + gsum.T
    gx = jnp.concatenate([gx[:, :HALF] + own, gx[:, HALF:]], axis=1)
    if layer > 0:
        r.send[...] = partner.T.astype(BF)
        r.gx[...] = gx.T
        r.second[:, : 2 * HALF] = r.out[...].T
        r.second[:, 2 * HALF :] = jnp.concatenate([partner, joined[:, :M]], axis=1).astype(BF)
        r.vec[...] = h.vec[...]
    else:
        h.second[:, : 2 * HALF] = gx.astype(BF)
        h.second[:, 2 * HALF : WIDE] = jnp.concatenate([partner, joined[:, :M]], axis=1).astype(BF)
        h.second[:, WIDE:] = r.later[...]
        for d in range(4):
            at = slice(SHARE * d, SHARE * (d + 1))
            for n, vec in enumerate((h.vec, r.vectors)):
                place = slice(SHARE * n, SHARE * (n + 1))
                wide = vec[10 + d : 11 + d, :]
                rows = [vec[:10, at]] + [wide[:, SHARE * j : SHARE * (j + 1)] for j in range(4)]
                rows = jnp.concatenate(rows + [jnp.zeros((2, SHARE), F32)], axis=0)
                h.parts[d, :, place] = rows.astype(BF)
        for n, message in enumerate(r.second):
            message[...] = h.second[aligned(SHARE * (section ^ n), SHARE), :]
        for n, message in enumerate(r.first):
            message[SHARE:, : 2 * SHARE] = h.parts[section ^ n]


def gathered_x(layer, r, h):
    for n in range(4):
        if layer == 0:
            rows = aligned((r.at[0] ^ n) * HALF, HALF)
            h.x[ROWS * n : ROWS * n + HALF, :] = r.content[rows, :]
            h.x[ROWS * n + HALF : ROWS * (n + 1), :] = r.query[rows, :]
        else:
            h.x[ROWS * n : ROWS * (n + 1), :] = r.before[n][ROWS:, :]


def put_halves(r, h):
    core = r.at[2]
    for j in range(4):
        r.kept[j] = h.pieces[2 * j + core]
        r.given[j] = h.pieces[2 * j + 1 - core]


def shares_kernel(r, h, go):
    wide, few = FF // 8, FF // 32
    for t in range(4):

        @pl.when(r.at[0] == t)
        def _():
            for d in range(8):
                at = slice(few * d, few * (d + 1))
                held = slice(wide * d + few * t, wide * d + few * (t + 1))
                r.bias[:, at] = r.fbin[:, held]
                for layer in range(LAYERS):
                    r.inner[layer, :, at] = r.win[layer, :, held]
                    r.outer[layer, at, :] = r.wout[layer, held, :]


def ffn_weights_kernel(layer, fast, r, h, go):
    mine = slice(layer, layer + 1)
    gathered_x(layer, r, h)
    attended = jnp.concatenate([a[:ROWS, :] for a in r.acts], axis=0)
    summed = dot_nn(attended, r.wo[layer]) + h.x[...].astype(F32)
    y = norm_parts(summed)[0] * r.again[mine, :] + r.ashift[mine, :]
    h.y[...] = y.astype(BF)
    for n, low in enumerate(r.low):
        rows = low[low.shape[0] - ROWS :, :]
        h.low[ROWS * n : ROWS * (n + 1), :] = rows
        h.lowt[:, ROWS * n : ROWS * (n + 1)] = rows.T
    width, few = FF // 8, FF // 32
    for t in range(2):
        at = slice(width * t, width * (t + 1))
        pre = dot_nn(h.y[...], r.inner[layer, :, at]) + r.bias[mine, at]
        active, slope = gelu_both(pre)
        gpre = (dot_nt(h.low[...], r.outer[layer, at, :]) * slope).astype(BF)
        grad_in = dot_nn(gpre.T, h.y[...]).astype(BF)
        grad_out = dot_nn(h.lowt[...], active.astype(BF)).astype(BF)
        if fast:
            for d in range(4):
                h.pieces[4 * t + d, :few, :] = grad_in[few * d : few * (d + 1), :]
            for d in range(8):
                h.pieces[d, few:, at] = grad_out[few * d : few * (d + 1), :]
        else:
            r.grads[0][at, :] = grad_in
            r.grads[1][:, at] = grad_out
    if fast:
        put_halves(r, h)


def attn_weights_kernel(layer, fast, r, h, go):
    section = r.at[0]
    half = section % 2
    gathered_x(layer, r, h)
    for pair in range(2):
        rows = aligned((section ^ (2 * pair)) // 2 * M, M)
        h.joined[pair, :M, :] = r.memory[layer, rows, :]
        for n in (2 * pair, 2 * pair + 1):
            place = half ^ (n & 1)
            h.joined[pair, aligned(M + HALF * place, HALF), :] = h.x[ROWS * n : ROWS * n + HALF, :]
    first = r.first
    low = jnp.concatenate([f[:SHARE, :128] for f in first], axis=1)
    proj = jnp.concatenate([f[:SHARE, 128:256] for f in first], axis=1)
    grad_q = dot_nn(proj, h.x[...]).astype(BF)
    attended = jnp.concatenate([a[:ROWS, :] for a in r.acts], axis=0)
    grad_o = dot_nn(low, attended).astype(BF)
    few = KEYS - 128
    grad_kv = None
    for pair in range(2):
        both = first[2 * pair][:SHARE, 512:].astype(F32) + first[2 * pair + 1][:SHARE, 512:].astype(F32)
        both = both.astype(BF)
        both = jnp.concatenate(
            [
                jnp.concatenate([both[:, :128], both[:, 256 : 256 + few]], axis=1),
                jnp.concatenate([both[:, 128:256], both[:, 256 + few :]], axis=1),
            ],
            axis=0,
        )
        part = dot_nn(both, h.joined[pair])
        grad_kv = part if grad_kv is None else grad_kv + part
    grad_kv = grad_kv.astype(BF)
    grad_rel = None
    for n in range(2):
        place = half ^ n
        total = first[n][:SHARE, 256:512].astype(F32) + first[n + 2][:SHARE, 256:512].astype(F32)
        rows = r.table[aligned(HALF * (1 - place), HALF, WIDE), :]
        part = dot_nn(total.astype(BF), rows)
        grad_rel = part if grad_rel is None else grad_rel + part
    grad_rel = grad_rel.astype(BF)
    if layer == 0:
        vectors = None
        for f in first:
            part = f[SHARE:, : 2 * SHARE].astype(F32)
            vectors = part if vectors is None else vectors + part
        if fast:
            for d in range(8):
                h.pieces[d, ROWS_ATTN:, :] = vectors.astype(BF)
        else:
            r.vectors[...] = vectors
    if fast:
        rows = SHARE // 2
        few = rows // 2
        left, right = slice(0, SHARE), slice(SHARE, 2 * SHARE)
        top, middle, bottom = slice(0, rows), slice(rows, 2 * rows), slice(2 * rows, ROWS_ATTN)
        for t in range(2):
            for s in range(4):
                piece = h.pieces.at[2 * (s ^ section) + t]
                at = slice(SHARE * s, SHARE * (s + 1))
                piece[top, left] = grad_q[rows * t : rows * (t + 1), at]
                piece[top, right] = grad_o[rows * t : rows * (t + 1), at]
                start = 2 * rows * t
                piece[middle, left] = grad_kv[start : start + rows, at]
                piece[middle, right] = grad_kv[start + rows : start + 2 * rows, at]
                start = rows * t
                piece[bottom, left] = grad_rel[start : start + few, at]
                piece[bottom, right] = grad_rel[start + few : start + rows, at]
        put_halves(r, h)
    else:
        for made, grad in zip(r.grads, (grad_q, grad_kv, grad_o, grad_rel)):
            made[...] = grad


def whole(shape):
    return pl.BlockSpec(shape, lambda i: (0,) * len(shape))


def gather_kernel(at_ref, *refs):
    section = at_ref[0]
    early = [r.at[:, pl.ds(0, WIDE)] for r in refs[:4]]
    late = [r.at[:, pl.ds(WIDE, WIDE)] for r in refs[:4]]
    small_ref = refs[4]
    outc_ref, outq_ref, gradc_ref, gradq_ref, mem_ref = refs[5:10]
    bias_ref, seg_ref, again_ref, ashift_ref, inb_ref, outb_ref, fgain_ref, fshift_ref = refs[10:18]

    def in_order(blocks):
        odd = jnp.zeros((1, 1), jnp.int32) + section % 2 == 1
        high = jnp.zeros((1, 1), jnp.int32) + section // 2 == 1
        a, b, c, d = blocks
        a, b, c, d = (
            jnp.where(odd, b, a), jnp.where(odd, a, b), jnp.where(odd, d, c), jnp.where(odd, c, d)
        )
        left, right = jnp.concatenate([a, b], axis=1), jnp.concatenate([c, d], axis=1)
        return jnp.concatenate([jnp.where(high, right, left), jnp.where(high, left, right)], axis=1)

    def blocks(four, start):
        return [f[:, start : start + HALF].astype(F32) for f in four]

    outc_ref[...] = in_order(blocks(late, 0)).astype(BF)
    outq_ref[...] = in_order(blocks(late, HALF)).astype(BF)
    own, passed = blocks(early, 0), blocks(early, 2 * HALF)
    gradc_ref[...] = in_order([own[k] + passed[k ^ 1] for k in range(4)])
    gradq_ref[...] = in_order(blocks(early, HALF))
    high = jnp.zeros((1, 1), jnp.int32) + section // 2 == 1
    for layer, four in ((0, early), (1, late)):
        a, b, c, d = blocks(four, 3 * HALF)
        one, two = a + b, c + d
        mem_ref[layer] = jnp.concatenate(
            [jnp.where(high, two, one), jnp.where(high, one, two)], axis=1
        )
    for layer in range(LAYERS):
        mine = slice(layer, layer + 1)

        held = slice(SHARE * layer, SHARE * (layer + 1))

        def vector(row):
            return small_ref[row : row + 1, held].astype(F32)

        for j in range(3):
            bias_ref[j, mine, :] = vector(2 + j)
        for j in range(2):
            seg_ref[layer, j : j + 1, :] = vector(5 + j)
        again_ref[mine, :] = vector(0)
        ashift_ref[mine, :] = vector(1)
        fgain_ref[mine, :] = vector(7)
        fshift_ref[mine, :] = vector(8)
        outb_ref[mine, :] = vector(9)
        for j in range(4):
            inb_ref[mine, SHARE * j : SHARE * (j + 1)] = vector(10 + j)


def gather_rows(at, rows_out, small):
    rows = 4 * HALF
    vector = ((LAYERS, SHARE), F32)
    shapes = [
        ((SHARE, rows), BF),
        ((SHARE, rows), BF),
        ((SHARE, rows), F32),
        ((SHARE, rows), F32),
        ((LAYERS, SHARE, 2 * M), F32),
        ((3, LAYERS, SHARE), F32),
        ((LAYERS, 2, SHARE), F32),
        vector,
        vector,
        ((LAYERS, FF // 4), F32),
        vector,
        vector,
        vector,
    ]
    return pl.pallas_call(
        gather_kernel,
        grid=(1,),
        in_specs=[SCALARS.spec] + [whole(a.shape) for a in (*rows_out, small)],
        out_specs=[whole(s) for s, _ in shapes],
        out_shape=[jax.ShapeDtypeStruct(s, t) for s, t in shapes],
        compiler_params=params(),
        cost_estimate=cost(1_000_000, 2_000_000),
        name="gather_rows",
    )(at, *rows_out, small)


def final_kernel(r, h, go):
    rows, few = SHARE // 2, FF // 32
    small = rows // 2
    section = r.at[0]
    for layer in range(LAYERS):
        for n, message in enumerate(r.ffn[4 * layer : 4 * (layer + 1)]):
            h.got[section ^ n] = message[...].astype(F32)
        for s in range(4):
            held = slice(few * s, few * (s + 1))
            r.fin[layer, :, held] = h.got[s, :, :SHARE].T
            for e in range(2):
                place = slice(FF // 8 * e + few * s, FF // 8 * e + few * (s + 1))
                start = SHARE + few * e
                r.fout[layer, :, place] = h.got[s, :, start : start + few]
        total = r.attn[layer][...].astype(F32)
        r.q[layer] = total[:rows, :SHARE].T
        r.o[layer] = total[:rows, SHARE:].T
        kv = jnp.concatenate([total[rows : 2 * rows, :SHARE], total[rows : 2 * rows, SHARE:]], axis=0)
        r.kv[layer] = kv.T
        rel = jnp.concatenate([total[2 * rows :, :SHARE], total[2 * rows :, SHARE:]], axis=0)
        r.rel[layer] = rel.T


def final_weights(at, ffn, attn):
    half = (LAYERS, SHARE, SHARE // 2)
    return run(
        final_kernel,
        "final_weights",
        dict(at=(at, SCALARS), ffn=(ffn, NEAR), attn=(attn, NEAR)),
        dict(
            q=(half, F32, SMALL),
            kv=((LAYERS, SHARE, SHARE), F32, SMALL),
            o=(half, F32, SMALL),
            rel=(half, F32, SMALL),
            fin=((LAYERS, SHARE, FF // 8), F32, SMALL),
            fout=((LAYERS, D // 8, FF // 4), F32, SMALL),
        ),
        dict(got=((4, FF // 32, 2 * SHARE), F32)),
    )


def add(a, b):
    return (a.astype(F32) + b.astype(F32)).astype(BF)


def split_kernel(r, h, go):
    chip = r.at[1]
    r.keep[0], r.keep[1] = [add(r.kept[p], r.got[p]) for p in (chip, chip ^ 2)]
    r.send[0], r.send[1] = [add(r.kept[p], r.got[p]) for p in (chip ^ 1, chip ^ 3)]


def fold_kernel(r, h, go):
    r.own[...], r.far[...] = [add(r.keep[n], r.got[n]) for n in range(2)]


def sum_kernel(r, h, go):
    total = add(r.own[...], r.got[...])
    r.total[...] = total[:ROWS_ATTN]
    if total.shape[0] > ROWS_ATTN:
        r.vectors[...] = total[ROWS_ATTN:]


def shared_kernel(r, h, go):
    few = FF // 32
    total = add(r.own[...], r.got[...])
    for t in range(4):
        at = slice(SHARE * t, SHARE * (t + 1))
        h.parts[t, :, :SHARE], h.parts[t, :, SHARE:] = total[:few, at], total[few:, at]
    for n, part in enumerate(r.parts):
        part[...] = h.parts[r.at[0] ^ n]


def split_pieces(at, made):
    got = swapped(made.given, DP, 1)
    shape = (2,) + made.kept.shape[1:]
    ins = dict(at=(at, SCALARS), kept=(made.kept, NEAR), got=(got, NEAR))
    return run(
        split_kernel, "split_pieces", ins, dict(keep=(shape, BF, NEAR), send=(shape, BF, NEAR)), {}
    )


def fold_pieces(split, got):
    shape = got.shape[1:]
    ins = dict(keep=(split.keep, NEAR), got=(got, NEAR))
    return run(
        fold_kernel, "fold_pieces", ins, dict(own=(shape, BF, NEAR), far=(shape, BF, NEAR)), {}
    )


def sum_pieces(folded, got):
    ins = dict(own=(folded.own, NEAR), got=(got, NEAR))
    outs = dict(total=((ROWS_ATTN, got.shape[1]), BF, NEAR))
    if got.shape[0] > ROWS_ATTN:
        outs.update(vectors=((ROWS_VEC, got.shape[1]), BF, NEAR))
    return run(sum_kernel, "sum_pieces", ins, outs, {})


def shared_pieces(at, folded, got):
    ins = dict(at=(at, SCALARS), own=(folded.own, NEAR), got=(got, NEAR))
    shape = (FF // 32, 2 * SHARE)
    return run(
        shared_kernel, "shared_pieces", ins, dict(parts=([shape] * 4, BF, NEAR)),
        dict(parts=((4,) + shape, BF)),
    ).parts


def swapped(x, axis, k):
    return lax.ppermute(x, axis, [(i, i ^ k) for i in range(lax.axis_size(axis))])


def from_all(x):
    return [x] + [swapped(x, SECTION, k) for k in (1, 2, 3)]


def messages(parts):
    return [parts[0]] + [swapped(parts[k], SECTION, k) for k in (1, 2, 3)]


def to_owner(piece):
    pairs = [
        (8 * s + 2 * z + c, 8 * (s ^ z) + 2 * s + c)
        for s in range(4) for z in range(4) for c in range(2)
    ]
    return lax.ppermute(piece, (SECTION, DP), pairs)


def on_device(
    content_in,
    query_in,
    memory,
    doc_lengths,
    perm_rank,
    segment_ids,
    w_query,
    w_keyval,
    w_out,
    w_rel,
    head_bias,
    seg_embed,
    attn_gain,
    attn_shift,
    ffn_in,
    ffn_in_bias,
    ffn_out,
    ffn_out_bias,
    ffn_gain,
    ffn_shift,
    cot_content,
    cot_query,
):
    ORDER.clear()
    dp = lax.axis_size(DP)
    fast = dp == 8
    index = lax.axis_index(DP)
    at = jnp.stack([lax.axis_index(SECTION), index // 2, index % 2]).astype(jnp.int32)
    table = position_table()
    marks = dict(
        at=(at, SCALARS),
        lengths=(doc_lengths, SCALARS),
        ranks=(perm_rank, SMALL),
        segments=(segment_ids, SMALL),
    )
    attn_v = dict(
        bias=(head_bias.transpose(1, 0, 2), SMALL),
        seg=(seg_embed, SMALL),
        again=(attn_gain, SMALL),
        ashift=(attn_shift, SMALL),
    )
    ffn_v = dict(
        fbin=(ffn_in_bias, SMALL),
        fbout=(ffn_out_bias, SMALL),
        fgain=(ffn_gain, SMALL),
        fshift=(ffn_shift, SMALL),
    )
    matrices = dict(
        wq=w_query, wkv=w_keyval, wr=w_rel, wo=w_out, win=ffn_in, wout=ffn_out,
    )
    near = {n: (a, NEAR) for n, a in matrices.items()}

    def of(which, *names):
        return {n: which[n] for n in which if n in names}

    first = run(
        forward_first_kernel,
        "forward_first",
        dict(
            **marks,
            content=(content_in, FAR),
            query=(query_in, FAR),
            memory=(memory, FAR),
            table=(table, FAR),
            **{n: (a, FAR) for n, a in matrices.items()},
            **attn_v,
            **ffn_v,
        ),
        dict(
            acts=((2 * ROWS, D), BF, NEAR),
            half=((HALF, D), BF, NEAR),
            pre0=((ROWS, FF), F32, FAR),
            fsum0=((ROWS, D), F32, FAR),
            **{n: (*s, FAR) for n, s in SAVED.items()},
        ),
        dict(**FORWARD_SCRATCH, table=((WIDE, D), BF), **WEIGHTS, **SAVED),
        copies=24,
        flops=2_400_000_000,
        moved=16_000_000,
    )
    other = swapped(first.half, SECTION, 1)
    acts0 = from_all(first.acts)
    second = run(
        forward_second_kernel,
        "forward_second",
        dict(
            **marks,
            acts0=(first.acts, NEAR),
            other=(other, NEAR),
            memory=(memory, FAR),
            table=(table, NEAR),
            cotc=(cot_content, FAR),
            cotq=(cot_query, FAR),
            **near,
            **attn_v,
            **ffn_v,
        ),
        dict(
            acts=((2 * ROWS, D), BF, NEAR),
            out=((ROWS, D), BF, NEAR),
            gy=((ROWS, D), BF, NEAR),
            fvec=((8, D), F32, NEAR),
            **{n: (*s, NEAR) for n, s in SAVED.items()},
        ),
        dict(**FORWARD_SCRATCH, grad=((ROWS, D), BF)),
        copies=4,
        flops=3_600_000_000,
        moved=16_000_000,
    )
    acts1 = from_all(second.acts)

    def attn_backward(layer, saved, gy, fvec, after=(), **extra):
        ins = dict(
            **marks,
            gy=(gy, NEAR),
            fvec=(fvec, NEAR),
            **{n: (saved.__dict__[n], FAR if layer == 0 else NEAR) for n in SAVED},
            **{n: near[n] for n in list(WEIGHTS)[:4] if n != list(WEIGHTS)[2]},
            **attn_v,
            **{n: (a, NEAR) for n, a in extra.items()},
        )
        scratch = dict(
            vec=((16, D), F32),
            turned=((D, 2 * ROWS), BF),
            gkv=((2 * D, KEYS), BF),
            grel=((D, WIDE), BF),
        )
        rows = FIRST[0] + (16 if layer == 0 else 0)
        outs = dict(first=([(rows, FIRST[1])] * 4, BF, NEAR))
        if layer == 0:
            outs.update(second=([SECOND] * 4, BF, NEAR))
            scratch.update(SAVED, second=((D, 2 * WIDE), BF), parts=((4, 16, 2 * SHARE), BF))
        else:
            outs.update(
                second=((D, WIDE), BF, NEAR),
                gx=((ROWS, D), F32, NEAR),
                send=((HALF, D), BF, NEAR),
                vec=((16, D), F32, NEAR),
            )
        return run(
            functools.partial(attn_backward_kernel, layer), "attn_backward", ins, outs, scratch,
            copies=10, flops=1_800_000_000, moved=10_000_000, after=after,
        )

    def inputs_of(layer):
        if layer == 0:
            return dict(content=(content_in, NEAR), query=(query_in, NEAR))
        return dict(before=(acts0, NEAR))

    def grads_of(shape, plain):
        if fast:
            whole_shape = (4,) + shape
            return dict(kept=(whole_shape, BF, NEAR), given=(whole_shape, BF, NEAR))
        return dict(grads=(plain, BF, SMALL))

    def ffn_weights(layer, acts, lows):
        ins = dict(
            at=marks["at"],
            **inputs_of(layer),
            **of(near, "wo"),
            **of(attn_v, "again", "ashift"),
            inner=(shares.inner, NEAR),
            outer=(shares.outer, NEAR),
            bias=(shares.bias, NEAR),
            acts=(acts, NEAR),
            low=(lows, NEAR),
        )
        shape = (ROWS_FFN, D)
        tall = ((4 * ROWS, D), BF)
        return run(
            functools.partial(ffn_weights_kernel, layer, fast),
            "ffn_weights",
            ins,
            grads_of(shape, [(D, D), (D, D)]),
            dict(x=tall, y=tall, low=tall, lowt=((D, 4 * ROWS), BF), pieces=((8,) + shape, BF)),
            flops=3_600_000_000,
            moved=8_000_000,
        )

    def attn_weights(layer, acts, notes):
        ins = dict(
            at=marks["at"],
            **inputs_of(layer),
            memory=(memory, NEAR),
            table=(table, NEAR),
            acts=(acts, NEAR),
            first=(notes, NEAR),
        )
        shape = (ROWS_ATTN + (ROWS_VEC if layer == 0 else 0), 2 * SHARE)
        outs = grads_of(shape, [(SHARE, D), (2 * SHARE, D), (SHARE, D), (SHARE, D)])
        if layer == 0 and not fast:
            outs.update(vectors=((ROWS_VEC, 2 * SHARE), F32, SMALL))
        return run(
            functools.partial(attn_weights_kernel, layer, fast),
            "attn_weights",
            ins,
            outs,
            dict(x=((4 * ROWS, D), BF), joined=((2, KEYS, D), BF), pieces=((8,) + shape, BF)),
            flops=1_000_000_000,
            moved=5_000_000,
        )

    back1 = attn_backward(1, second, second.gy, second.fvec, acts0[1:], out=second.out)
    received = swapped(back1.send, SECTION, 1)
    parts1 = messages(back1.first)
    shares = run(
        shares_kernel,
        "shares",
        dict(at=marks["at"], **of(near, "win", "wout"), **of(ffn_v, "fbin")),
        dict(
            inner=((LAYERS, D, D), BF, NEAR),
            outer=((LAYERS, D, D), BF, NEAR),
            bias=((LAYERS, D), F32, NEAR),
        ),
        {},
    )
    third = run(
        ffn_backward_kernel,
        "ffn_backward",
        dict(
            gx=(back1.gx, NEAR),
            other=(received, NEAR),
            fsum0=(first.fsum0, FAR),
            pre0=(first.pre0, FAR),
            **of(near, "win", "wout"),
            **of(ffn_v, "fgain"),
        ),
        dict(
            low=((ROWS, D), BF, NEAR), gy=((ROWS, D), BF, NEAR), fvec=((8, D), F32, NEAR)
        ),
        dict(fsum=((ROWS, D), F32), pre=((ROWS, FF), F32)),
        copies=4,
        flops=1_200_000_000,
        moved=12_000_000,
        after=acts1[1:],
    )
    lows0 = from_all(third.low)
    fgrads1 = ffn_weights(1, acts1, acts1)
    back0 = attn_backward(
        0, first, third.gy, third.fvec, later=back1.second, vectors=back1.vec
    )
    parts0 = messages(back0.first)
    rows_out = messages(back0.second)
    if fast:
        split_f1 = split_pieces(at, fgrads1)
        z_f1 = swapped(split_f1.send, DP, 2)
        agrads1 = attn_weights(1, acts1, parts1)
        fgrads0 = ffn_weights(0, acts0, lows0)
        split_a1 = split_pieces(at, agrads1)
        z_a1 = swapped(split_a1.send, DP, 2)
        fold_f1 = fold_pieces(split_f1, z_f1)
        z_f1 = swapped(fold_f1.far, DP, 4)
        split_f0 = split_pieces(at, fgrads0)
        z_f0 = swapped(split_f0.send, DP, 2)
        agrads0 = attn_weights(0, acts0, parts0)
        fold_a1 = fold_pieces(split_a1, z_a1)
        z_a1 = swapped(fold_a1.far, DP, 4)
        split_a0 = split_pieces(at, agrads0)
        z_a0 = swapped(split_a0.send, DP, 2)
        ffn1 = messages(shared_pieces(at, fold_f1, z_f1))
        fold_f0 = fold_pieces(split_f0, z_f0)
        z_f0 = swapped(fold_f0.far, DP, 4)
        attn1 = to_owner(sum_pieces(fold_a1, z_a1).total)
        fold_a0 = fold_pieces(split_a0, z_a0)
        z_a0 = swapped(fold_a0.far, DP, 4)
        ffn0 = messages(shared_pieces(at, fold_f0, z_f0))
        sum_a0 = sum_pieces(fold_a0, z_a0)
        attn0 = to_owner(sum_a0.total)
        outs = gather_rows(at, rows_out, sum_a0.vectors)
        made = final_weights(at, ffn0 + ffn1, [attn0, attn1])
        wq, wkv, wo, wr, fin, fout = made.q, made.kv, made.o, made.rel, made.fin, made.fout
        fout = fout.transpose(0, 2, 1)
    else:
        agrads1 = attn_weights(1, acts1, parts1)
        fgrads0 = ffn_weights(0, acts0, lows0)
        agrads0 = attn_weights(0, acts0, parts0)
        outs = gather_rows(at, rows_out, lax.psum(agrads0.vectors, DP))
        section = at[0]

        def owned(rows):
            part = rows.reshape((dp, -1) + rows.shape[1:])
            part = lax.psum_scatter(part, DP, scatter_dimension=0, tiled=False)
            part = lax.psum(part, SECTION)
            width = part.shape[1] // 4
            return lax.dynamic_slice_in_dim(part, section * width, width, 1).astype(F32).T

        def at_share(share, count, axis=0):
            cut = share.reshape(share.shape[:axis] + (count, 1, -1) + share.shape[axis + 1 :])
            full = jnp.zeros(cut.shape[: axis + 1] + (4,) + cut.shape[axis + 2 :], BF)
            full = lax.dynamic_update_slice_in_dim(full, cut, section, axis + 1)
            return full.reshape(share.shape[:axis] + (-1,) + share.shape[axis + 1 :])

        def plain(fgrads, agrads):
            parts = [at_share(a, 1) for a in agrads]
            parts += [at_share(fgrads[0], 8), at_share(fgrads[1], 8, 1)]
            return [owned(a) for a in parts]

        pairs = zip(plain(fgrads0.grads, agrads0.grads), plain(fgrads1.grads, agrads1.grads))
        wq, wkv, wo, wr, fin, fout = [jnp.stack(p) for p in pairs]
    return (
        outs[0].T,
        outs[1].T,
        outs[2].T,
        outs[3].T,
        outs[4].transpose(0, 2, 1),
        wq,
        wkv,
        wo,
        wr,
        outs[5].transpose(1, 0, 2),
        outs[6],
        outs[7],
        outs[8],
        fin,
        outs[9],
        fout,
        outs[10],
        outs[11],
        outs[12],
    )


def solution(mesh):
    in_specs = (
        P(DP, None),
        P(DP, None),
        P(None, DP, None),
        P(DP),
        P(DP, None),
        P(DP, None),
    ) + (P(),) * 14 + (P(DP, None), P(DP, None))
    weight, vector = P(None, SECTION, DP), P(None, SECTION)
    out_specs = (
        P(DP, SECTION),
        P(DP, SECTION),
        P(DP, SECTION),
        P(DP, SECTION),
        P(None, DP, SECTION),
        weight,
        weight,
        weight,
        weight,
        P(None, None, SECTION),
        P(None, None, SECTION),
        vector,
        vector,
        weight,
        vector,
        weight,
        vector,
        vector,
        vector,
    )
    return jax.shard_map(
        on_device, mesh=mesh, in_specs=in_specs, out_specs=out_specs, check_vma=False
    )
```

```python
import functools
import math

import jax
import jax.numpy as jnp
import numpy as np
from jax import lax
from jax.experimental import pallas as pl
from jax.experimental.pallas import tpu as pltpu
from jax.sharding import PartitionSpec as P

D = 768
HEADS = 12
HEAD = 64
FF = 3072
S = 128
M = 64
LAYERS = 2
HALF = S // 2
KEYS = M + S
TABLE = M + 2 * S - 1
WIDE = 256
ROWS = 2 * HALF
PAIRS = HEADS // 2
SHARE = D // 4
SCALE = HEAD**-0.5
NEGATIVE = -1e30
EPSILON = 1e-05
SECTION, DP = "section", "dp"
BF = jnp.bfloat16
F32 = jnp.float32
GELU_C = math.sqrt(2.0 / math.pi)
MEG = 1 << 20

FIRST = (SHARE, 7 * 128)
SECOND = (SHARE, 2 * WIDE)
ROWS_ATTN = 120
ROWS_VEC = 8
ROWS_FFN = FF // 16


def position_table():
    distance = (M + S - 1 - np.arange(TABLE)).astype(np.float32)
    inverse = np.exp(np.arange(0, D, 2).astype(np.float32) * np.float32(-math.log(10000.0) / D))
    angles = distance[:, None] * inverse[None, :].astype(np.float32)
    table = np.concatenate([np.sin(angles), np.cos(angles)], axis=1)
    table = np.concatenate([table, np.zeros((1, D), np.float32)], axis=0)
    return jnp.asarray(table, jnp.float32).astype(BF)


def dot_nn(a, b):
    return lax.dot_general(a, b, (((1,), (0,)), ((), ())), preferred_element_type=F32)


def dot_nt(a, b):
    return lax.dot_general(a, b, (((1,), (1,)), ((), ())), preferred_element_type=F32)


def norm_parts(values):
    centre = values - jnp.mean(values, axis=-1, keepdims=True)
    spread = jnp.mean(centre * centre, axis=-1, keepdims=True)
    root = lax.rsqrt(spread + EPSILON)
    return centre * root, root


def norm_back(values, gain, grad):
    normal, root = norm_parts(values)
    scaled = grad * gain
    grad_gain = jnp.sum(grad * normal, axis=0, keepdims=True)
    grad_shift = jnp.sum(grad, axis=0, keepdims=True)
    first = jnp.mean(scaled, axis=-1, keepdims=True)
    second = jnp.mean(scaled * normal, axis=-1, keepdims=True)
    return root * (scaled - first - normal * second), grad_gain, grad_shift


def gelu(v):
    return 0.5 * v * (1.0 + jnp.tanh(GELU_C * (v + 0.044715 * (v * v * v))))


def gelu_both(v):
    square = v * v
    bend = jnp.tanh(GELU_C * (v + 0.044715 * (square * v)))
    half = 0.5 * (1.0 + bend)
    slope = half + 0.5 * v * (1.0 - bend * bend) * (GELU_C * (1.0 + 3 * 0.044715 * square))
    return v * half, slope


def low_lanes():
    return lax.broadcasted_iota(jnp.int32, (1, 2 * HEAD), 1) < HEAD


def two_heads(pair):
    low = low_lanes()
    zero = jnp.zeros_like(pair)
    return jnp.concatenate([jnp.where(low, pair, zero), jnp.where(low, zero, pair)], axis=0)


def one_pair(stacked):
    half = stacked.shape[0] // 2
    return jnp.where(low_lanes(), stacked[:half], stacked[half:])


def in_two(values):
    high = values.astype(BF)
    return jnp.concatenate([high, (values - high.astype(F32)).astype(BF)], axis=1)


def skewed_scores(wide):
    parts = [
        pltpu.roll(wide[HALF * b : HALF * (b + 1)], WIDE - HALF + 1, 1, stride=1, stride_axis=0)
        for b in range(4)
    ]
    return jnp.concatenate(parts, axis=0)[:, :KEYS]


def unskewed_scores(scores):
    rows, wide = 4 * HALF, WIDE // 2
    shift = HALF - 1 - lax.broadcasted_iota(jnp.int32, (rows, wide), 0) % HALF
    lane = lax.broadcasted_iota(jnp.int32, (rows, wide), 1)
    source = (lane - shift) & (wide - 1)
    wrapped = lane < shift
    rest = jnp.concatenate([scores[:, wide:], jnp.zeros((rows, WIDE - KEYS), F32)], axis=1)
    first, second = (
        jnp.take_along_axis(a, source, axis=1, mode=lax.GatherScatterMode.PROMISE_IN_BOUNDS)
        for a in (scores[:, :wide], rest)
    )
    return jnp.concatenate(
        [jnp.where(wrapped, 0.0, first), jnp.where(wrapped, first, second)], axis=1
    )


def sight(at_ref, lengths_ref, ranks_ref, segments_ref):
    seq, half = at_ref[0] // 2, at_ref[0] % 2
    ranks = ranks_ref[pl.ds(seq, 1), :]
    segments = segments_ref[pl.ds(seq, 1), :]
    place = lax.broadcasted_iota(jnp.int32, (1, S), 1)
    live = jnp.where(place < lengths_ref[seq], ranks, 2 * S)
    key_rank = jnp.concatenate([jnp.full((1, M), -1, jnp.int32), live], axis=1)
    key_segment = jnp.concatenate([jnp.zeros((1, M), jnp.int32), segments], axis=1)
    row = lax.broadcasted_iota(jnp.int32, (HALF, S), 0) + half * HALF
    column = lax.broadcasted_iota(jnp.int32, (HALF, S), 1)

    def upright(values):
        wide = jnp.where(row == column, values.astype(F32), 0.0)
        return jnp.sum(wide, axis=-1, keepdims=True).astype(jnp.int32)

    own_rank, own_segment = upright(ranks), upright(segments)
    reach = jnp.concatenate([own_rank, own_rank - 1], axis=0)
    hidden = jnp.where(key_rank <= reach, 0.0, 1.0)
    differs = jnp.where(jnp.concatenate([own_segment] * 2, axis=0) != key_segment, 1.0, 0.0)
    return [jnp.concatenate([a] * 2, axis=0) > 0.0 for a in (hidden, differs)]


class Mover:
    def __init__(self, semaphores):
        self.semaphores, self.count, self.open = semaphores, 0, []

    def __call__(self, source, target):
        copy = pltpu.make_async_copy(source, target, self.semaphores.at[self.count])
        self.count += 1
        copy.start()
        self.open.append(copy)
        return copy

    def wait(self, *copies):
        for copy in copies:
            if any(copy is other for other in self.open):
                self.open = [other for other in self.open if other is not copy]
                copy.wait()

    def finish(self):
        self.wait(*list(self.open))


class Bag:
    def __init__(self, names, values):
        self.__dict__.update(zip(names, values))


class Place:
    def __init__(self, seen, space):
        self.spec, self.space = pl.BlockSpec(memory_space=seen), space

    def operand(self, array):
        if self.space is None:
            return array
        return pltpu.with_memory_space_constraint(array, self.space)

    def result(self, shape, kind):
        return jax.ShapeDtypeStruct(shape, kind) if self.space is None else self.space(shape, kind)


SCALARS = Place(pltpu.SMEM, None)
SMALL = Place(pltpu.VMEM, pltpu.HBM)
FAR = Place(pl.ANY, pltpu.HBM)
NEAR = Place(pltpu.VMEM, pltpu.VMEM)
TOKEN = pl.BlockSpec(memory_space=pl.ANY)
SPARE = 4 * MEG


def padded_bytes(shape, kind):
    *front, rows, columns = shape
    return math.prod(front) * -(-rows // 16) * 16 * -(-columns // 128) * 128 * jnp.dtype(kind).itemsize


def params(limit=8 * MEG):
    return pltpu.CompilerParams(vmem_limit_bytes=limit)


def cost(flops, moved):
    return pl.CostEstimate(flops=flops, bytes_accessed=moved, transcendentals=0)


ORDER = []


def run(kernel, name, ins, outs, scratch, copies=1, flops=1000, moved=1000, after=()):
    after = ORDER[-1:] + list(after)
    arrays, counts, specs, held_bytes = [], [], [], 0
    for value, place in ins.values():
        many = isinstance(value, (list, tuple))
        counts.append(len(value) if many else 0)
        for a in value if many else [value]:
            arrays.append(place.operand(a))
            specs.append(place.spec)
            held_bytes += padded_bytes(a.shape, a.dtype) if place is SMALL else 0
    shapes, out_specs = [], []
    for shape, kind, place in outs.values():
        many = isinstance(shape, list)
        counts.append(len(shape) if many else 0)
        for one in shape if many else [shape]:
            shapes.append(place.result(one, kind))
            out_specs.append(place.spec)
            held_bytes += 2 * padded_bytes(one, kind) if place is SMALL else 0
    held_bytes += sum(padded_bytes(*s) for s in scratch.values())

    def grouped(refs, counts):
        refs = list(refs)
        taken = []
        for count in counts:
            taken.append([refs.pop(0) for _ in range(count)] if count else refs.pop(0))
        return taken

    def body(*refs):
        refs = refs[: len(arrays)] + refs[len(arrays) + len(after) :]
        split = len(arrays) + len(shapes)
        go = Mover(refs[-1])
        kernel(
            Bag([*ins, *outs], grouped(refs[:split], counts)), Bag(scratch, refs[split:-1]), go
        )
        go.finish()

    results = pl.pallas_call(
        body,
        in_specs=specs + [TOKEN] * len(after),
        out_specs=out_specs,
        out_shape=shapes,
        scratch_shapes=[pltpu.VMEM(*s) for s in scratch.values()]
        + [pltpu.SemaphoreType.DMA((copies,))],
        compiler_params=params(held_bytes + SPARE),
        cost_estimate=cost(flops, moved),
        name=name,
    )(*arrays, *after)
    ORDER.append(results[0])
    return Bag(outs, grouped(results, counts[len(ins) :]))


def aligned(start, multiple, size=None):
    return pl.ds(pl.multiple_of(start, multiple), size or multiple)


SAVED = dict(
    summed=((ROWS, D), F32),
    qc=((ROWS, D), BF),
    qp=((ROWS, D), BF),
    qs=((ROWS, D), F32),
    kv=((KEYS, 2 * D), BF),
    rel=((WIDE, D), BF),
    mix=((ROWS, D), F32),
    prob=((PAIRS, 2 * ROWS, KEYS), F32),
)
FF_STEPS = 4
FF_BLOCK = FF // FF_STEPS


def attn_forward_body(layer, r, h, saved, w, go, ready, after=()):
    mine = slice(layer, layer + 1)
    go.wait(*ready)
    started = [go(*pair) for pair in after]
    projected = dot_nn(h.x[...], w.wq[...])
    saved.qc[...] = ((projected + r.bias[0, mine, :]) * SCALE).astype(BF)
    saved.qp[...] = ((projected + r.bias[1, mine, :]) * SCALE).astype(BF)
    saved.qs[...] = (projected + r.bias[2, mine, :]) * SCALE
    saved.kv[...] = dot_nn(h.joined[...], w.wkv[...]).astype(BF)
    half = r.at[0] % 2
    rows = h.table[...] if layer == 0 else r.table[aligned(HALF * (1 - half), HALF, WIDE), :]
    saved.rel[...] = dot_nn(rows, w.wr[...]).astype(BF)
    hidden, differs = sight(r.at, r.lengths, r.ranks, r.segments)
    ones = jnp.ones((WIDE, KEYS), BF)
    beside = jnp.ones((KEYS, 2 * HEAD), BF)
    for p in range(PAIRS):
        at = slice(2 * HEAD * p, 2 * HEAD * (p + 1))
        later = slice(D + 2 * HEAD * p, D + 2 * HEAD * (p + 1))
        content = dot_nt(two_heads(saved.qc[:, at]), saved.kv[:, at])
        wide = dot_nt(two_heads(saved.qp[:, at]), saved.rel[:, at])
        segment = saved.qs[:, at]
        same = dot_nn(in_two(two_heads(segment * r.seg[layer, 0:1, at])), ones)
        other = dot_nn(in_two(two_heads(segment * r.seg[layer, 1:2, at])), ones)
        raw = content + skewed_scores(wide) + jnp.where(differs, other, same)
        scores = jnp.where(hidden, NEGATIVE, raw)
        exponent = jnp.exp(scores - jnp.max(scores, axis=-1, keepdims=True))
        values = jnp.concatenate([saved.kv[:, later], beside], axis=1)
        mixed = dot_nn(exponent.astype(BF), values)
        share = 1.0 / mixed[:, 2 * HEAD :]
        saved.prob[p] = exponent * jnp.concatenate([share, share[:, : KEYS - 2 * HEAD]], axis=1)
        attended = one_pair(mixed[:, : 2 * HEAD] * share)
        saved.mix[:, at] = attended
        h.att[:, at] = attended.astype(BF)
    summed = dot_nn(h.att[...], w.wo[...]) + h.x[...].astype(F32)
    saved.summed[...] = summed
    h.y[...] = (norm_parts(summed)[0] * r.again[mine, :] + r.ashift[mine, :]).astype(BF)
    return started


def ffn_forward_body(layer, r, h, w, go, ready=()):
    mine = slice(layer, layer + 1)
    y = h.y[...]
    go.wait(*ready)
    total = None
    for c in range(FF_STEPS):
        at = slice(FF_BLOCK * c, FF_BLOCK * (c + 1))
        pre = dot_nn(y, w.win[:, at]) + r.fbin[mine, at]
        h.pre[:, at] = pre
        part = dot_nn(gelu(pre).astype(BF), w.wout[at, :])
        total = part if total is None else total + part
    summed = total + r.fbout[mine, :] + y.astype(F32)
    h.fsum[...] = summed
    return (norm_parts(summed)[0] * r.fgain[mine, :] + r.fshift[mine, :]).astype(BF)


def ffn_backward_body(layer, grad, r, h, w):
    gsum, ggain, gshift = norm_back(h.fsum[...], r.fgain[layer : layer + 1, :], grad)
    low = gsum.astype(BF)
    gbias = jnp.sum(gsum, axis=0, keepdims=True)
    vectors = [ggain, gshift, gbias]
    total = gsum
    for c in range(FF_STEPS):
        at = slice(FF_BLOCK * c, FF_BLOCK * (c + 1))
        slope = gelu_both(h.pre[:, at])[1]
        gpre = (dot_nt(low, w.wout[at, :]) * slope).astype(BF)
        vectors.append(jnp.sum(gpre.astype(F32), axis=0, keepdims=True))
        total = total + dot_nt(gpre, w.win[:, at])
    vectors = jnp.concatenate(vectors + [jnp.zeros((1, D), F32)], axis=0)
    return total.astype(BF), low, vectors


def near_weights(layer, r):
    names = [n for n in WEIGHTS if n in r.__dict__]
    return Bag(names, [r.__dict__[n].at[layer] for n in names])


WEIGHTS = dict(
    wq=((D, D), BF), wkv=((D, 2 * D), BF), wr=((D, D), BF), wo=((D, D), BF), win=((D, FF), BF),
    wout=((FF, D), BF),
)
FORWARD_SCRATCH = dict(
    x=((ROWS, D), BF),
    joined=((KEYS, D), BF),
    att=((ROWS, D), BF),
    y=((ROWS, D), BF),
    pre=((ROWS, FF), F32),
    fsum=((ROWS, D), F32),
)


def forward_first_kernel(r, h, go):
    section = r.at[0]
    seq, half = section // 2, section % 2
    own = aligned(section * HALF, HALF)
    ready = [
        go(r.content.at[own], h.x.at[pl.ds(0, HALF)]),
        go(r.query.at[own], h.x.at[pl.ds(HALF, HALF)]),
        go(r.memory.at[0, aligned(seq * M, M)], h.joined.at[pl.ds(0, M)]),
        go(r.content.at[aligned(seq * S, S)], h.joined.at[pl.ds(M, S)]),
        go(r.table.at[aligned(HALF * (1 - half), HALF, WIDE)], h.table),
        go(r.wq.at[0], h.wq),
        go(r.wkv.at[0], h.wkv),
        go(r.wr.at[0], h.wr),
        go(r.wo.at[0], h.wo),
    ]
    weights = ((r.win.at[0], h.win), (r.wout.at[0], h.wout))
    later = attn_forward_body(0, r, h, h, h, go, ready, weights)
    for n in SAVED:
        go(h.__dict__[n], r.__dict__[n])
    r.acts[:ROWS, :] = h.att[...]
    x = ffn_forward_body(0, r, h, h, go, later)
    go(h.pre, r.pre0)
    go(h.fsum, r.fsum0)
    r.acts[ROWS:, :] = x
    r.half[...] = x[:HALF]


def forward_second_kernel(r, h, go):
    section = r.at[0]
    seq, half = section // 2, section % 2
    own = aligned(section * HALF, HALF)
    w = near_weights(1, r)
    ready = [
        go(r.memory.at[1, aligned(seq * M, M)], h.joined.at[pl.ds(0, M)]),
        go(r.cotc.at[own], h.grad.at[pl.ds(0, HALF)]),
        go(r.cotq.at[own], h.grad.at[pl.ds(HALF, HALF)]),
    ]
    h.x[...] = r.acts0[ROWS:, :]
    h.joined[aligned(M + HALF * half, HALF), :] = r.acts0[ROWS : ROWS + HALF, :]
    h.joined[aligned(M + HALF * (1 - half), HALF), :] = r.other[...]
    attn_forward_body(1, r, h, r, w, go, ready)
    r.acts[:ROWS, :] = h.att[...]
    r.out[...] = ffn_forward_body(1, r, h, w, go)
    gy, low, vectors = ffn_backward_body(1, h.grad[...].astype(F32), r, h, w)
    r.acts[ROWS:, :] = low
    r.gy[...] = gy
    r.fvec[...] = vectors


def ffn_backward_kernel(r, h, go):
    go(r.fsum0, h.fsum)
    go(r.pre0, h.pre)
    w = near_weights(0, r)
    gx = r.gx
    grad = jnp.concatenate([gx[:HALF, :] + r.other[...].astype(F32), gx[HALF:, :]], axis=0)
    go.finish()
    gy, low, vectors = ffn_backward_body(0, grad.astype(BF).astype(F32), r, h, w)
    r.low[...] = low
    r.gy[...] = gy
    r.fvec[...] = vectors


def attn_backward_kernel(layer, r, h, go):
    section = r.at[0]
    half = section % 2
    mine = slice(layer, layer + 1)
    w = near_weights(layer, r)
    if layer == 0:
        for n in SAVED:
            go(r.__dict__[n], h.__dict__[n])
        go.finish()
    k = h if layer == 0 else r
    gsum, ggain, gshift = norm_back(k.summed[...], r.again[mine, :], r.gy[...].astype(F32))
    low = gsum.astype(BF)
    h.vec[0:1, :] = ggain
    h.vec[1:2, :] = gshift
    h.vec[7:15, :] = r.fvec[...]
    h.vec[15:16, :] = jnp.zeros((1, D), F32)
    g_attended = dot_nt(low, w.wo[...]).astype(BF)
    differs = sight(r.at, r.lengths, r.ranks, r.segments)[1]
    lowest = low_lanes()
    ones = jnp.ones((WIDE, KEYS), BF)
    for p in range(PAIRS):
        at = slice(2 * HEAD * p, 2 * HEAD * (p + 1))
        later = slice(D + 2 * HEAD * p, D + 2 * HEAD * (p + 1))
        prob = k.prob[p]
        ga = two_heads(g_attended[:, at])
        gprob = dot_nt(ga, k.kv[:, later])
        h.gkv[later, :] = dot_nn(ga.T, prob.astype(BF)).astype(BF)
        centre = dot_nn(in_two(two_heads(g_attended[:, at].astype(F32) * k.mix[:, at])), ones)
        gscores = (prob * (gprob - centre)).astype(BF)
        gqc = one_pair(dot_nn(gscores, k.kv[:, at]))
        h.gkv[at, :] = dot_nn(two_heads(k.qc[:, at]).T, gscores).astype(BF)
        gwhole = gscores.astype(F32)
        gwide = unskewed_scores(gwhole).astype(BF)
        gqp = one_pair(dot_nn(gwide, k.rel[:, at]))
        h.grel[at, :] = dot_nn(two_heads(k.qp[:, at]).T, gwide)
        other_part = jnp.where(differs, gwhole, 0.0)
        other = jnp.sum(other_part, axis=-1, keepdims=True)
        same = jnp.sum(gwhole - other_part, axis=-1, keepdims=True)
        same_pair = jnp.where(lowest, same[:ROWS], same[ROWS:])
        other_pair = jnp.where(lowest, other[:ROWS], other[ROWS:])
        gqs = same_pair * r.seg[layer, 0:1, at] + other_pair * r.seg[layer, 1:2, at]
        segment = k.qs[:, at]
        h.vec[2:3, at] = jnp.sum(gqc, axis=0, keepdims=True) * SCALE
        h.vec[3:4, at] = jnp.sum(gqp, axis=0, keepdims=True) * SCALE
        h.vec[4:5, at] = jnp.sum(gqs, axis=0, keepdims=True) * SCALE
        h.vec[5:6, at] = jnp.sum(same_pair * segment, axis=0, keepdims=True)
        h.vec[6:7, at] = jnp.sum(other_pair * segment, axis=0, keepdims=True)
        h.turned[at, :ROWS] = low[:, at].astype(F32).T
        h.turned[at, ROWS:] = ((gqc + gqp + gqs) * SCALE).T
    few, step = KEYS - 128, D // 8
    for n, message in enumerate(r.first):
        d = section ^ n

        def chosen(ref, size, multiple):
            starts = [4 * size * e + size * d for e in range(8)]
            return jnp.concatenate([ref[aligned(m, multiple, size), :] for m in starts], axis=0)

        message[:SHARE, :256] = chosen(h.turned, step // 4, 8).astype(BF)
        message[:SHARE, 256:512] = chosen(h.grel, step // 4, 8).astype(BF)
        keyval = chosen(h.gkv, step // 2, 16)
        for j in range(2):
            rows = keyval[SHARE * j : SHARE * (j + 1)]
            message[:SHARE, 512 + 128 * j : 640 + 128 * j] = rows[:, :128]
            message[:SHARE, 768 + few * j : 768 + few * (j + 1)] = rows[:, 128:]
    joined = dot_nn(w.wkv[...], h.gkv[...])
    one, two = joined[:, M : M + HALF], joined[:, M + HALF :]
    first_half = jnp.zeros((1, 1), jnp.int32) + half == 0
    own, partner = jnp.where(first_half, one, two), jnp.where(first_half, two, one)
    gx = dot_nn(w.wq[...], h.turned[:, ROWS:].astype(BF)) + gsum.T
    gx = jnp.concatenate([gx[:, :HALF] + own, gx[:, HALF:]], axis=1)
    if layer > 0:
        r.send[...] = partner.T.astype(BF)
        r.gx[...] = gx.T
        r.second[:, : 2 * HALF] = r.out[...].T
        r.second[:, 2 * HALF :] = jnp.concatenate([partner, joined[:, :M]], axis=1).astype(BF)
        r.vec[...] = h.vec[...]
    else:
        h.second[:, : 2 * HALF] = gx.astype(BF)
        h.second[:, 2 * HALF : WIDE] = jnp.concatenate([partner, joined[:, :M]], axis=1).astype(BF)
        h.second[:, WIDE:] = r.later[...]
        for d in range(4):
            at = slice(SHARE * d, SHARE * (d + 1))
            for n, vec in enumerate((h.vec, r.vectors)):
                place = slice(SHARE * n, SHARE * (n + 1))
                wide = vec[10 + d : 11 + d, :]
                rows = [vec[:10, at]] + [wide[:, SHARE * j : SHARE * (j + 1)] for j in range(4)]
                rows = jnp.concatenate(rows + [jnp.zeros((2, SHARE), F32)], axis=0)
                h.parts[d, :, place] = rows.astype(BF)
        for n, message in enumerate(r.second):
            message[...] = h.second[aligned(SHARE * (section ^ n), SHARE), :]
        for n, message in enumerate(r.first):
            message[SHARE : SHARE + 16, : 2 * SHARE] = h.parts[section ^ n]
            message[SHARE + 16 :, :] = r.earlier[n][...]


def gathered_x(layer, r, h):
    for n in range(4):
        if layer == 0:
            rows = aligned((r.at[0] ^ n) * HALF, HALF)
            h.x[ROWS * n : ROWS * n + HALF, :] = r.content[rows, :]
            h.x[ROWS * n + HALF : ROWS * (n + 1), :] = r.query[rows, :]
        else:
            h.x[ROWS * n : ROWS * (n + 1), :] = r.before[n][ROWS:, :]


def put_halves(r, h):
    core = r.at[2]
    for j in range(4):
        r.kept[j] = h.pieces[2 * j + core]
        for part, given in enumerate(r.given):
            n = given.shape[1]
            given[j] = h.pieces[2 * j + 1 - core, n * part : n * (part + 1), :]


def shares_kernel(layer, r, h, go):
    wide, few = FF // 8, FF // 32
    for t in range(4):

        @pl.when(r.at[0] == t)
        def _():
            for d in range(8):
                at = slice(few * d, few * (d + 1))
                held = slice(wide * d + few * t, wide * d + few * (t + 1))
                r.bias[:, at] = r.fbin[layer : layer + 1, held]
                r.inner[:, at] = r.win[layer, :, held]
                r.outer[at, :] = r.wout[layer, held, :]


def ffn_weights_kernel(layer, fast, r, h, go):
    mine = slice(layer, layer + 1)
    gathered_x(layer, r, h)
    attended = jnp.concatenate([a[:ROWS, :] for a in r.acts], axis=0)
    summed = dot_nn(attended, r.wo[layer]) + h.x[...].astype(F32)
    y = norm_parts(summed)[0] * r.again[mine, :] + r.ashift[mine, :]
    h.y[...] = y.astype(BF)
    for n, low in enumerate(r.low):
        rows = low[low.shape[0] - ROWS :, :]
        h.low[ROWS * n : ROWS * (n + 1), :] = rows
        h.lowt[:, ROWS * n : ROWS * (n + 1)] = rows.T
    width, few = FF // 8, FF // 32
    for t in range(2):
        at = slice(width * t, width * (t + 1))
        pre = dot_nn(h.y[...], r.inner[:, at]) + r.bias[:, at]
        active, slope = gelu_both(pre)
        gpre = (dot_nt(h.low[...], r.outer[at, :]) * slope).astype(BF)
        grad_in = dot_nn(gpre.T, h.y[...]).astype(BF)
        grad_out = dot_nn(h.lowt[...], active.astype(BF)).astype(BF)
        if fast:
            for d in range(4):
                h.pieces[4 * t + d, :few, :] = grad_in[few * d : few * (d + 1), :]
            for d in range(8):
                h.pieces[d, few:, at] = grad_out[few * d : few * (d + 1), :]
        else:
            r.grads[0][at, :] = grad_in
            r.grads[1][:, at] = grad_out
    if fast:
        put_halves(r, h)


def attn_weights_kernel(fast, r, h, go):
    parts = []
    for layer in range(LAYERS):
        grads = attn_grads(layer, r, h)
        if fast:
            for n, grad in enumerate(grads):
                h.grads[layer, SHARE * n : SHARE * n + grad.shape[0], :] = grad
        else:
            for n, grad in enumerate(grads):
                r.grads[4 * layer + n][...] = grad.astype(BF)
    vectors = None
    for f in r.first:
        part = f[SHARE : SHARE + 16, : 2 * SHARE].astype(F32)
        vectors = part if vectors is None else vectors + part
    if not fast:
        r.vectors[...] = vectors
        return
    vectors = jnp.concatenate([vectors[:8], vectors[8:]], axis=1)
    step = D // 8
    for d in range(8):
        rows = []
        for layer in range(LAYERS):
            for n in range(4):
                size = step // 2 if n == 3 else step // 4
                start = SHARE * n + size * d
                rows.append(h.grads[layer, start : start + size, :])
        rows = jnp.concatenate(rows + [vectors, jnp.zeros_like(vectors)], axis=0)
        h.pieces[d] = rows.astype(BF)
    put_halves(r, h)


def attn_grads(layer, r, h):
    section = r.at[0]
    half = section % 2
    first = [f.at[pl.ds((SHARE + 16) * layer, SHARE)] for f in r.first]
    gathered_x(layer, r, h)
    for pair in range(2):
        rows = aligned((section ^ (2 * pair)) // 2 * M, M)
        h.joined[pair, :M, :] = r.memory[layer, rows, :]
        for n in (2 * pair, 2 * pair + 1):
            place = half ^ (n & 1)
            h.joined[pair, aligned(M + HALF * place, HALF), :] = h.x[ROWS * n : ROWS * n + HALF, :]
    low = jnp.concatenate([f[:, :128] for f in first], axis=1)
    proj = jnp.concatenate([f[:, 128:256] for f in first], axis=1)
    grad_q = dot_nn(proj, h.x[...])
    attended = jnp.concatenate([a[:ROWS, :] for a in (r.acts0, r.acts1)[layer]], axis=0)
    grad_o = dot_nn(low, attended)
    few = KEYS - 128
    grad_kv = grad_rel = None
    for pair in range(2):
        both = add(first[2 * pair][:, 512:], first[2 * pair + 1][:, 512:])
        both = jnp.concatenate(
            [
                jnp.concatenate([both[:, :128], both[:, 256 : 256 + few]], axis=1),
                jnp.concatenate([both[:, 128:256], both[:, 256 + few :]], axis=1),
            ],
            axis=0,
        )
        part = dot_nn(both, h.joined[pair])
        grad_kv = part if grad_kv is None else grad_kv + part
    for n in range(2):
        place = half ^ n
        total = add(first[n][:, 256:512], first[n + 2][:, 256:512])
        rows = r.table[aligned(HALF * (1 - place), HALF, WIDE), :]
        part = dot_nn(total, rows)
        grad_rel = part if grad_rel is None else grad_rel + part
    return grad_q, grad_o, grad_rel, grad_kv


def add(a, b):
    return (a.astype(F32) + b.astype(F32)).astype(BF)


def whole(shape):
    return pl.BlockSpec(shape, lambda i: (0,) * len(shape))


def gather_kernel(at_ref, *refs):
    section = at_ref[0]
    start = refs[0].shape[1] - 2 * WIDE
    early = [r.at[:, pl.ds(start, WIDE)] for r in refs[:4]]
    late = [r.at[:, pl.ds(start + WIDE, WIDE)] for r in refs[:4]]
    small_ref = refs[4]
    outc_ref, outq_ref, gradc_ref, gradq_ref, mem_ref = refs[5:10]
    bias_ref, seg_ref, again_ref, ashift_ref, inb_ref, outb_ref, fgain_ref, fshift_ref = refs[10:18]

    def in_order(blocks):
        odd = jnp.zeros((1, 1), jnp.int32) + section % 2 == 1
        high = jnp.zeros((1, 1), jnp.int32) + section // 2 == 1
        a, b, c, d = blocks
        a, b, c, d = (
            jnp.where(odd, b, a), jnp.where(odd, a, b), jnp.where(odd, d, c), jnp.where(odd, c, d)
        )
        left, right = jnp.concatenate([a, b], axis=1), jnp.concatenate([c, d], axis=1)
        return jnp.concatenate([jnp.where(high, right, left), jnp.where(high, left, right)], axis=1)

    def blocks(four, start):
        return [f[:, start : start + HALF].astype(F32) for f in four]

    outc_ref[...] = in_order(blocks(late, 0)).astype(BF)
    outq_ref[...] = in_order(blocks(late, HALF)).astype(BF)
    own, passed = blocks(early, 0), blocks(early, 2 * HALF)
    gradc_ref[...] = in_order([own[k] + passed[k ^ 1] for k in range(4)])
    gradq_ref[...] = in_order(blocks(early, HALF))
    high = jnp.zeros((1, 1), jnp.int32) + section // 2 == 1
    for layer, four in ((0, early), (1, late)):
        a, b, c, d = blocks(four, 3 * HALF)
        one, two = a + b, c + d
        mem_ref[layer] = jnp.concatenate(
            [jnp.where(high, two, one), jnp.where(high, one, two)], axis=1
        )
    for layer in range(LAYERS):
        mine = slice(layer, layer + 1)

        held = slice(SHARE * layer, SHARE * (layer + 1))

        def vector(row):
            return small_ref[row : row + 1, held].astype(F32)

        for j in range(3):
            bias_ref[j, mine, :] = vector(2 + j)
        for j in range(2):
            seg_ref[layer, j : j + 1, :] = vector(5 + j)
        again_ref[mine, :] = vector(0)
        ashift_ref[mine, :] = vector(1)
        fgain_ref[mine, :] = vector(7)
        fshift_ref[mine, :] = vector(8)
        outb_ref[mine, :] = vector(9)
        for j in range(4):
            inb_ref[mine, SHARE * j : SHARE * (j + 1)] = vector(10 + j)


def gather_rows(at, rows_out, small):
    rows = 4 * HALF
    vector = ((LAYERS, SHARE), F32)
    shapes = [
        ((SHARE, rows), BF),
        ((SHARE, rows), BF),
        ((SHARE, rows), F32),
        ((SHARE, rows), F32),
        ((LAYERS, SHARE, 2 * M), F32),
        ((3, LAYERS, SHARE), F32),
        ((LAYERS, 2, SHARE), F32),
        vector,
        vector,
        ((LAYERS, FF // 4), F32),
        vector,
        vector,
        vector,
    ]
    return pl.pallas_call(
        gather_kernel,
        grid=(1,),
        in_specs=[SCALARS.spec] + [whole(a.shape) for a in (*rows_out, small)],
        out_specs=[whole(s) for s, _ in shapes],
        out_shape=[jax.ShapeDtypeStruct(s, t) for s, t in shapes],
        compiler_params=params(),
        cost_estimate=cost(1_000_000, 2_000_000),
        name="gather_rows",
    )(at, *rows_out, small)


def final_ffn_kernel(r, h, go):
    few = FF // 32
    for n, message in enumerate(r.ffn):
        h.got[r.at[0] ^ n] = message[...].astype(F32)
    for layer in range(LAYERS):
        rows_at = slice(few * layer, few * (layer + 1))
        for s in range(4):
            held = slice(few * s, few * (s + 1))
            r.fin[layer, :, held] = h.got[s, rows_at, :SHARE].T
            for e in range(2):
                place = slice(FF // 8 * e + few * s, FF // 8 * e + few * (s + 1))
                start = SHARE + few * e
                r.fout[layer, :, place] = h.got[s, rows_at, start : start + few]


def final_attn_kernel(r, h, go):
    for n, message in enumerate(r.attn):
        h.attn[r.at[0] ^ n] = message[...].astype(F32)
    step = D // 8
    for layer in range(LAYERS):
        lanes = slice(SHARE * layer, SHARE * (layer + 1))
        start = 0
        for made, size in ((r.q, step // 4), (r.o, step // 4), (r.rel, step // 4), (r.kv, step // 2)):
            blocks = [h.attn[s, start : start + size, lanes] for s in range(4)]
            made[layer] = jnp.concatenate(blocks, axis=0).T
            start += size


def final_ffn(at, ffn):
    return run(
        final_ffn_kernel,
        "final_ffn",
        dict(at=(at, SCALARS), ffn=(ffn, NEAR)),
        dict(
            fin=((LAYERS, SHARE, FF // 8), F32, SMALL),
            fout=((LAYERS, D // 8, FF // 4), F32, SMALL),
        ),
        dict(got=((4, FF // 16, 2 * SHARE), F32)),
    )


def final_attn(at, attn):
    half = ((LAYERS, SHARE, SHARE // 2), F32, SMALL)
    return run(
        final_attn_kernel,
        "final_attn",
        dict(at=(at, SCALARS), attn=(attn, NEAR)),
        dict(q=half, kv=((LAYERS, SHARE, SHARE), F32, SMALL), o=half, rel=half),
        dict(attn=((4, ROWS_ATTN + 8, 2 * SHARE), F32)),
    )


def split_kernel(r, h, go):
    chip = r.at[1]
    for part, got in enumerate(r.got):
        n = got.shape[1]
        rows = pl.ds(n * part, n)
        for put, places in ((r.keep, (chip, chip ^ 2)), (r.send, (chip ^ 1, chip ^ 3))):
            for m, p in enumerate(places):
                put[m, rows, :] = add(r.kept[p, rows, :], got[p])


def fold_kernel(r, h, go):
    r.own[...], r.far[...] = [add(r.keep[n], r.got[n]) for n in range(2)]


def sum_kernel(r, h, go):
    r.total[...] = add(r.own[...], r.got[...])


def shared_attn_kernel(r, h, go):
    total = r.own[...].astype(F32) + r.got[...].astype(F32)
    layers = [total[ROWS_ATTN * n : ROWS_ATTN * (n + 1)] for n in range(LAYERS)]
    for t in range(4):
        at = slice(SHARE * t, SHARE * (t + 1))
        rows = jnp.concatenate([m[:, at] for m in layers], axis=1)
        h.parts[t] = jnp.concatenate([rows, jnp.zeros((8, 2 * SHARE), F32)], axis=0).astype(BF)
    for n, part in enumerate(r.parts):
        part[...] = h.parts[r.at[0] ^ n]
    vectors = total[LAYERS * ROWS_ATTN : LAYERS * ROWS_ATTN + 8]
    r.vectors[...] = jnp.concatenate([vectors[:, : 2 * SHARE], vectors[:, 2 * SHARE :]], axis=0)


def shared_kernel(r, h, go):
    few = FF // 32
    for layer, total in enumerate((add(r.own[...], r.got[...]), r.later[...])):
        rows = slice(few * layer, few * (layer + 1))
        for t in range(4):
            at = slice(SHARE * t, SHARE * (t + 1))
            h.parts[t, rows, :SHARE], h.parts[t, rows, SHARE:] = total[:few, at], total[few:, at]
    for n, part in enumerate(r.parts):
        part[...] = h.parts[r.at[0] ^ n]


def split_pieces(at, made, after=()):
    got = [swapped(a, DP, 1) for a in made.given]
    shape = (2,) + made.kept.shape[1:]
    ins = dict(at=(at, SCALARS), kept=(made.kept, NEAR), got=(got, NEAR))
    return run(
        split_kernel, "split_pieces", ins, dict(keep=(shape, BF, NEAR), send=(shape, BF, NEAR)), {},
        after=after,
    )


def fold_pieces(split, got, after=()):
    shape = got.shape[1:]
    ins = dict(keep=(split.keep, NEAR), got=(got, NEAR))
    return run(
        fold_kernel, "fold_pieces", ins, dict(own=(shape, BF, NEAR), far=(shape, BF, NEAR)), {},
        after=after,
    )


def sum_pieces(folded, got, after=()):
    ins = dict(own=(folded.own, NEAR), got=(got, NEAR))
    return run(
        sum_kernel, "sum_pieces", ins, dict(total=(got.shape, BF, NEAR)), {}, after=after
    ).total


def shared_attn(at, folded, got, after=()):
    ins = dict(at=(at, SCALARS), own=(folded.own, NEAR), got=(got, NEAR))
    shape = (ROWS_ATTN + 8, 2 * SHARE)
    return run(
        shared_attn_kernel, "shared_attn", ins,
        dict(parts=([shape] * 4, BF, NEAR), vectors=((16, 2 * SHARE), F32, NEAR)),
        dict(parts=((4,) + shape, BF)), after=after,
    )


def shared_pieces(at, folded, got, later, after=()):
    ins = dict(
        at=(at, SCALARS), own=(folded.own, NEAR), got=(got, NEAR), later=(later, NEAR)
    )
    shape = (FF // 16, 2 * SHARE)
    return run(
        shared_kernel, "shared_pieces", ins,
        dict(parts=([shape] * 4, BF, NEAR)),
        dict(parts=((4,) + shape, BF)), after=after,
    ).parts


def swapped(x, axis, k):
    return lax.ppermute(x, axis, [(i, i ^ k) for i in range(lax.axis_size(axis))])


def from_all(x):
    return [x] + [swapped(x, SECTION, k) for k in (1, 2, 3)]


def messages(parts):
    return [parts[0]] + [swapped(parts[k], SECTION, k) for k in (1, 2, 3)]


def on_device(
    content_in,
    query_in,
    memory,
    doc_lengths,
    perm_rank,
    segment_ids,
    w_query,
    w_keyval,
    w_out,
    w_rel,
    head_bias,
    seg_embed,
    attn_gain,
    attn_shift,
    ffn_in,
    ffn_in_bias,
    ffn_out,
    ffn_out_bias,
    ffn_gain,
    ffn_shift,
    cot_content,
    cot_query,
):
    ORDER.clear()
    dp = lax.axis_size(DP)
    fast = dp == 8
    index = lax.axis_index(DP)
    at = jnp.stack([lax.axis_index(SECTION), index // 2, index % 2]).astype(jnp.int32)
    table = position_table()
    marks = dict(
        at=(at, SCALARS),
        lengths=(doc_lengths, SCALARS),
        ranks=(perm_rank, SMALL),
        segments=(segment_ids, SMALL),
    )
    attn_v = dict(
        bias=(head_bias.transpose(1, 0, 2), SMALL),
        seg=(seg_embed, SMALL),
        again=(attn_gain, SMALL),
        ashift=(attn_shift, SMALL),
    )
    ffn_v = dict(
        fbin=(ffn_in_bias, SMALL),
        fbout=(ffn_out_bias, SMALL),
        fgain=(ffn_gain, SMALL),
        fshift=(ffn_shift, SMALL),
    )
    matrices = dict(
        wq=w_query, wkv=w_keyval, wr=w_rel, wo=w_out, win=ffn_in, wout=ffn_out,
    )
    near = {n: (a, NEAR) for n, a in matrices.items()}

    def of(which, *names):
        return {n: which[n] for n in which if n in names}

    first = run(
        forward_first_kernel,
        "forward_first",
        dict(
            **marks,
            content=(content_in, FAR),
            query=(query_in, FAR),
            memory=(memory, FAR),
            table=(table, FAR),
            **{n: (a, FAR) for n, a in matrices.items()},
            **attn_v,
            **ffn_v,
        ),
        dict(
            acts=((2 * ROWS, D), BF, NEAR),
            half=((HALF, D), BF, NEAR),
            pre0=((ROWS, FF), F32, FAR),
            fsum0=((ROWS, D), F32, FAR),
            **{n: (*s, FAR) for n, s in SAVED.items()},
        ),
        dict(**FORWARD_SCRATCH, table=((WIDE, D), BF), **WEIGHTS, **SAVED),
        copies=24,
        flops=2_400_000_000,
        moved=16_000_000,
    )
    other = swapped(first.half, SECTION, 1)
    acts0 = from_all(first.acts)
    second = run(
        forward_second_kernel,
        "forward_second",
        dict(
            **marks,
            acts0=(first.acts, NEAR),
            other=(other, NEAR),
            memory=(memory, FAR),
            table=(table, NEAR),
            cotc=(cot_content, FAR),
            cotq=(cot_query, FAR),
            **near,
            **attn_v,
            **ffn_v,
        ),
        dict(
            acts=((2 * ROWS, D), BF, NEAR),
            out=((ROWS, D), BF, NEAR),
            gy=((ROWS, D), BF, NEAR),
            fvec=((8, D), F32, NEAR),
            **{n: (*s, NEAR) for n, s in SAVED.items()},
        ),
        dict(**FORWARD_SCRATCH, grad=((ROWS, D), BF)),
        copies=4,
        flops=3_600_000_000,
        moved=16_000_000,
    )
    acts1 = from_all(second.acts)

    def attn_backward(layer, saved, gy, fvec, after=(), **extra):
        ins = dict(
            **marks,
            gy=(gy, NEAR),
            fvec=(fvec, NEAR),
            **{n: (saved.__dict__[n], FAR if layer == 0 else NEAR) for n in SAVED},
            **{n: near[n] for n in list(WEIGHTS)[:4] if n != list(WEIGHTS)[2]},
            **attn_v,
            **{n: (a, NEAR) for n, a in extra.items()},
        )
        scratch = dict(
            vec=((16, D), F32),
            turned=((D, 2 * ROWS), F32),
            gkv=((2 * D, KEYS), BF),
            grel=((D, WIDE), F32),
        )
        rows = FIRST[0] if layer else 2 * FIRST[0] + 16
        outs = dict(first=([(rows, FIRST[1])] * 4, BF, NEAR))
        if layer == 0:
            outs.update(second=([SECOND] * 4, BF, NEAR))
            scratch.update(SAVED, second=((D, 2 * WIDE), BF), parts=((4, 16, 2 * SHARE), BF))
        else:
            outs.update(
                second=((D, WIDE), BF, NEAR),
                gx=((ROWS, D), F32, NEAR),
                send=((HALF, D), BF, NEAR),
                vec=((16, D), F32, NEAR),
            )
        return run(
            functools.partial(attn_backward_kernel, layer), "attn_backward", ins, outs, scratch,
            copies=10, flops=1000, moved=1000, after=after,
        )

    def inputs_of(layer):
        if layer == 0:
            return dict(content=(content_in, NEAR), query=(query_in, NEAR))
        return dict(before=(acts0, NEAR))

    def grads_of(shape, plain, cuts=2):
        if fast:
            parts = [(4, shape[0] // cuts, shape[1])] * cuts
            return dict(kept=((4,) + shape, BF, NEAR), given=(parts, BF, NEAR))
        return dict(grads=(plain, BF, SMALL))

    def shares_of(layer):
        return run(
            functools.partial(shares_kernel, layer),
            "shares",
            dict(at=marks["at"], **of(near, "win", "wout"), **of(ffn_v, "fbin")),
            dict(
                inner=((D, D), BF, NEAR),
                outer=((D, D), BF, NEAR),
                bias=((1, D), F32, NEAR),
            ),
            {},
        )

    def ffn_weights(layer, acts, lows, after=()):
        shares = shares_of(layer)
        ins = dict(
            at=marks["at"],
            **inputs_of(layer),
            **of(near, "wo"),
            **of(attn_v, "again", "ashift"),
            inner=(shares.inner, NEAR),
            outer=(shares.outer, NEAR),
            bias=(shares.bias, NEAR),
            acts=(acts, NEAR),
            low=(lows, NEAR),
        )
        shape = (ROWS_FFN, D)
        tall = ((4 * ROWS, D), BF)
        return run(
            functools.partial(ffn_weights_kernel, layer, fast),
            "ffn_weights",
            ins,
            grads_of(shape, [(D, D), (D, D)]),
            dict(x=tall, y=tall, low=tall, lowt=((D, 4 * ROWS), BF), pieces=((8,) + shape, BF)),
            flops=1000,
            moved=1000,
            after=after,
        )

    def attn_weights(notes, after=()):
        ins = dict(
            at=marks["at"],
            content=(content_in, NEAR),
            query=(query_in, NEAR),
            before=(acts0, NEAR),
            memory=(memory, NEAR),
            table=(table, NEAR),
            acts0=(acts0, NEAR),
            acts1=(acts1, NEAR),
            first=(notes, NEAR),
        )
        shape = (2 * ROWS_ATTN + 2 * ROWS_VEC, D)
        outs = grads_of(shape, [(SHARE, D), (SHARE, D), (SHARE, D), (2 * SHARE, D)] * 2, 4)
        if not fast:
            outs.update(vectors=((2 * ROWS_VEC, 2 * SHARE), F32, SMALL))
        return run(
            functools.partial(attn_weights_kernel, fast),
            "attn_weights",
            ins,
            outs,
            dict(
                x=((4 * ROWS, D), BF),
                joined=((2, KEYS, D), BF),
                grads=((LAYERS, 5 * SHARE, D), F32),
                pieces=((8,) + shape, BF),
            ),
            flops=10**12,
            moved=10**9,
            after=after,
        )

    back1 = attn_backward(1, second, second.gy, second.fvec, acts0[1:], out=second.out)
    received = swapped(back1.send, SECTION, 1)
    fgrads1 = ffn_weights(1, acts1, acts1)
    third = run(
        ffn_backward_kernel,
        "ffn_backward",
        dict(
            gx=(back1.gx, NEAR),
            other=(received, NEAR),
            fsum0=(first.fsum0, FAR),
            pre0=(first.pre0, FAR),
            **of(near, "win", "wout"),
            **of(ffn_v, "fgain"),
        ),
        dict(
            low=((ROWS, D), BF, NEAR), gy=((ROWS, D), BF, NEAR), fvec=((8, D), F32, NEAR)
        ),
        dict(fsum=((ROWS, D), F32), pre=((ROWS, FF), F32)),
        copies=4,
        flops=10**12,
        moved=10**9,
    )
    lows0 = from_all(third.low)
    if fast:
        split_f1 = split_pieces(at, fgrads1)
        z_f1 = swapped(split_f1.send, DP, 2)
    back0 = attn_backward(
        0, first, third.gy, third.fvec, later=back1.second, vectors=back1.vec, earlier=back1.first
    )
    parts0 = messages(back0.first)
    rows_out = back0.second
    fgrads0 = ffn_weights(0, acts0, lows0)
    if fast:
        fold_f1 = fold_pieces(split_f1, z_f1)
        z_f1 = swapped(fold_f1.far, DP, 4)
        split_f0 = split_pieces(at, fgrads0)
        z_f0 = swapped(split_f0.send, DP, 2)
    agrads = attn_weights(parts0)
    if fast:
        sum_f1 = sum_pieces(fold_f1, z_f1)
        fold_f0 = fold_pieces(split_f0, z_f0)
        z_f0 = swapped(fold_f0.far, DP, 4)
        split_a = split_pieces(at, agrads)
        z_a = swapped(split_a.send, DP, 2)
        rows_all = messages(rows_out)
        ffn = messages(shared_pieces(at, fold_f0, z_f0, sum_f1, rows_all[1:]))
        fold_a = fold_pieces(split_a, z_a)
        z_a = swapped(fold_a.far, DP, 4)
        made = final_ffn(at, ffn)
        fin, fout = made.fin, made.fout
        shared_a = shared_attn(at, fold_a, z_a)
        attn_all = messages(shared_a.parts)
        outs = gather_rows(at, rows_all, shared_a.vectors)
        made = final_attn(at, attn_all)
        wq, wkv, wo, wr = made.q, made.kv, made.o, made.rel
        fout = fout.transpose(0, 2, 1)
    else:
        outs = gather_rows(at, messages(rows_out), lax.psum(agrads.vectors, DP))
        section = at[0]

        def owned(rows):
            part = rows.reshape((dp, -1) + rows.shape[1:])
            part = lax.psum_scatter(part, DP, scatter_dimension=0, tiled=False)
            part = lax.psum(part, SECTION)
            width = part.shape[1] // 4
            return lax.dynamic_slice_in_dim(part, section * width, width, 1).astype(F32).T

        def at_share(share, count, axis=0):
            cut = share.reshape(share.shape[:axis] + (count, 1, -1) + share.shape[axis + 1 :])
            full = jnp.zeros(cut.shape[: axis + 1] + (4,) + cut.shape[axis + 2 :], BF)
            full = lax.dynamic_update_slice_in_dim(full, cut, section, axis + 1)
            return full.reshape(share.shape[:axis] + (-1,) + share.shape[axis + 1 :])

        def plain(fgrads, agrads):
            parts = [at_share(a, 8) for a in agrads]
            parts += [at_share(fgrads[0], 8), at_share(fgrads[1], 8, 1)]
            q, o, rel, kv, fin, fout = [owned(a) for a in parts]
            return q, kv, o, rel, fin, fout

        pairs = zip(plain(fgrads0.grads, agrads.grads[:4]), plain(fgrads1.grads, agrads.grads[4:]))
        wq, wkv, wo, wr, fin, fout = [jnp.stack(p) for p in pairs]
    return (
        outs[0].T,
        outs[1].T,
        outs[2].T,
        outs[3].T,
        outs[4].transpose(0, 2, 1),
        wq,
        wkv,
        wo,
        wr,
        outs[5].transpose(1, 0, 2),
        outs[6],
        outs[7],
        outs[8],
        fin,
        outs[9],
        fout,
        outs[10],
        outs[11],
        outs[12],
    )


def solution(mesh):
    in_specs = (
        P(DP, None),
        P(DP, None),
        P(None, DP, None),
        P(DP),
        P(DP, None),
        P(DP, None),
    ) + (P(),) * 14 + (P(DP, None), P(DP, None))
    weight, vector = P(None, SECTION, DP), P(None, SECTION)
    out_specs = (
        P(DP, SECTION),
        P(DP, SECTION),
        P(DP, SECTION),
        P(DP, SECTION),
        P(None, DP, SECTION),
        weight,
        weight,
        weight,
        weight,
        P(None, None, SECTION),
        P(None, None, SECTION),
        vector,
        vector,
        weight,
        vector,
        weight,
        vector,
        vector,
        vector,
    )
    return jax.shard_map(
        on_device, mesh=mesh, in_specs=in_specs, out_specs=out_specs, check_vma=False
    )
```

```python
import functools
import math

import jax
import jax.numpy as jnp
import numpy as np
from jax import lax
from jax.experimental import pallas as pl
from jax.experimental.pallas import tpu as pltpu
from jax.sharding import PartitionSpec as P

D = 768
HEADS = 12
HEAD = 64
FF = 3072
S = 128
M = 64
LAYERS = 2
HALF = S // 2
KEYS = M + S
TABLE = M + 2 * S - 1
WIDE = 256
ROWS = 2 * HALF
PAIRS = HEADS // 2
SHARE = D // 4
SCALE = HEAD**-0.5
NEGATIVE = -1e30
EPSILON = 1e-05
SECTION, DP = "section", "dp"
BF = jnp.bfloat16
F32 = jnp.float32
GELU_C = math.sqrt(2.0 / math.pi)
MEG = 1 << 20

FIRST = (SHARE, 7 * 128)
SECOND = (SHARE, 2 * WIDE)
ROWS_ATTN = 120
ROWS_VEC = 8
ROWS_FFN = FF // 16


def position_table():
    distance = (M + S - 1 - np.arange(TABLE)).astype(np.float32)
    inverse = np.exp(np.arange(0, D, 2).astype(np.float32) * np.float32(-math.log(10000.0) / D))
    angles = distance[:, None] * inverse[None, :].astype(np.float32)
    table = np.concatenate([np.sin(angles), np.cos(angles)], axis=1)
    table = np.concatenate([table, np.zeros((1, D), np.float32)], axis=0)
    return jnp.asarray(table, jnp.float32).astype(BF)


def dot_nn(a, b):
    return lax.dot_general(a, b, (((1,), (0,)), ((), ())), preferred_element_type=F32)


def dot_nt(a, b):
    return lax.dot_general(a, b, (((1,), (1,)), ((), ())), preferred_element_type=F32)


def norm_parts(values):
    centre = values - jnp.mean(values, axis=-1, keepdims=True)
    spread = jnp.mean(centre * centre, axis=-1, keepdims=True)
    root = lax.rsqrt(spread + EPSILON)
    return centre * root, root


def norm_back(values, gain, grad):
    normal, root = norm_parts(values)
    scaled = grad * gain
    grad_gain = jnp.sum(grad * normal, axis=0, keepdims=True)
    grad_shift = jnp.sum(grad, axis=0, keepdims=True)
    first = jnp.mean(scaled, axis=-1, keepdims=True)
    second = jnp.mean(scaled * normal, axis=-1, keepdims=True)
    return root * (scaled - first - normal * second), grad_gain, grad_shift


def gelu(v):
    return 0.5 * v * (1.0 + jnp.tanh(GELU_C * (v + 0.044715 * (v * v * v))))


def gelu_both(v):
    square = v * v
    bend = jnp.tanh(GELU_C * (v + 0.044715 * (square * v)))
    half = 0.5 * (1.0 + bend)
    slope = half + 0.5 * v * (1.0 - bend * bend) * (GELU_C * (1.0 + 3 * 0.044715 * square))
    return v * half, slope


def low_lanes():
    return lax.broadcasted_iota(jnp.int32, (1, 2 * HEAD), 1) < HEAD


def two_heads(pair):
    low = low_lanes()
    zero = jnp.zeros_like(pair)
    return jnp.concatenate([jnp.where(low, pair, zero), jnp.where(low, zero, pair)], axis=0)


def one_pair(stacked):
    half = stacked.shape[0] // 2
    return jnp.where(low_lanes(), stacked[:half], stacked[half:])


def in_two(values):
    high = values.astype(BF)
    return jnp.concatenate([high, (values - high.astype(F32)).astype(BF)], axis=1)


def skewed_scores(wide):
    parts = [
        pltpu.roll(wide[HALF * b : HALF * (b + 1)], WIDE - HALF + 1, 1, stride=1, stride_axis=0)
        for b in range(4)
    ]
    return jnp.concatenate(parts, axis=0)[:, :KEYS]


def unskewed_scores(scores):
    rows, wide = 4 * HALF, WIDE // 2
    shift = HALF - 1 - lax.broadcasted_iota(jnp.int32, (rows, wide), 0) % HALF
    lane = lax.broadcasted_iota(jnp.int32, (rows, wide), 1)
    source = (lane - shift) & (wide - 1)
    wrapped = lane < shift
    rest = jnp.concatenate([scores[:, wide:], jnp.zeros((rows, WIDE - KEYS), F32)], axis=1)
    first, second = (
        jnp.take_along_axis(a, source, axis=1, mode=lax.GatherScatterMode.PROMISE_IN_BOUNDS)
        for a in (scores[:, :wide], rest)
    )
    return jnp.concatenate(
        [jnp.where(wrapped, 0.0, first), jnp.where(wrapped, first, second)], axis=1
    )


def sight(at_ref, lengths_ref, ranks_ref, segments_ref):
    seq, half = at_ref[0] // 2, at_ref[0] % 2
    ranks = ranks_ref[pl.ds(seq, 1), :]
    segments = segments_ref[pl.ds(seq, 1), :]
    place = lax.broadcasted_iota(jnp.int32, (1, S), 1)
    live = jnp.where(place < lengths_ref[seq], ranks, 2 * S)
    key_rank = jnp.concatenate([jnp.full((1, M), -1, jnp.int32), live], axis=1)
    key_segment = jnp.concatenate([jnp.zeros((1, M), jnp.int32), segments], axis=1)
    row = lax.broadcasted_iota(jnp.int32, (HALF, S), 0) + half * HALF
    column = lax.broadcasted_iota(jnp.int32, (HALF, S), 1)

    def upright(values):
        wide = jnp.where(row == column, values.astype(F32), 0.0)
        return jnp.sum(wide, axis=-1, keepdims=True).astype(jnp.int32)

    own_rank, own_segment = upright(ranks), upright(segments)
    reach = jnp.concatenate([own_rank, own_rank - 1], axis=0)
    hidden = jnp.where(key_rank <= reach, 0.0, 1.0)
    differs = jnp.where(jnp.concatenate([own_segment] * 2, axis=0) != key_segment, 1.0, 0.0)
    return [jnp.concatenate([a] * 2, axis=0) > 0.0 for a in (hidden, differs)]


class Mover:
    def __init__(self, semaphores):
        self.semaphores, self.count, self.open = semaphores, 0, []

    def __call__(self, source, target):
        copy = pltpu.make_async_copy(source, target, self.semaphores.at[self.count])
        self.count += 1
        copy.start()
        self.open.append(copy)
        return copy

    def wait(self, *copies):
        for copy in copies:
            if any(copy is other for other in self.open):
                self.open = [other for other in self.open if other is not copy]
                copy.wait()

    def finish(self):
        self.wait(*list(self.open))


class Bag:
    def __init__(self, names, values):
        self.__dict__.update(zip(names, values))


class Place:
    def __init__(self, seen, space):
        self.spec, self.space = pl.BlockSpec(memory_space=seen), space

    def operand(self, array):
        if self.space is None:
            return array
        return pltpu.with_memory_space_constraint(array, self.space)

    def result(self, shape, kind):
        return jax.ShapeDtypeStruct(shape, kind) if self.space is None else self.space(shape, kind)


SCALARS = Place(pltpu.SMEM, pltpu.HBM)
SMALL = Place(pltpu.VMEM, pltpu.HBM)
FAR = Place(pl.ANY, pltpu.HBM)
NEAR = Place(pltpu.VMEM, pltpu.VMEM)
TOKEN = pl.BlockSpec(memory_space=pl.ANY)
SPARE = 3 * MEG


def padded_bytes(shape, kind):
    *front, rows, columns = shape
    return math.prod(front) * -(-rows // 16) * 16 * -(-columns // 128) * 128 * jnp.dtype(kind).itemsize


def params(limit=8 * MEG):
    return pltpu.CompilerParams(vmem_limit_bytes=limit)


def cost(flops, moved):
    return pl.CostEstimate(flops=flops, bytes_accessed=moved, transcendentals=0)


ORDER = []


def run(kernel, name, ins, outs, scratch, copies=1, flops=1000, moved=1000, after=()):
    after = ORDER[-1:] + list(after)
    arrays, counts, specs, held_bytes = [], [], [], 0
    for value, place in ins.values():
        many = isinstance(value, (list, tuple))
        counts.append(len(value) if many else 0)
        for a in value if many else [value]:
            arrays.append(place.operand(a))
            specs.append(place.spec)
            held_bytes += padded_bytes(a.shape, a.dtype) if place is SMALL else 0
    shapes, out_specs = [], []
    for shape, kind, place in outs.values():
        many = isinstance(shape, list)
        counts.append(len(shape) if many else 0)
        for one in shape if many else [shape]:
            shapes.append(place.result(one, kind))
            out_specs.append(place.spec)
            held_bytes += 2 * padded_bytes(one, kind) if place is SMALL else 0
    held_bytes += sum(padded_bytes(*s) for s in scratch.values())

    def grouped(refs, counts):
        refs = list(refs)
        taken = []
        for count in counts:
            taken.append([refs.pop(0) for _ in range(count)] if count else refs.pop(0))
        return taken

    def body(*refs):
        refs = refs[: len(arrays)] + refs[len(arrays) + len(after) :]
        split = len(arrays) + len(shapes)
        go = Mover(refs[-1])
        kernel(
            Bag([*ins, *outs], grouped(refs[:split], counts)), Bag(scratch, refs[split:-1]), go
        )
        go.finish()

    results = pl.pallas_call(
        body,
        in_specs=specs + [TOKEN] * len(after),
        out_specs=out_specs,
        out_shape=shapes,
        scratch_shapes=[pltpu.VMEM(*s) for s in scratch.values()]
        + [pltpu.SemaphoreType.DMA((copies,))],
        compiler_params=params(held_bytes + SPARE),
        cost_estimate=cost(flops, moved),
        name=name,
    )(*arrays, *after)
    ORDER.append(results[0])
    return Bag(outs, grouped(results, counts[len(ins) :]))


def aligned(start, multiple, size=None):
    return pl.ds(pl.multiple_of(start, multiple), size or multiple)


SAVED = dict(
    summed=((ROWS, D), F32),
    qc=((ROWS, D), BF),
    qp=((ROWS, D), BF),
    qs=((ROWS, D), F32),
    kv=((KEYS, 2 * D), BF),
    rel=((WIDE, D), BF),
    mix=((ROWS, D), F32),
    prob=((PAIRS, 2 * ROWS, KEYS), F32),
)
FF_STEPS = 4
FF_BLOCK = FF // FF_STEPS


def attn_forward_body(layer, r, h, saved, w, go, ready):
    mine = slice(layer, layer + 1)
    go.wait(*ready)
    projected = dot_nn(h.x[...], w.wq[...])
    saved.qc[...] = ((projected + r.bias[0, mine, :]) * SCALE).astype(BF)
    saved.qp[...] = ((projected + r.bias[1, mine, :]) * SCALE).astype(BF)
    saved.qs[...] = (projected + r.bias[2, mine, :]) * SCALE
    saved.kv[...] = dot_nn(h.joined[...], w.wkv[...]).astype(BF)
    half = r.at[0] % 2
    rows = h.table[...] if layer == 0 else r.table[aligned(HALF * (1 - half), HALF, WIDE), :]
    saved.rel[...] = dot_nn(rows, w.wr[...]).astype(BF)
    hidden, differs = sight(r.at, r.lengths, r.ranks, r.segments)
    ones = jnp.ones((WIDE, KEYS), BF)
    beside = jnp.ones((KEYS, 2 * HEAD), BF)
    for p in range(PAIRS):
        at = slice(2 * HEAD * p, 2 * HEAD * (p + 1))
        later = slice(D + 2 * HEAD * p, D + 2 * HEAD * (p + 1))
        content = dot_nt(two_heads(saved.qc[:, at]), saved.kv[:, at])
        wide = dot_nt(two_heads(saved.qp[:, at]), saved.rel[:, at])
        segment = saved.qs[:, at]
        same = dot_nn(in_two(two_heads(segment * r.seg[layer, 0:1, at])), ones)
        other = dot_nn(in_two(two_heads(segment * r.seg[layer, 1:2, at])), ones)
        raw = content + skewed_scores(wide) + jnp.where(differs, other, same)
        scores = jnp.where(hidden, NEGATIVE, raw)
        exponent = jnp.exp(scores - jnp.max(scores, axis=-1, keepdims=True))
        values = jnp.concatenate([saved.kv[:, later], beside], axis=1)
        mixed = dot_nn(exponent.astype(BF), values)
        share = 1.0 / mixed[:, 2 * HEAD :]
        saved.prob[p] = exponent * jnp.concatenate([share, share[:, : KEYS - 2 * HEAD]], axis=1)
        attended = one_pair(mixed[:, : 2 * HEAD] * share)
        saved.mix[:, at] = attended
        h.att[:, at] = attended.astype(BF)
    summed = dot_nn(h.att[...], w.wo[...]) + h.x[...].astype(F32)
    saved.summed[...] = summed
    h.y[...] = (norm_parts(summed)[0] * r.again[mine, :] + r.ashift[mine, :]).astype(BF)


def ffn_forward_body(layer, r, h, w, go, ready=()):
    mine = slice(layer, layer + 1)
    y = h.y[...]
    go.wait(*ready)
    total = None
    for c in range(FF_STEPS):
        at = slice(FF_BLOCK * c, FF_BLOCK * (c + 1))
        pre = dot_nn(y, w.win[:, at]) + r.fbin[mine, at]
        h.pre[:, at] = pre
        part = dot_nn(gelu(pre).astype(BF), w.wout[at, :])
        total = part if total is None else total + part
    summed = total + r.fbout[mine, :] + y.astype(F32)
    h.fsum[...] = summed
    return (norm_parts(summed)[0] * r.fgain[mine, :] + r.fshift[mine, :]).astype(BF)


def ffn_backward_body(layer, grad, r, h, w):
    gsum, ggain, gshift = norm_back(h.fsum[...], r.fgain[layer : layer + 1, :], grad)
    low = gsum.astype(BF)
    gbias = jnp.sum(gsum, axis=0, keepdims=True)
    vectors = [ggain, gshift, gbias]
    total = gsum
    for c in range(FF_STEPS):
        at = slice(FF_BLOCK * c, FF_BLOCK * (c + 1))
        slope = gelu_both(h.pre[:, at])[1]
        gpre = (dot_nt(low, w.wout[at, :]) * slope).astype(BF)
        vectors.append(jnp.sum(gpre.astype(F32), axis=0, keepdims=True))
        total = total + dot_nt(gpre, w.win[:, at])
    vectors = jnp.concatenate(vectors + [jnp.zeros((1, D), F32)], axis=0)
    return total.astype(BF), low, vectors


def near_weights(layer, r):
    names = [n for n in WEIGHTS if n in r.__dict__]
    return Bag(names, [r.__dict__[n].at[layer] for n in names])


WEIGHTS = dict(
    wq=((D, D), BF), wkv=((D, 2 * D), BF), wr=((D, D), BF), wo=((D, D), BF), win=((D, FF), BF),
    wout=((FF, D), BF),
)
FORWARD_SCRATCH = dict(
    x=((ROWS, D), BF),
    joined=((KEYS, D), BF),
    att=((ROWS, D), BF),
    y=((ROWS, D), BF),
    pre=((ROWS, FF), F32),
    fsum=((ROWS, D), F32),
)


def forward_first_kernel(r, h, go):
    section = r.at[0]
    seq, half = section // 2, section % 2
    own = aligned(section * HALF, HALF)
    ready = [
        go(r.content.at[own], h.x.at[pl.ds(0, HALF)]),
        go(r.query.at[own], h.x.at[pl.ds(HALF, HALF)]),
        go(r.memory.at[0, aligned(seq * M, M)], h.joined.at[pl.ds(0, M)]),
        go(r.content.at[aligned(seq * S, S)], h.joined.at[pl.ds(M, S)]),
        go(r.table.at[aligned(HALF * (1 - half), HALF, WIDE)], h.table),
        go(r.wq.at[0], h.wq),
        go(r.wkv.at[0], h.wkv),
        go(r.wr.at[0], h.wr),
        go(r.wo.at[0], h.wo),
    ]
    later = [go(r.win.at[0], h.win), go(r.wout.at[0], h.wout)]
    attn_forward_body(0, r, h, h, h, go, ready)
    for n in SAVED:
        go(h.__dict__[n], r.__dict__[n])
    r.acts[:ROWS, :] = h.att[...]
    x = ffn_forward_body(0, r, h, h, go, later)
    go(h.pre, r.pre0)
    go(h.fsum, r.fsum0)
    r.acts[ROWS:, :] = x
    r.half[...] = x[:HALF]


def forward_second_kernel(r, h, go):
    section = r.at[0]
    seq, half = section // 2, section % 2
    own = aligned(section * HALF, HALF)
    w = near_weights(1, r)
    ready = [
        go(r.memory.at[1, aligned(seq * M, M)], h.joined.at[pl.ds(0, M)]),
        go(r.cotc.at[own], h.grad.at[pl.ds(0, HALF)]),
        go(r.cotq.at[own], h.grad.at[pl.ds(HALF, HALF)]),
    ]
    h.x[...] = r.acts0[ROWS:, :]
    h.joined[aligned(M + HALF * half, HALF), :] = r.acts0[ROWS : ROWS + HALF, :]
    h.joined[aligned(M + HALF * (1 - half), HALF), :] = r.other[...]
    attn_forward_body(1, r, h, r, w, go, ready)
    r.acts[:ROWS, :] = h.att[...]
    r.out[...] = ffn_forward_body(1, r, h, w, go)
    gy, low, vectors = ffn_backward_body(1, h.grad[...].astype(F32), r, h, w)
    r.acts[ROWS:, :] = low
    r.gy[...] = gy
    r.fvec[...] = vectors


def ffn_backward_kernel(r, h, go):
    go(r.fsum0, h.fsum)
    go(r.pre0, h.pre)
    w = near_weights(0, r)
    gx = r.gx
    grad = jnp.concatenate([gx[:HALF, :] + r.other[...].astype(F32), gx[HALF:, :]], axis=0)
    go.finish()
    gy, low, vectors = ffn_backward_body(0, grad.astype(BF).astype(F32), r, h, w)
    r.low[...] = low
    r.gy[...] = gy
    r.fvec[...] = vectors


def attn_backward_kernel(layer, r, h, go):
    section = r.at[0]
    half = section % 2
    mine = slice(layer, layer + 1)
    w = near_weights(layer, r)
    if layer == 0:
        loads = [go(r.__dict__[n], h.__dict__[n]) for n in SAVED]
        go.wait(loads[0])
    k = h if layer == 0 else r
    gsum, ggain, gshift = norm_back(k.summed[...], r.again[mine, :], r.gy[...].astype(F32))
    low = gsum.astype(BF)
    h.vec[0:1, :] = ggain
    h.vec[1:2, :] = gshift
    h.vec[7:15, :] = r.fvec[...]
    h.vec[15:16, :] = jnp.zeros((1, D), F32)
    g_attended = dot_nt(low, w.wo[...]).astype(BF)
    go.finish()
    differs = sight(r.at, r.lengths, r.ranks, r.segments)[1]
    lowest = low_lanes()
    ones = jnp.ones((WIDE, KEYS), BF)
    for p in range(PAIRS):
        at = slice(2 * HEAD * p, 2 * HEAD * (p + 1))
        later = slice(D + 2 * HEAD * p, D + 2 * HEAD * (p + 1))
        prob = k.prob[p]
        ga = two_heads(g_attended[:, at])
        gprob = dot_nt(ga, k.kv[:, later])
        h.gkv[later, :] = dot_nn(ga.T, prob.astype(BF)).astype(BF)
        centre = dot_nn(in_two(two_heads(g_attended[:, at].astype(F32) * k.mix[:, at])), ones)
        gscores = (prob * (gprob - centre)).astype(BF)
        gqc = one_pair(dot_nn(gscores, k.kv[:, at]))
        h.gkv[at, :] = dot_nn(two_heads(k.qc[:, at]).T, gscores).astype(BF)
        gwhole = gscores.astype(F32)
        gwide = unskewed_scores(gwhole).astype(BF)
        gqp = one_pair(dot_nn(gwide, k.rel[:, at]))
        h.grel[at, :] = dot_nn(two_heads(k.qp[:, at]).T, gwide)
        other_part = jnp.where(differs, gwhole, 0.0)
        other = jnp.sum(other_part, axis=-1, keepdims=True)
        same = jnp.sum(gwhole - other_part, axis=-1, keepdims=True)
        same_pair = jnp.where(lowest, same[:ROWS], same[ROWS:])
        other_pair = jnp.where(lowest, other[:ROWS], other[ROWS:])
        gqs = same_pair * r.seg[layer, 0:1, at] + other_pair * r.seg[layer, 1:2, at]
        segment = k.qs[:, at]
        h.vec[2:3, at] = jnp.sum(gqc, axis=0, keepdims=True) * SCALE
        h.vec[3:4, at] = jnp.sum(gqp, axis=0, keepdims=True) * SCALE
        h.vec[4:5, at] = jnp.sum(gqs, axis=0, keepdims=True) * SCALE
        h.vec[5:6, at] = jnp.sum(same_pair * segment, axis=0, keepdims=True)
        h.vec[6:7, at] = jnp.sum(other_pair * segment, axis=0, keepdims=True)
        h.turned[at, :ROWS] = low[:, at].astype(F32).T
        h.turned[at, ROWS:] = ((gqc + gqp + gqs) * SCALE).T
    few, step = KEYS - 128, D // 8
    for n, message in enumerate(r.first):
        d = section ^ n

        def chosen(ref, size, multiple):
            starts = [4 * size * e + size * d for e in range(8)]
            return jnp.concatenate([ref[aligned(m, multiple, size), :] for m in starts], axis=0)

        message[:SHARE, :256] = chosen(h.turned, step // 4, 8).astype(BF)
        message[:SHARE, 256:512] = chosen(h.grel, step // 4, 8).astype(BF)
        keyval = chosen(h.gkv, step // 2, 16)
        for j in range(2):
            rows = keyval[SHARE * j : SHARE * (j + 1)]
            message[:SHARE, 512 + 128 * j : 640 + 128 * j] = rows[:, :128]
            message[:SHARE, 768 + few * j : 768 + few * (j + 1)] = rows[:, 128:]
    joined = dot_nn(w.wkv[...], h.gkv[...])
    one, two = joined[:, M : M + HALF], joined[:, M + HALF :]
    first_half = jnp.zeros((1, 1), jnp.int32) + half == 0
    own, partner = jnp.where(first_half, one, two), jnp.where(first_half, two, one)
    gx = dot_nn(w.wq[...], h.turned[:, ROWS:].astype(BF)) + gsum.T
    gx = jnp.concatenate([gx[:, :HALF] + own, gx[:, HALF:]], axis=1)
    if layer > 0:
        r.send[...] = partner.T.astype(BF)
        r.gx[...] = gx.T
        r.second[:, : 2 * HALF] = r.out[...].T
        r.second[:, 2 * HALF :] = jnp.concatenate([partner, joined[:, :M]], axis=1).astype(BF)
        r.vec[...] = h.vec[...]
    else:
        h.second[:, : 2 * HALF] = gx.astype(BF)
        h.second[:, 2 * HALF : WIDE] = jnp.concatenate([partner, joined[:, :M]], axis=1).astype(BF)
        h.second[:, WIDE:] = r.later[...]
        for d in range(4):
            at = slice(SHARE * d, SHARE * (d + 1))
            for n, vec in enumerate((h.vec, r.vectors)):
                place = slice(SHARE * n, SHARE * (n + 1))
                wide = vec[10 + d : 11 + d, :]
                rows = [vec[:10, at]] + [wide[:, SHARE * j : SHARE * (j + 1)] for j in range(4)]
                rows = jnp.concatenate(rows + [jnp.zeros((2, SHARE), F32)], axis=0)
                h.parts[d, :, place] = rows.astype(BF)
        for n, message in enumerate(r.second):
            message[...] = h.second[aligned(SHARE * (section ^ n), SHARE), :]
        for n, message in enumerate(r.first):
            message[SHARE:, : 2 * SHARE] = h.parts[section ^ n]


def gathered_x(layer, r, h):
    for n in range(4):
        if layer == 0:
            rows = aligned((r.at[0] ^ n) * HALF, HALF)
            h.x[ROWS * n : ROWS * n + HALF, :] = r.content[rows, :]
            h.x[ROWS * n + HALF : ROWS * (n + 1), :] = r.query[rows, :]
        else:
            h.x[ROWS * n : ROWS * (n + 1), :] = r.before[n][ROWS:, :]


def put_halves(r, h):
    core = r.at[2]
    for j in range(4):
        r.kept[j] = h.pieces[2 * j + core]
        for part, given in enumerate(r.given):
            n = given.shape[1]
            given[j] = h.pieces[2 * j + 1 - core, n * part : n * (part + 1), :]


def shares_kernel(layer, r, h, go):
    wide, few = FF // 8, FF // 32
    for t in range(4):

        @pl.when(r.at[0] == t)
        def _():
            for d in range(8):
                at = slice(few * d, few * (d + 1))
                held = slice(wide * d + few * t, wide * d + few * (t + 1))
                r.bias[:, at] = r.fbin[layer : layer + 1, held]
                r.inner[:, at] = r.win[layer, :, held]
                r.outer[at, :] = r.wout[layer, held, :]


def ffn_weights_kernel(layer, fast, r, h, go):
    mine = slice(layer, layer + 1)
    gathered_x(layer, r, h)
    attended = jnp.concatenate([a[:ROWS, :] for a in r.acts], axis=0)
    summed = dot_nn(attended, r.wo[layer]) + h.x[...].astype(F32)
    y = norm_parts(summed)[0] * r.again[mine, :] + r.ashift[mine, :]
    h.y[...] = y.astype(BF)
    for n, low in enumerate(r.low):
        rows = low[low.shape[0] - ROWS :, :]
        h.low[ROWS * n : ROWS * (n + 1), :] = rows
        h.lowt[:, ROWS * n : ROWS * (n + 1)] = rows.T
    width, few = FF // 8, FF // 32
    for t in range(2):
        at = slice(width * t, width * (t + 1))
        pre = dot_nn(h.y[...], r.inner[:, at]) + r.bias[:, at]
        active, slope = gelu_both(pre)
        gpre = (dot_nt(h.low[...], r.outer[at, :]) * slope).astype(BF)
        grad_in = dot_nn(gpre.T, h.y[...]).astype(BF)
        grad_out = dot_nn(h.lowt[...], active.astype(BF)).astype(BF)
        if fast:
            for d in range(4):
                h.pieces[4 * t + d, :few, :] = grad_in[few * d : few * (d + 1), :]
            for d in range(8):
                h.pieces[d, few:, at] = grad_out[few * d : few * (d + 1), :]
        else:
            r.grads[0][at, :] = grad_in
            r.grads[1][:, at] = grad_out
    if fast:
        put_halves(r, h)


def attn_weights_kernel(fast, r, h, go):
    parts = []
    for layer in range(LAYERS):
        grads = attn_grads(layer, r, h)
        if fast:
            for n, grad in enumerate(grads):
                h.grads[layer, SHARE * n : SHARE * n + grad.shape[0], :] = grad
        else:
            for n, grad in enumerate(grads):
                r.grads[4 * layer + n][...] = grad.astype(BF)
    vectors = None
    for f in r.first:
        part = f[SHARE : SHARE + 16, : 2 * SHARE].astype(F32)
        vectors = part if vectors is None else vectors + part
    if not fast:
        r.vectors[...] = vectors
        return
    vectors = jnp.concatenate([vectors[:8], vectors[8:]], axis=1)
    step = D // 8
    for d in range(8):
        rows = []
        for layer in range(LAYERS):
            for n in range(4):
                size = step // 2 if n == 3 else step // 4
                start = SHARE * n + size * d
                rows.append(h.grads[layer, start : start + size, :])
        rows = jnp.concatenate(rows + [vectors, jnp.zeros_like(vectors)], axis=0)
        h.pieces[d] = rows.astype(BF)
    put_halves(r, h)


def attn_grads(layer, r, h):
    section = r.at[0]
    half = section % 2
    first = [f.at[pl.ds(0, SHARE)] for f in (r.first, r.earlier)[layer]]
    gathered_x(layer, r, h)
    for pair in range(2):
        rows = aligned((section ^ (2 * pair)) // 2 * M, M)
        h.joined[pair, :M, :] = r.memory[layer, rows, :]
        for n in (2 * pair, 2 * pair + 1):
            place = half ^ (n & 1)
            h.joined[pair, aligned(M + HALF * place, HALF), :] = h.x[ROWS * n : ROWS * n + HALF, :]
    low = jnp.concatenate([f[:, :128] for f in first], axis=1)
    proj = jnp.concatenate([f[:, 128:256] for f in first], axis=1)
    grad_q = dot_nn(proj, h.x[...])
    attended = jnp.concatenate([a[:ROWS, :] for a in (r.acts0, r.acts1)[layer]], axis=0)
    grad_o = dot_nn(low, attended)
    few = KEYS - 128
    grad_kv = grad_rel = None
    for pair in range(2):
        both = add(first[2 * pair][:, 512:], first[2 * pair + 1][:, 512:])
        both = jnp.concatenate(
            [
                jnp.concatenate([both[:, :128], both[:, 256 : 256 + few]], axis=1),
                jnp.concatenate([both[:, 128:256], both[:, 256 + few :]], axis=1),
            ],
            axis=0,
        )
        part = dot_nn(both, h.joined[pair])
        grad_kv = part if grad_kv is None else grad_kv + part
    for n in range(2):
        place = half ^ n
        total = add(first[n][:, 256:512], first[n + 2][:, 256:512])
        rows = r.table[aligned(HALF * (1 - place), HALF, WIDE), :]
        part = dot_nn(total, rows)
        grad_rel = part if grad_rel is None else grad_rel + part
    return grad_q, grad_o, grad_rel, grad_kv


def add(a, b):
    return (a.astype(F32) + b.astype(F32)).astype(BF)


def whole(shape):
    return pl.BlockSpec(shape, lambda i: (0,) * len(shape))


def gather_kernel(at_ref, *refs):
    section = at_ref[0]
    start = refs[0].shape[1] - 2 * WIDE
    early = [r.at[:, pl.ds(start, WIDE)] for r in refs[:4]]
    late = [r.at[:, pl.ds(start + WIDE, WIDE)] for r in refs[:4]]
    small_ref = refs[4]
    outc_ref, outq_ref, gradc_ref, gradq_ref, mem_ref = refs[5:10]
    bias_ref, seg_ref, again_ref, ashift_ref, inb_ref, outb_ref, fgain_ref, fshift_ref = refs[10:18]

    def in_order(blocks):
        odd = jnp.zeros((1, 1), jnp.int32) + section % 2 == 1
        high = jnp.zeros((1, 1), jnp.int32) + section // 2 == 1
        a, b, c, d = blocks
        a, b, c, d = (
            jnp.where(odd, b, a), jnp.where(odd, a, b), jnp.where(odd, d, c), jnp.where(odd, c, d)
        )
        left, right = jnp.concatenate([a, b], axis=1), jnp.concatenate([c, d], axis=1)
        return jnp.concatenate([jnp.where(high, right, left), jnp.where(high, left, right)], axis=1)

    def blocks(four, start):
        return [f[:, start : start + HALF].astype(F32) for f in four]

    outc_ref[...] = in_order(blocks(late, 0)).astype(BF)
    outq_ref[...] = in_order(blocks(late, HALF)).astype(BF)
    own, passed = blocks(early, 0), blocks(early, 2 * HALF)
    gradc_ref[...] = in_order([own[k] + passed[k ^ 1] for k in range(4)])
    gradq_ref[...] = in_order(blocks(early, HALF))
    high = jnp.zeros((1, 1), jnp.int32) + section // 2 == 1
    for layer, four in ((0, early), (1, late)):
        a, b, c, d = blocks(four, 3 * HALF)
        one, two = a + b, c + d
        mem_ref[layer] = jnp.concatenate(
            [jnp.where(high, two, one), jnp.where(high, one, two)], axis=1
        )
    for layer in range(LAYERS):
        mine = slice(layer, layer + 1)

        held = slice(SHARE * layer, SHARE * (layer + 1))

        def vector(row):
            return small_ref[row : row + 1, held].astype(F32)

        for j in range(3):
            bias_ref[j, mine, :] = vector(2 + j)
        for j in range(2):
            seg_ref[layer, j : j + 1, :] = vector(5 + j)
        again_ref[mine, :] = vector(0)
        ashift_ref[mine, :] = vector(1)
        fgain_ref[mine, :] = vector(7)
        fshift_ref[mine, :] = vector(8)
        outb_ref[mine, :] = vector(9)
        for j in range(4):
            inb_ref[mine, SHARE * j : SHARE * (j + 1)] = vector(10 + j)


def gather_rows(at, rows_out, small):
    rows = 4 * HALF
    vector = ((LAYERS, SHARE), F32)
    shapes = [
        ((SHARE, rows), BF),
        ((SHARE, rows), BF),
        ((SHARE, rows), F32),
        ((SHARE, rows), F32),
        ((LAYERS, SHARE, 2 * M), F32),
        ((3, LAYERS, SHARE), F32),
        ((LAYERS, 2, SHARE), F32),
        vector,
        vector,
        ((LAYERS, FF // 4), F32),
        vector,
        vector,
        vector,
    ]
    return pl.pallas_call(
        gather_kernel,
        grid=(1,),
        in_specs=[SCALARS.spec] + [whole(a.shape) for a in (*rows_out, small)],
        out_specs=[whole(s) for s, _ in shapes],
        out_shape=[jax.ShapeDtypeStruct(s, t) for s, t in shapes],
        compiler_params=params(),
        cost_estimate=cost(1_000_000, 2_000_000),
        name="gather_rows",
    )(at, *rows_out, small)


def final_ffn_kernel(r, h, go):
    few = FF // 32
    for n, message in enumerate(r.ffn):
        h.got[r.at[0] ^ n] = message[...].astype(F32)
    for layer in range(LAYERS):
        rows_at = slice(few * layer, few * (layer + 1))
        for s in range(4):
            held = slice(few * s, few * (s + 1))
            r.fin[layer, :, held] = h.got[s, rows_at, :SHARE].T
            for e in range(2):
                place = slice(FF // 8 * e + few * s, FF // 8 * e + few * (s + 1))
                start = SHARE + few * e
                r.fout[layer, :, place] = h.got[s, rows_at, start : start + few]


def final_attn_kernel(r, h, go):
    for n, message in enumerate(r.attn):
        h.attn[r.at[0] ^ n] = message[...].astype(F32)
    step = D // 8
    for layer in range(LAYERS):
        lanes = slice(SHARE * layer, SHARE * (layer + 1))
        start = 0
        for made, size in ((r.q, step // 4), (r.o, step // 4), (r.rel, step // 4), (r.kv, step // 2)):
            blocks = [h.attn[s, start : start + size, lanes] for s in range(4)]
            made[layer] = jnp.concatenate(blocks, axis=0).T
            start += size


def final_ffn(at, ffn):
    return run(
        final_ffn_kernel,
        "final_ffn",
        dict(at=(at, SCALARS), ffn=(ffn, NEAR)),
        dict(
            fin=((LAYERS, SHARE, FF // 8), F32, SMALL),
            fout=((LAYERS, D // 8, FF // 4), F32, SMALL),
        ),
        dict(got=((4, FF // 16, 2 * SHARE), F32)),
    )


def final_attn(at, attn):
    half = ((LAYERS, SHARE, SHARE // 2), F32, SMALL)
    return run(
        final_attn_kernel,
        "final_attn",
        dict(at=(at, SCALARS), attn=(attn, NEAR)),
        dict(q=half, kv=((LAYERS, SHARE, SHARE), F32, SMALL), o=half, rel=half),
        dict(attn=((4, ROWS_ATTN + 8, 2 * SHARE), F32)),
    )


def split_kernel(r, h, go):
    chip = r.at[1]
    for part, got in enumerate(r.got):
        n = got.shape[1]
        rows = pl.ds(n * part, n)
        for m, p in enumerate((chip, chip ^ 2)):
            r.keep[m, rows, :] = add(r.kept[p, rows, :], got[p])
        place, put = n * part, 0
        while place >= r.send[put].shape[1]:
            place, put = place - r.send[put].shape[1], put + 1
        for m, p in enumerate((chip ^ 1, chip ^ 3)):
            r.send[put][m, pl.ds(place, n), :] = add(r.kept[p, rows, :], got[p])


def fold_kernel(start, r, h, go):
    rows = pl.ds(start, r.got.shape[1])
    r.own[...], r.far[...] = [add(r.keep[m, rows, :], r.got[m]) for m in range(2)]


def sum_kernel(r, h, go):
    r.total[...] = add(r.own[...], r.got[...])


def shared_attn_kernel(r, h, go):
    total = [own[...].astype(F32) + got[...].astype(F32) for own, got in zip(r.own, r.got)]
    total = jnp.concatenate(total, axis=0)
    layers = [total[ROWS_ATTN * n : ROWS_ATTN * (n + 1)] for n in range(LAYERS)]
    for t in range(4):
        at = slice(SHARE * t, SHARE * (t + 1))
        rows = jnp.concatenate([m[:, at] for m in layers], axis=1)
        h.parts[t] = jnp.concatenate([rows, jnp.zeros((8, 2 * SHARE), F32)], axis=0).astype(BF)
    for n, part in enumerate(r.parts):
        part[...] = h.parts[r.at[0] ^ n]
    vectors = total[LAYERS * ROWS_ATTN : LAYERS * ROWS_ATTN + 8]
    r.vectors[...] = jnp.concatenate([vectors[:, : 2 * SHARE], vectors[:, 2 * SHARE :]], axis=0)


def shared_kernel(r, h, go):
    few = FF // 32
    for layer, total in enumerate((add(r.own[...], r.got[...]), r.later[...])):
        rows = slice(few * layer, few * (layer + 1))
        for t in range(4):
            at = slice(SHARE * t, SHARE * (t + 1))
            h.parts[t, rows, :SHARE], h.parts[t, rows, SHARE:] = total[:few, at], total[few:, at]
    for n, part in enumerate(r.parts):
        part[...] = h.parts[r.at[0] ^ n]


def split_pieces(at, made, cuts=(), after=()):
    got = [swapped(a, DP, 1) for a in made.given]
    shape = (2,) + made.kept.shape[1:]
    ins = dict(at=(at, SCALARS), kept=(made.kept, NEAR), got=(got, NEAR))
    parts = [(2, n, shape[2]) for n in cuts or shape[1:2]]
    return run(
        split_kernel, "split_pieces", ins, dict(keep=(shape, BF, NEAR), send=(parts, BF, NEAR)), {},
        after=after,
    )


def fold_pieces(split, part=0, after=()):
    got = swapped(split.send[part], DP, 2)
    start = sum(a.shape[1] for a in split.send[:part])
    ins = dict(keep=(split.keep, NEAR), got=(got, NEAR))
    shape = got.shape[1:]
    folded = run(
        functools.partial(fold_kernel, start), "fold_pieces", ins,
        dict(own=(shape, BF, NEAR), far=(shape, BF, NEAR)), {}, after=after,
    )
    return folded.own, swapped(folded.far, DP, 4)


def sum_pieces(folded, after=()):
    own, got = folded
    ins = dict(own=(own, NEAR), got=(got, NEAR))
    return run(
        sum_kernel, "sum_pieces", ins, dict(total=(got.shape, BF, NEAR)), {}, after=after
    ).total


def shared_attn(at, folded, after=()):
    ins = dict(
        at=(at, SCALARS), own=([f[0] for f in folded], NEAR), got=([f[1] for f in folded], NEAR)
    )
    shape = (ROWS_ATTN + 8, 2 * SHARE)
    return run(
        shared_attn_kernel, "shared_attn", ins,
        dict(parts=([shape] * 4, BF, NEAR), vectors=((16, 2 * SHARE), F32, NEAR)),
        dict(parts=((4,) + shape, BF)), after=after,
    )


def shared_pieces(at, folded, later, after=()):
    own, got = folded
    ins = dict(
        at=(at, SCALARS), own=(own, NEAR), got=(got, NEAR), later=(later, NEAR)
    )
    shape = (FF // 16, 2 * SHARE)
    return run(
        shared_kernel, "shared_pieces", ins,
        dict(parts=([shape] * 4, BF, NEAR)),
        dict(parts=((4,) + shape, BF)), after=after,
    ).parts


def swapped(x, axis, k):
    return lax.ppermute(x, axis, [(i, i ^ k) for i in range(lax.axis_size(axis))])


def from_all(x):
    return [x] + [swapped(x, SECTION, k) for k in (1, 2, 3)]


def messages(parts):
    return [parts[0]] + [swapped(parts[k], SECTION, k) for k in (1, 2, 3)]


def on_device(
    content_in,
    query_in,
    memory,
    doc_lengths,
    perm_rank,
    segment_ids,
    w_query,
    w_keyval,
    w_out,
    w_rel,
    head_bias,
    seg_embed,
    attn_gain,
    attn_shift,
    ffn_in,
    ffn_in_bias,
    ffn_out,
    ffn_out_bias,
    ffn_gain,
    ffn_shift,
    cot_content,
    cot_query,
):
    ORDER.clear()
    dp = lax.axis_size(DP)
    fast = dp == 8
    index = lax.axis_index(DP)
    at = jnp.stack([lax.axis_index(SECTION), index // 2, index % 2]).astype(jnp.int32)
    table = position_table()
    marks = dict(
        at=(at, SCALARS),
        lengths=(doc_lengths, SCALARS),
        ranks=(perm_rank, SMALL),
        segments=(segment_ids, SMALL),
    )
    attn_v = dict(
        bias=(head_bias.transpose(1, 0, 2), SMALL),
        seg=(seg_embed, SMALL),
        again=(attn_gain, SMALL),
        ashift=(attn_shift, SMALL),
    )
    ffn_v = dict(
        fbin=(ffn_in_bias, SMALL),
        fbout=(ffn_out_bias, SMALL),
        fgain=(ffn_gain, SMALL),
        fshift=(ffn_shift, SMALL),
    )
    matrices = dict(
        wq=w_query, wkv=w_keyval, wr=w_rel, wo=w_out, win=ffn_in, wout=ffn_out,
    )
    near = {n: (a, NEAR) for n, a in matrices.items()}

    def of(which, *names):
        return {n: which[n] for n in which if n in names}

    first = run(
        forward_first_kernel,
        "forward_first",
        dict(
            **marks,
            content=(content_in, FAR),
            query=(query_in, FAR),
            memory=(memory, FAR),
            table=(table, FAR),
            **{n: (a, FAR) for n, a in matrices.items()},
            **attn_v,
            **ffn_v,
        ),
        dict(
            acts=((2 * ROWS, D), BF, NEAR),
            half=((HALF, D), BF, NEAR),
            pre0=((ROWS, FF), F32, FAR),
            fsum0=((ROWS, D), F32, FAR),
            **{n: (*s, FAR) for n, s in SAVED.items()},
        ),
        dict(**FORWARD_SCRATCH, table=((WIDE, D), BF), **WEIGHTS, **SAVED),
        copies=24,
        flops=2_400_000_000,
        moved=16_000_000,
    )
    other = swapped(first.half, SECTION, 1)
    acts0 = from_all(first.acts)
    second = run(
        forward_second_kernel,
        "forward_second",
        dict(
            **marks,
            acts0=(first.acts, NEAR),
            other=(other, NEAR),
            memory=(memory, FAR),
            table=(table, NEAR),
            cotc=(cot_content, FAR),
            cotq=(cot_query, FAR),
            **near,
            **attn_v,
            **ffn_v,
        ),
        dict(
            acts=((2 * ROWS, D), BF, NEAR),
            out=((ROWS, D), BF, NEAR),
            gy=((ROWS, D), BF, NEAR),
            fvec=((8, D), F32, NEAR),
            **{n: (*s, NEAR) for n, s in SAVED.items()},
        ),
        dict(**FORWARD_SCRATCH, grad=((ROWS, D), BF)),
        copies=4,
        flops=3_600_000_000,
        moved=16_000_000,
    )
    acts1 = from_all(second.acts)

    def attn_backward(layer, saved, gy, fvec, after=(), **extra):
        ins = dict(
            **marks,
            gy=(gy, NEAR),
            fvec=(fvec, NEAR),
            **{n: (saved.__dict__[n], FAR if layer == 0 else NEAR) for n in SAVED},
            **{n: near[n] for n in list(WEIGHTS)[:4] if n != list(WEIGHTS)[2]},
            **attn_v,
            **{n: (a, NEAR) for n, a in extra.items()},
        )
        scratch = dict(
            vec=((16, D), F32),
            turned=((D, 2 * ROWS), F32),
            gkv=((2 * D, KEYS), BF),
            grel=((D, WIDE), F32),
        )
        rows = FIRST[0] if layer else FIRST[0] + 16
        outs = dict(first=([(rows, FIRST[1])] * 4, BF, NEAR))
        if layer == 0:
            outs.update(second=([SECOND] * 4, BF, NEAR))
            scratch.update(SAVED, second=((D, 2 * WIDE), BF), parts=((4, 16, 2 * SHARE), BF))
        else:
            outs.update(
                second=((D, WIDE), BF, NEAR),
                gx=((ROWS, D), F32, NEAR),
                send=((HALF, D), BF, NEAR),
                vec=((16, D), F32, NEAR),
            )
        return run(
            functools.partial(attn_backward_kernel, layer), "attn_backward", ins, outs, scratch,
            copies=10, flops=1000, moved=1000, after=after,
        )

    def inputs_of(layer):
        if layer == 0:
            return dict(content=(content_in, NEAR), query=(query_in, NEAR))
        return dict(before=(acts0, NEAR))

    def grads_of(shape, plain, cuts=2):
        if fast:
            parts = [(4, shape[0] // cuts, shape[1])] * cuts
            return dict(kept=((4,) + shape, BF, NEAR), given=(parts, BF, NEAR))
        return dict(grads=(plain, BF, SMALL))

    def shares_of(layer):
        return run(
            functools.partial(shares_kernel, layer),
            "shares",
            dict(at=marks["at"], **of(near, "win", "wout"), **of(ffn_v, "fbin")),
            dict(
                inner=((D, D), BF, NEAR),
                outer=((D, D), BF, NEAR),
                bias=((1, D), F32, NEAR),
            ),
            {},
        )

    def ffn_weights(layer, shares, acts, lows, after=()):
        ins = dict(
            at=marks["at"],
            **inputs_of(layer),
            **of(near, "wo"),
            **of(attn_v, "again", "ashift"),
            inner=(shares.inner, NEAR),
            outer=(shares.outer, NEAR),
            bias=(shares.bias, NEAR),
            acts=(acts, NEAR),
            low=(lows, NEAR),
        )
        shape = (ROWS_FFN, D)
        tall = ((4 * ROWS, D), BF)
        return run(
            functools.partial(ffn_weights_kernel, layer, fast),
            "ffn_weights",
            ins,
            grads_of(shape, [(D, D), (D, D)]),
            dict(x=tall, y=tall, low=tall, lowt=((D, 4 * ROWS), BF), pieces=((8,) + shape, BF)),
            flops=1000,
            moved=1000,
            after=after,
        )

    def attn_weights(notes, earlier, after=()):
        ins = dict(
            at=marks["at"],
            content=(content_in, NEAR),
            query=(query_in, NEAR),
            before=(acts0, NEAR),
            memory=(memory, NEAR),
            table=(table, NEAR),
            acts0=(acts0, NEAR),
            acts1=(acts1, NEAR),
            first=(notes, NEAR),
            earlier=(earlier, NEAR),
        )
        shape = (2 * ROWS_ATTN + 2 * ROWS_VEC, D)
        outs = grads_of(shape, [(SHARE, D), (SHARE, D), (SHARE, D), (2 * SHARE, D)] * 2, 4)
        if not fast:
            outs.update(vectors=((2 * ROWS_VEC, 2 * SHARE), F32, SMALL))
        return run(
            functools.partial(attn_weights_kernel, fast),
            "attn_weights",
            ins,
            outs,
            dict(
                x=((4 * ROWS, D), BF),
                joined=((2, KEYS, D), BF),
                grads=((LAYERS, 5 * SHARE, D), F32),
                pieces=((8,) + shape, BF),
            ),
            flops=10**12,
            moved=10**9,
            after=after,
        )

    back1 = attn_backward(1, second, second.gy, second.fvec, acts0[1:], out=second.out)
    received = swapped(back1.send, SECTION, 1)
    parts1 = messages(back1.first)
    shares1, shares0 = shares_of(1), shares_of(0)
    fgrads1 = ffn_weights(1, shares1, acts1, acts1)
    third = run(
        ffn_backward_kernel,
        "ffn_backward",
        dict(
            gx=(back1.gx, NEAR),
            other=(received, NEAR),
            fsum0=(first.fsum0, FAR),
            pre0=(first.pre0, FAR),
            **of(near, "win", "wout"),
            **of(ffn_v, "fgain"),
        ),
        dict(
            low=((ROWS, D), BF, NEAR), gy=((ROWS, D), BF, NEAR), fvec=((8, D), F32, NEAR)
        ),
        dict(fsum=((ROWS, D), F32), pre=((ROWS, FF), F32)),
        copies=4,
        flops=10**12,
        moved=10**9,
    )
    lows0 = from_all(third.low)
    if fast:
        split_f1 = split_pieces(at, fgrads1, after=parts1[1:])
    back0 = attn_backward(
        0, first, third.gy, third.fvec, later=back1.second, vectors=back1.vec
    )
    parts0 = messages(back0.first)
    rows_out = back0.second
    fgrads0 = ffn_weights(0, shares0, acts0, lows0)
    if fast:
        fold_f1 = fold_pieces(split_f1)
        split_f0 = split_pieces(at, fgrads0)
    agrads = attn_weights(parts0, parts1)
    if fast:
        sum_f1 = sum_pieces(fold_f1)
        fold_f0 = fold_pieces(split_f0)
        split_a = split_pieces(at, agrads, (192, 64))
        folded = [fold_pieces(split_a, 0)]
        rows_all = messages(rows_out)
        ffn = messages(shared_pieces(at, fold_f0, sum_f1, rows_all[1:]))
        folded.append(fold_pieces(split_a, 1))
        made = final_ffn(at, ffn)
        fin, fout = made.fin, made.fout
        shared_a = shared_attn(at, folded)
        attn_all = messages(shared_a.parts)
        outs = gather_rows(at, rows_all, shared_a.vectors)
        made = final_attn(at, attn_all)
        wq, wkv, wo, wr = made.q, made.kv, made.o, made.rel
        fout = fout.transpose(0, 2, 1)
    else:
        outs = gather_rows(at, messages(rows_out), lax.psum(agrads.vectors, DP))
        section = at[0]

        def owned(rows):
            part = rows.reshape((dp, -1) + rows.shape[1:])
            part = lax.psum_scatter(part, DP, scatter_dimension=0, tiled=False)
            part = lax.psum(part, SECTION)
            width = part.shape[1] // 4
            return lax.dynamic_slice_in_dim(part, section * width, width, 1).astype(F32).T

        def at_share(share, count, axis=0):
            cut = share.reshape(share.shape[:axis] + (count, 1, -1) + share.shape[axis + 1 :])
            full = jnp.zeros(cut.shape[: axis + 1] + (4,) + cut.shape[axis + 2 :], BF)
            full = lax.dynamic_update_slice_in_dim(full, cut, section, axis + 1)
            return full.reshape(share.shape[:axis] + (-1,) + share.shape[axis + 1 :])

        def plain(fgrads, agrads):
            parts = [at_share(a, 8) for a in agrads]
            parts += [at_share(fgrads[0], 8), at_share(fgrads[1], 8, 1)]
            q, o, rel, kv, fin, fout = [owned(a) for a in parts]
            return q, kv, o, rel, fin, fout

        pairs = zip(plain(fgrads0.grads, agrads.grads[:4]), plain(fgrads1.grads, agrads.grads[4:]))
        wq, wkv, wo, wr, fin, fout = [jnp.stack(p) for p in pairs]
    return (
        outs[0].T,
        outs[1].T,
        outs[2].T,
        outs[3].T,
        outs[4].transpose(0, 2, 1),
        wq,
        wkv,
        wo,
        wr,
        outs[5].transpose(1, 0, 2),
        outs[6],
        outs[7],
        outs[8],
        fin,
        outs[9],
        fout,
        outs[10],
        outs[11],
        outs[12],
    )


def solution(mesh):
    in_specs = (
        P(DP, None),
        P(DP, None),
        P(None, DP, None),
        P(DP),
        P(DP, None),
        P(DP, None),
    ) + (P(),) * 14 + (P(DP, None), P(DP, None))
    weight, vector = P(None, SECTION, DP), P(None, SECTION)
    out_specs = (
        P(DP, SECTION),
        P(DP, SECTION),
        P(DP, SECTION),
        P(DP, SECTION),
        P(None, DP, SECTION),
        weight,
        weight,
        weight,
        weight,
        P(None, None, SECTION),
        P(None, None, SECTION),
        vector,
        vector,
        weight,
        vector,
        weight,
        vector,
        vector,
        vector,
    )
    return jax.shard_map(
        on_device, mesh=mesh, in_specs=in_specs, out_specs=out_specs, check_vma=False
    )
```

```python
import functools
import math

import jax
import jax.numpy as jnp
import numpy as np
from jax import lax
from jax.experimental import pallas as pl
from jax.experimental.pallas import tpu as pltpu
from jax.sharding import PartitionSpec as P

D = 768
HEADS = 12
HEAD = 64
FF = 3072
S = 128
M = 64
LAYERS = 2
HALF = S // 2
KEYS = M + S
TABLE = M + 2 * S - 1
WIDE = 256
ROWS = 2 * HALF
PAIRS = HEADS // 2
SHARE = D // 4
SCALE = HEAD**-0.5
NEGATIVE = -1e30
EPSILON = 1e-05
SECTION, DP = "section", "dp"
BF = jnp.bfloat16
F32 = jnp.float32
GELU_C = math.sqrt(2.0 / math.pi)
MEG = 1 << 20

FIRST = (SHARE, 7 * 128)
SECOND = (SHARE, 2 * WIDE)
ROWS_ATTN = 120
ROWS_VEC = 8
ROWS_FFN = FF // 16


def position_table():
    distance = (M + S - 1 - np.arange(TABLE)).astype(np.float32)
    inverse = np.exp(np.arange(0, D, 2).astype(np.float32) * np.float32(-math.log(10000.0) / D))
    angles = distance[:, None] * inverse[None, :].astype(np.float32)
    table = np.concatenate([np.sin(angles), np.cos(angles)], axis=1)
    table = np.concatenate([table, np.zeros((1, D), np.float32)], axis=0)
    return jnp.asarray(table, jnp.float32).astype(BF)


def dot_nn(a, b):
    return lax.dot_general(a, b, (((1,), (0,)), ((), ())), preferred_element_type=F32)


def dot_nt(a, b):
    return lax.dot_general(a, b, (((1,), (1,)), ((), ())), preferred_element_type=F32)


def norm_parts(values):
    centre = values - jnp.mean(values, axis=-1, keepdims=True)
    spread = jnp.mean(centre * centre, axis=-1, keepdims=True)
    root = lax.rsqrt(spread + EPSILON)
    return centre * root, root


def norm_back(values, gain, grad):
    normal, root = norm_parts(values)
    scaled = grad * gain
    grad_gain = jnp.sum(grad * normal, axis=0, keepdims=True)
    grad_shift = jnp.sum(grad, axis=0, keepdims=True)
    first = jnp.mean(scaled, axis=-1, keepdims=True)
    second = jnp.mean(scaled * normal, axis=-1, keepdims=True)
    return root * (scaled - first - normal * second), grad_gain, grad_shift


def gelu(v):
    return 0.5 * v * (1.0 + jnp.tanh(GELU_C * (v + 0.044715 * (v * v * v))))


def gelu_both(v):
    square = v * v
    bend = jnp.tanh(GELU_C * (v + 0.044715 * (square * v)))
    half = 0.5 * (1.0 + bend)
    slope = half + 0.5 * v * (1.0 - bend * bend) * (GELU_C * (1.0 + 3 * 0.044715 * square))
    return v * half, slope


def low_lanes():
    return lax.broadcasted_iota(jnp.int32, (1, 2 * HEAD), 1) < HEAD


def two_heads(pair):
    low = low_lanes()
    zero = jnp.zeros_like(pair)
    return jnp.concatenate([jnp.where(low, pair, zero), jnp.where(low, zero, pair)], axis=0)


def one_pair(stacked):
    half = stacked.shape[0] // 2
    return jnp.where(low_lanes(), stacked[:half], stacked[half:])


def in_two(values):
    high = values.astype(BF)
    return jnp.concatenate([high, (values - high.astype(F32)).astype(BF)], axis=1)


def skewed_scores(wide):
    parts = [
        pltpu.roll(wide[HALF * b : HALF * (b + 1)], WIDE - HALF + 1, 1, stride=1, stride_axis=0)
        for b in range(4)
    ]
    return jnp.concatenate(parts, axis=0)[:, :KEYS]


def unskewed_scores(scores):
    rows, wide = 4 * HALF, WIDE // 2
    shift = HALF - 1 - lax.broadcasted_iota(jnp.int32, (rows, wide), 0) % HALF
    lane = lax.broadcasted_iota(jnp.int32, (rows, wide), 1)
    source = (lane - shift) & (wide - 1)
    wrapped = lane < shift
    rest = jnp.concatenate([scores[:, wide:], jnp.zeros((rows, WIDE - KEYS), F32)], axis=1)
    first, second = (
        jnp.take_along_axis(a, source, axis=1, mode=lax.GatherScatterMode.PROMISE_IN_BOUNDS)
        for a in (scores[:, :wide], rest)
    )
    return jnp.concatenate(
        [jnp.where(wrapped, 0.0, first), jnp.where(wrapped, first, second)], axis=1
    )


def sight(at_ref, lengths_ref, ranks_ref, segments_ref):
    seq, half = at_ref[0] // 2, at_ref[0] % 2
    ranks = ranks_ref[pl.ds(seq, 1), :]
    segments = segments_ref[pl.ds(seq, 1), :]
    place = lax.broadcasted_iota(jnp.int32, (1, S), 1)
    lengths = lengths_ref[...].astype(F32)
    own = lax.broadcasted_iota(jnp.int32, lengths.shape, 1) == seq
    length = jnp.sum(jnp.where(own, lengths, 0.0), axis=-1, keepdims=True)
    live = jnp.where(place.astype(F32) < length, ranks, 2 * S)
    key_rank = jnp.concatenate([jnp.full((1, M), -1, jnp.int32), live], axis=1)
    key_segment = jnp.concatenate([jnp.zeros((1, M), jnp.int32), segments], axis=1)
    row = lax.broadcasted_iota(jnp.int32, (HALF, S), 0) + half * HALF
    column = lax.broadcasted_iota(jnp.int32, (HALF, S), 1)

    def upright(values):
        wide = jnp.where(row == column, values.astype(F32), 0.0)
        return jnp.sum(wide, axis=-1, keepdims=True).astype(jnp.int32)

    own_rank, own_segment = upright(ranks), upright(segments)
    reach = jnp.concatenate([own_rank, own_rank - 1], axis=0)
    hidden = jnp.where(key_rank <= reach, 0.0, 1.0)
    differs = jnp.where(jnp.concatenate([own_segment] * 2, axis=0) != key_segment, 1.0, 0.0)
    return [jnp.concatenate([a] * 2, axis=0) > 0.0 for a in (hidden, differs)]


class Mover:
    def __init__(self, semaphores):
        self.semaphores, self.count, self.open = semaphores, 0, []

    def __call__(self, source, target):
        copy = pltpu.make_async_copy(source, target, self.semaphores.at[self.count])
        self.count += 1
        copy.start()
        self.open.append(copy)
        return copy

    def wait(self, *copies):
        for copy in copies:
            if any(copy is other for other in self.open):
                self.open = [other for other in self.open if other is not copy]
                copy.wait()

    def finish(self):
        self.wait(*list(self.open))


class Bag:
    def __init__(self, names, values):
        self.__dict__.update(zip(names, values))


class Place:
    def __init__(self, seen, space):
        self.spec, self.space = pl.BlockSpec(memory_space=seen), space

    def operand(self, array):
        if self.space is None:
            return array
        return pltpu.with_memory_space_constraint(array, self.space)

    def result(self, shape, kind):
        return jax.ShapeDtypeStruct(shape, kind) if self.space is None else self.space(shape, kind)


SCALARS = Place(pltpu.SMEM, pltpu.HBM)
SMALL = Place(pltpu.VMEM, pltpu.HBM)
HERE = None
FAR = Place(pl.ANY, pltpu.HBM)
NEAR = Place(pltpu.VMEM, pltpu.VMEM)
TOKEN = pl.BlockSpec(memory_space=pl.ANY)
SPARE = 4 * MEG


def padded_bytes(shape, kind):
    *front, rows, columns = shape
    return math.prod(front) * -(-rows // 16) * 16 * -(-columns // 128) * 128 * jnp.dtype(kind).itemsize


def params(limit=8 * MEG):
    return pltpu.CompilerParams(vmem_limit_bytes=limit)


def cost(flops, moved):
    return pl.CostEstimate(flops=flops, bytes_accessed=moved, transcendentals=0)


ORDER = []


def position():
    index = lax.axis_index(DP)
    return [lax.axis_index(SECTION), index // 2, index % 2]


def run(kernel, name, ins, outs, scratch, copies=1, flops=1000, moved=1000, after=()):
    after = [place.operand(a) for a, place in ORDER[-1:]] + list(after)
    ins = {n: value for n, value in ins.items() if value[1] is not HERE}
    arrays, counts, specs, held_bytes = [], [], [], 0
    for value, place in ins.values():
        many = isinstance(value, (list, tuple))
        counts.append(len(value) if many else 0)
        for a in value if many else [value]:
            arrays.append(place.operand(a))
            specs.append(place.spec)
            held_bytes += padded_bytes(a.shape, a.dtype) if place is SMALL else 0
    shapes, out_specs = [], []
    for shape, kind, place in outs.values():
        many = isinstance(shape, list)
        counts.append(len(shape) if many else 0)
        for one in shape if many else [shape]:
            shapes.append(place.result(one, kind))
            out_specs.append(place.spec)
            held_bytes += 2 * padded_bytes(one, kind) if place is SMALL else 0
    held_bytes += sum(padded_bytes(*s) for s in scratch.values())

    def grouped(refs, counts):
        refs = list(refs)
        taken = []
        for count in counts:
            taken.append([refs.pop(0) for _ in range(count)] if count else refs.pop(0))
        return taken

    def body(*refs):
        refs = refs[: len(arrays)] + refs[len(arrays) + len(after) :]
        split = len(arrays) + len(shapes)
        go = Mover(refs[-1])
        named = Bag([*ins, *outs], grouped(refs[:split], counts))
        named.at = position()
        kernel(named, Bag(scratch, refs[split:-1]), go)
        go.finish()

    results = pl.pallas_call(
        body,
        in_specs=specs + [TOKEN] * len(after),
        out_specs=out_specs,
        out_shape=shapes,
        scratch_shapes=[pltpu.VMEM(*s) for s in scratch.values()]
        + [pltpu.SemaphoreType.DMA((copies,))],
        compiler_params=params(held_bytes + SPARE),
        cost_estimate=cost(flops, moved),
        name=name,
    )(*arrays, *after)
    ORDER.append((results[0], next(iter(outs.values()))[2]))
    return Bag(outs, grouped(results, counts[len(ins) :]))


def aligned(start, multiple, size=None):
    return pl.ds(pl.multiple_of(start, multiple), size or multiple)


SAVED = dict(
    summed=((ROWS, D), F32),
    qc=((ROWS, D), BF),
    qp=((ROWS, D), BF),
    qs=((ROWS, D), F32),
    kv=((KEYS, 2 * D), BF),
    rel=((WIDE, D), BF),
    mix=((ROWS, D), F32),
    prob=((PAIRS, 2 * ROWS, KEYS), F32),
)
FF_STEPS = 4
FF_BLOCK = FF // FF_STEPS


def attn_forward_body(layer, r, h, saved, w, go, ready):
    mine = slice(layer, layer + 1)
    go.wait(*ready)
    projected = dot_nn(h.x[...], w.wq[...])
    saved.qc[...] = ((projected + r.bias[0, mine, :]) * SCALE).astype(BF)
    saved.qp[...] = ((projected + r.bias[1, mine, :]) * SCALE).astype(BF)
    saved.qs[...] = (projected + r.bias[2, mine, :]) * SCALE
    saved.kv[...] = dot_nn(h.joined[...], w.wkv[...]).astype(BF)
    half = r.at[0] % 2
    rows = h.table[...] if layer == 0 else r.table[aligned(HALF * (1 - half), HALF, WIDE), :]
    saved.rel[...] = dot_nn(rows, w.wr[...]).astype(BF)
    hidden, differs = sight(r.at, r.lengths, r.ranks, r.segments)
    ones = jnp.ones((WIDE, KEYS), BF)
    beside = jnp.ones((KEYS, 2 * HEAD), BF)
    for p in range(PAIRS):
        at = slice(2 * HEAD * p, 2 * HEAD * (p + 1))
        later = slice(D + 2 * HEAD * p, D + 2 * HEAD * (p + 1))
        content = dot_nt(two_heads(saved.qc[:, at]), saved.kv[:, at])
        wide = dot_nt(two_heads(saved.qp[:, at]), saved.rel[:, at])
        segment = saved.qs[:, at]
        same = dot_nn(in_two(two_heads(segment * r.seg[layer, 0:1, at])), ones)
        other = dot_nn(in_two(two_heads(segment * r.seg[layer, 1:2, at])), ones)
        raw = content + skewed_scores(wide) + jnp.where(differs, other, same)
        scores = jnp.where(hidden, NEGATIVE, raw)
        exponent = jnp.exp(scores - jnp.max(scores, axis=-1, keepdims=True))
        values = jnp.concatenate([saved.kv[:, later], beside], axis=1)
        mixed = dot_nn(exponent.astype(BF), values)
        share = 1.0 / mixed[:, 2 * HEAD :]
        saved.prob[p] = exponent * jnp.concatenate([share, share[:, : KEYS - 2 * HEAD]], axis=1)
        attended = one_pair(mixed[:, : 2 * HEAD] * share)
        saved.mix[:, at] = attended
        h.att[:, at] = attended.astype(BF)
    summed = dot_nn(h.att[...], w.wo[...]) + h.x[...].astype(F32)
    saved.summed[...] = summed
    h.y[...] = (norm_parts(summed)[0] * r.again[mine, :] + r.ashift[mine, :]).astype(BF)


def ffn_forward_body(layer, r, h, w, go, ready=()):
    mine = slice(layer, layer + 1)
    y = h.y[...]
    go.wait(*ready)
    total = None
    for c in range(FF_STEPS):
        at = slice(FF_BLOCK * c, FF_BLOCK * (c + 1))
        pre = dot_nn(y, w.win[:, at]) + r.fbin[mine, at]
        h.pre[:, at] = pre
        part = dot_nn(gelu(pre).astype(BF), w.wout[at, :])
        total = part if total is None else total + part
    summed = total + r.fbout[mine, :] + y.astype(F32)
    h.fsum[...] = summed
    return (norm_parts(summed)[0] * r.fgain[mine, :] + r.fshift[mine, :]).astype(BF)


def ffn_backward_body(layer, grad, r, h, w):
    gsum, ggain, gshift = norm_back(h.fsum[...], r.fgain[layer : layer + 1, :], grad)
    low = gsum.astype(BF)
    gbias = jnp.sum(gsum, axis=0, keepdims=True)
    vectors = [ggain, gshift, gbias]
    total = gsum
    for c in range(FF_STEPS):
        at = slice(FF_BLOCK * c, FF_BLOCK * (c + 1))
        slope = gelu_both(h.pre[:, at])[1]
        gpre = (dot_nt(low, w.wout[at, :]) * slope).astype(BF)
        vectors.append(jnp.sum(gpre.astype(F32), axis=0, keepdims=True))
        total = total + dot_nt(gpre, w.win[:, at])
    vectors = jnp.concatenate(vectors + [jnp.zeros((1, D), F32)], axis=0)
    return total.astype(BF), low, vectors


def near_weights(layer, r):
    names = [n for n in WEIGHTS if n in r.__dict__]
    return Bag(names, [r.__dict__[n].at[layer] for n in names])


WEIGHTS = dict(
    wq=((D, D), BF), wkv=((D, 2 * D), BF), wr=((D, D), BF), wo=((D, D), BF), win=((D, FF), BF),
    wout=((FF, D), BF),
)
FORWARD_SCRATCH = dict(
    x=((ROWS, D), BF),
    joined=((KEYS, D), BF),
    att=((ROWS, D), BF),
    y=((ROWS, D), BF),
    pre=((ROWS, FF), F32),
    fsum=((ROWS, D), F32),
)


def forward_first_kernel(r, h, go):
    section = r.at[0]
    seq, half = section // 2, section % 2
    own = aligned(section * HALF, HALF)
    ready = [
        go(r.content.at[own], h.x.at[pl.ds(0, HALF)]),
        go(r.query.at[own], h.x.at[pl.ds(HALF, HALF)]),
        go(r.memory.at[0, aligned(seq * M, M)], h.joined.at[pl.ds(0, M)]),
        go(r.content.at[aligned(seq * S, S)], h.joined.at[pl.ds(M, S)]),
        go(r.table.at[aligned(HALF * (1 - half), HALF, WIDE)], h.table),
        go(r.wq.at[0], h.wq),
        go(r.wkv.at[0], h.wkv),
        go(r.wr.at[0], h.wr),
        go(r.wo.at[0], h.wo),
    ]
    later = [go(r.win.at[0], h.win), go(r.wout.at[0], h.wout)]
    attn_forward_body(0, r, h, h, h, go, ready)
    for n in SAVED:
        go(h.__dict__[n], r.__dict__[n])
    r.acts[:ROWS, :] = h.att[...]
    x = ffn_forward_body(0, r, h, h, go, later)
    go(h.pre, r.pre0)
    go(h.fsum, r.fsum0)
    r.acts[ROWS:, :] = x
    r.half[...] = x[:HALF]


def forward_second_kernel(r, h, go):
    section = r.at[0]
    seq, half = section // 2, section % 2
    own = aligned(section * HALF, HALF)
    w = near_weights(1, r)
    ready = [
        go(r.memory.at[1, aligned(seq * M, M)], h.joined.at[pl.ds(0, M)]),
        go(r.cotc.at[own], h.grad.at[pl.ds(0, HALF)]),
        go(r.cotq.at[own], h.grad.at[pl.ds(HALF, HALF)]),
    ]
    h.x[...] = r.acts0[ROWS:, :]
    h.joined[aligned(M + HALF * half, HALF), :] = r.acts0[ROWS : ROWS + HALF, :]
    h.joined[aligned(M + HALF * (1 - half), HALF), :] = r.other[...]
    attn_forward_body(1, r, h, r, w, go, ready)
    r.acts[:ROWS, :] = h.att[...]
    r.out[...] = ffn_forward_body(1, r, h, w, go)
    gy, low, vectors = ffn_backward_body(1, h.grad[...].astype(F32), r, h, w)
    r.acts[ROWS:, :] = low
    r.gy[...] = gy
    r.fvec[...] = vectors


def ffn_backward_kernel(r, h, go):
    go(r.fsum0, h.fsum)
    go(r.pre0, h.pre)
    w = near_weights(0, r)
    gx = r.gx
    grad = jnp.concatenate([gx[:HALF, :] + r.other[...].astype(F32), gx[HALF:, :]], axis=0)
    go.finish()
    gy, low, vectors = ffn_backward_body(0, grad.astype(BF).astype(F32), r, h, w)
    r.low[...] = low
    r.gy[...] = gy
    r.fvec[...] = vectors


def attn_backward_kernel(layer, r, h, go):
    section = r.at[0]
    half = section % 2
    mine = slice(layer, layer + 1)
    w = near_weights(layer, r)
    if layer == 0:
        loads = [go(r.__dict__[n], h.__dict__[n]) for n in SAVED]
        go.wait(loads[0])
    k = h if layer == 0 else r
    gsum, ggain, gshift = norm_back(k.summed[...], r.again[mine, :], r.gy[...].astype(F32))
    low = gsum.astype(BF)
    h.vec[0:1, :] = ggain
    h.vec[1:2, :] = gshift
    h.vec[7:15, :] = r.fvec[...]
    h.vec[15:16, :] = jnp.zeros((1, D), F32)
    g_attended = dot_nt(low, w.wo[...]).astype(BF)
    go.finish()
    differs = sight(r.at, r.lengths, r.ranks, r.segments)[1]
    lowest = low_lanes()
    ones = jnp.ones((WIDE, KEYS), BF)
    for p in range(PAIRS):
        at = slice(2 * HEAD * p, 2 * HEAD * (p + 1))
        later = slice(D + 2 * HEAD * p, D + 2 * HEAD * (p + 1))
        prob = k.prob[p]
        ga = two_heads(g_attended[:, at])
        gprob = dot_nt(ga, k.kv[:, later])
        h.gkv[later, :] = dot_nn(ga.T, prob.astype(BF)).astype(BF)
        centre = dot_nn(in_two(two_heads(g_attended[:, at].astype(F32) * k.mix[:, at])), ones)
        gscores = (prob * (gprob - centre)).astype(BF)
        gqc = one_pair(dot_nn(gscores, k.kv[:, at]))
        h.gkv[at, :] = dot_nn(two_heads(k.qc[:, at]).T, gscores).astype(BF)
        gwhole = gscores.astype(F32)
        gwide = unskewed_scores(gwhole).astype(BF)
        gqp = one_pair(dot_nn(gwide, k.rel[:, at]))
        h.grel[at, :] = dot_nn(two_heads(k.qp[:, at]).T, gwide)
        other_part = jnp.where(differs, gwhole, 0.0)
        other = jnp.sum(other_part, axis=-1, keepdims=True)
        same = jnp.sum(gwhole - other_part, axis=-1, keepdims=True)
        same_pair = jnp.where(lowest, same[:ROWS], same[ROWS:])
        other_pair = jnp.where(lowest, other[:ROWS], other[ROWS:])
        gqs = same_pair * r.seg[layer, 0:1, at] + other_pair * r.seg[layer, 1:2, at]
        segment = k.qs[:, at]
        h.vec[2:3, at] = jnp.sum(gqc, axis=0, keepdims=True) * SCALE
        h.vec[3:4, at] = jnp.sum(gqp, axis=0, keepdims=True) * SCALE
        h.vec[4:5, at] = jnp.sum(gqs, axis=0, keepdims=True) * SCALE
        h.vec[5:6, at] = jnp.sum(same_pair * segment, axis=0, keepdims=True)
        h.vec[6:7, at] = jnp.sum(other_pair * segment, axis=0, keepdims=True)
        h.turned[at, :ROWS] = low[:, at].astype(F32).T
        h.turned[at, ROWS:] = ((gqc + gqp + gqs) * SCALE).T
    few, step = KEYS - 128, D // 8
    for n, message in enumerate(r.first):
        d = section ^ n

        def chosen(ref, size, multiple):
            starts = [4 * size * e + size * d for e in range(8)]
            return jnp.concatenate([ref[aligned(m, multiple, size), :] for m in starts], axis=0)

        message[:SHARE, :256] = chosen(h.turned, step // 4, 8).astype(BF)
        message[:SHARE, 256:512] = chosen(h.grel, step // 4, 8).astype(BF)
        keyval = chosen(h.gkv, step // 2, 16)
        for j in range(2):
            rows = keyval[SHARE * j : SHARE * (j + 1)]
            message[:SHARE, 512 + 128 * j : 640 + 128 * j] = rows[:, :128]
            message[:SHARE, 768 + few * j : 768 + few * (j + 1)] = rows[:, 128:]
    joined = dot_nn(w.wkv[...], h.gkv[...])
    one, two = joined[:, M : M + HALF], joined[:, M + HALF :]
    first_half = jnp.zeros((1, 1), jnp.int32) + half == 0
    own, partner = jnp.where(first_half, one, two), jnp.where(first_half, two, one)
    gx = dot_nn(w.wq[...], h.turned[:, ROWS:].astype(BF)) + gsum.T
    gx = jnp.concatenate([gx[:, :HALF] + own, gx[:, HALF:]], axis=1)
    if layer > 0:
        r.send[...] = partner.T.astype(BF)
        r.gx[...] = gx.T
        r.second[:, : 2 * HALF] = r.out[...].T
        r.second[:, 2 * HALF :] = jnp.concatenate([partner, joined[:, :M]], axis=1).astype(BF)
        r.vec[...] = h.vec[...]
    else:
        h.second[:, : 2 * HALF] = gx.astype(BF)
        h.second[:, 2 * HALF : WIDE] = jnp.concatenate([partner, joined[:, :M]], axis=1).astype(BF)
        h.second[:, WIDE:] = r.later[...]
        for d in range(4):
            at = slice(SHARE * d, SHARE * (d + 1))
            for n, vec in enumerate((h.vec, r.vectors)):
                place = slice(SHARE * n, SHARE * (n + 1))
                wide = vec[10 + d : 11 + d, :]
                rows = [vec[:10, at]] + [wide[:, SHARE * j : SHARE * (j + 1)] for j in range(4)]
                rows = jnp.concatenate(rows + [jnp.zeros((2, SHARE), F32)], axis=0)
                h.parts[d, :, place] = rows.astype(BF)
        for n, message in enumerate(r.second):
            message[...] = h.second[aligned(SHARE * (section ^ n), SHARE), :]
        for n, message in enumerate(r.first):
            message[SHARE:, : 2 * SHARE] = h.parts[section ^ n]


def gathered_x(layer, r, h):
    for n in range(4):
        if layer == 0:
            rows = aligned((r.at[0] ^ n) * HALF, HALF)
            h.x[ROWS * n : ROWS * n + HALF, :] = r.content[rows, :]
            h.x[ROWS * n + HALF : ROWS * (n + 1), :] = r.query[rows, :]
        else:
            h.x[ROWS * n : ROWS * (n + 1), :] = r.before[n][ROWS:, :]


def put_halves(r, h):
    core = r.at[2]
    for j in range(4):
        r.kept[j] = h.pieces[2 * j + core]
        for part, given in enumerate(r.given):
            n = given.shape[1]
            given[j] = h.pieces[2 * j + 1 - core, n * part : n * (part + 1), :]


def shares_kernel(layer, r, h, go):
    wide, few = FF // 8, FF // 32
    for t in range(4):

        @pl.when(r.at[0] == t)
        def _():
            for d in range(8):
                at = slice(few * d, few * (d + 1))
                held = slice(wide * d + few * t, wide * d + few * (t + 1))
                r.bias[:, at] = r.fbin[layer : layer + 1, held]
                r.inner[:, at] = r.win[layer, :, held]
                r.outer[at, :] = r.wout[layer, held, :]


def ffn_weights_kernel(layer, fast, r, h, go):
    mine = slice(layer, layer + 1)
    gathered_x(layer, r, h)
    attended = jnp.concatenate([a[:ROWS, :] for a in r.acts], axis=0)
    summed = dot_nn(attended, r.wo[layer]) + h.x[...].astype(F32)
    y = norm_parts(summed)[0] * r.again[mine, :] + r.ashift[mine, :]
    h.y[...] = y.astype(BF)
    for n, low in enumerate(r.low):
        rows = low[low.shape[0] - ROWS :, :]
        h.low[ROWS * n : ROWS * (n + 1), :] = rows
        h.lowt[:, ROWS * n : ROWS * (n + 1)] = rows.T
    width, few = FF // 8, FF // 32
    for t in range(2):
        at = slice(width * t, width * (t + 1))
        pre = dot_nn(h.y[...], r.inner[:, at]) + r.bias[:, at]
        active, slope = gelu_both(pre)
        gpre = (dot_nt(h.low[...], r.outer[at, :]) * slope).astype(BF)
        grad_in = dot_nn(gpre.T, h.y[...]).astype(BF)
        grad_out = dot_nn(h.lowt[...], active.astype(BF)).astype(BF)
        if fast:
            for d in range(4):
                h.pieces[4 * t + d, :few, :] = grad_in[few * d : few * (d + 1), :]
            for d in range(8):
                h.pieces[d, few:, at] = grad_out[few * d : few * (d + 1), :]
        else:
            r.grads[0][at, :] = grad_in
            r.grads[1][:, at] = grad_out
    if fast:
        put_halves(r, h)


def attn_weights_kernel(fast, r, h, go):
    parts = []
    for layer in range(LAYERS):
        grads = attn_grads(layer, r, h)
        if fast:
            for n, grad in enumerate(grads):
                h.grads[layer, SHARE * n : SHARE * n + grad.shape[0], :] = grad
        else:
            for n, grad in enumerate(grads):
                r.grads[4 * layer + n][...] = grad.astype(BF)
    vectors = None
    for f in r.first:
        part = f[SHARE : SHARE + 16, : 2 * SHARE].astype(F32)
        vectors = part if vectors is None else vectors + part
    if not fast:
        r.vectors[...] = vectors
        return
    vectors = jnp.concatenate([vectors[:8], vectors[8:]], axis=1)
    step = D // 8
    for d in range(8):
        rows = []
        for layer in range(LAYERS):
            for n in range(4):
                size = step // 2 if n == 3 else step // 4
                start = SHARE * n + size * d
                rows.append(h.grads[layer, start : start + size, :])
        rows = jnp.concatenate(rows + [vectors, jnp.zeros_like(vectors)], axis=0)
        h.pieces[d] = rows.astype(BF)
    put_halves(r, h)


def attn_grads(layer, r, h):
    section = r.at[0]
    half = section % 2
    first = [f.at[pl.ds(0, SHARE)] for f in (r.first, r.earlier)[layer]]
    gathered_x(layer, r, h)
    for pair in range(2):
        rows = aligned((section ^ (2 * pair)) // 2 * M, M)
        h.joined[pair, :M, :] = r.memory[layer, rows, :]
        for n in (2 * pair, 2 * pair + 1):
            place = half ^ (n & 1)
            h.joined[pair, aligned(M + HALF * place, HALF), :] = h.x[ROWS * n : ROWS * n + HALF, :]
    low = jnp.concatenate([f[:, :128] for f in first], axis=1)
    proj = jnp.concatenate([f[:, 128:256] for f in first], axis=1)
    grad_q = dot_nn(proj, h.x[...])
    attended = jnp.concatenate([a[:ROWS, :] for a in (r.acts0, r.acts1)[layer]], axis=0)
    grad_o = dot_nn(low, attended)
    few = KEYS - 128
    grad_kv = grad_rel = None
    for pair in range(2):
        both = add(first[2 * pair][:, 512:], first[2 * pair + 1][:, 512:])
        both = jnp.concatenate(
            [
                jnp.concatenate([both[:, :128], both[:, 256 : 256 + few]], axis=1),
                jnp.concatenate([both[:, 128:256], both[:, 256 + few :]], axis=1),
            ],
            axis=0,
        )
        part = dot_nn(both, h.joined[pair])
        grad_kv = part if grad_kv is None else grad_kv + part
    for n in range(2):
        place = half ^ n
        total = add(first[n][:, 256:512], first[n + 2][:, 256:512])
        rows = r.table[aligned(HALF * (1 - place), HALF, WIDE), :]
        part = dot_nn(total, rows)
        grad_rel = part if grad_rel is None else grad_rel + part
    return grad_q, grad_o, grad_rel, grad_kv


def add(a, b):
    return (a.astype(F32) + b.astype(F32)).astype(BF)


def whole(shape):
    return pl.BlockSpec(shape, lambda i: (0,) * len(shape))


def gather_kernel(*refs):
    section = position()[0]
    start = refs[0].shape[1] - 2 * WIDE
    early = [r.at[:, pl.ds(start, WIDE)] for r in refs[:4]]
    late = [r.at[:, pl.ds(start + WIDE, WIDE)] for r in refs[:4]]
    small_ref = refs[4]
    outc_ref, outq_ref, gradc_ref, gradq_ref, mem_ref = refs[5:10]
    bias_ref, seg_ref, again_ref, ashift_ref, inb_ref, outb_ref, fgain_ref, fshift_ref = refs[10:18]

    def in_order(blocks):
        odd = jnp.zeros((1, 1), jnp.int32) + section % 2 == 1
        high = jnp.zeros((1, 1), jnp.int32) + section // 2 == 1
        a, b, c, d = blocks
        a, b, c, d = (
            jnp.where(odd, b, a), jnp.where(odd, a, b), jnp.where(odd, d, c), jnp.where(odd, c, d)
        )
        left, right = jnp.concatenate([a, b], axis=1), jnp.concatenate([c, d], axis=1)
        return jnp.concatenate([jnp.where(high, right, left), jnp.where(high, left, right)], axis=1)

    def blocks(four, start):
        return [f[:, start : start + HALF].astype(F32) for f in four]

    outc_ref[...] = in_order(blocks(late, 0)).astype(BF)
    outq_ref[...] = in_order(blocks(late, HALF)).astype(BF)
    own, passed = blocks(early, 0), blocks(early, 2 * HALF)
    gradc_ref[...] = in_order([own[k] + passed[k ^ 1] for k in range(4)])
    gradq_ref[...] = in_order(blocks(early, HALF))
    high = jnp.zeros((1, 1), jnp.int32) + section // 2 == 1
    for layer, four in ((0, early), (1, late)):
        a, b, c, d = blocks(four, 3 * HALF)
        one, two = a + b, c + d
        mem_ref[layer] = jnp.concatenate(
            [jnp.where(high, two, one), jnp.where(high, one, two)], axis=1
        )
    for layer in range(LAYERS):
        mine = slice(layer, layer + 1)

        held = slice(SHARE * layer, SHARE * (layer + 1))

        def vector(row):
            return small_ref[row : row + 1, held].astype(F32)

        for j in range(3):
            bias_ref[j, mine, :] = vector(2 + j)
        for j in range(2):
            seg_ref[layer, j : j + 1, :] = vector(5 + j)
        again_ref[mine, :] = vector(0)
        ashift_ref[mine, :] = vector(1)
        fgain_ref[mine, :] = vector(7)
        fshift_ref[mine, :] = vector(8)
        outb_ref[mine, :] = vector(9)
        for j in range(4):
            inb_ref[mine, SHARE * j : SHARE * (j + 1)] = vector(10 + j)


def gather_rows(at, rows_out, small):
    rows = 4 * HALF
    vector = ((LAYERS, SHARE), F32)
    shapes = [
        ((SHARE, rows), BF),
        ((SHARE, rows), BF),
        ((SHARE, rows), F32),
        ((SHARE, rows), F32),
        ((LAYERS, SHARE, 2 * M), F32),
        ((3, LAYERS, SHARE), F32),
        ((LAYERS, 2, SHARE), F32),
        vector,
        vector,
        ((LAYERS, FF // 4), F32),
        vector,
        vector,
        vector,
    ]
    return pl.pallas_call(
        gather_kernel,
        grid=(1,),
        in_specs=[whole(a.shape) for a in (*rows_out, small)],
        out_specs=[whole(s) for s, _ in shapes],
        out_shape=[jax.ShapeDtypeStruct(s, t) for s, t in shapes],
        compiler_params=params(),
        cost_estimate=cost(1_000_000, 2_000_000),
        name="gather_rows",
    )(*rows_out, small)


def final_ffn_kernel(r, h, go):
    few = FF // 32
    for n, message in enumerate(r.ffn):
        h.got[r.at[0] ^ n] = message[...].astype(F32)
    for layer in range(LAYERS):
        rows_at = slice(few * layer, few * (layer + 1))
        for s in range(4):
            held = slice(few * s, few * (s + 1))
            r.fin[layer, :, held] = h.got[s, rows_at, :SHARE].T
            for e in range(2):
                place = slice(FF // 8 * e + few * s, FF // 8 * e + few * (s + 1))
                start = SHARE + few * e
                r.fout[layer, :, place] = h.got[s, rows_at, start : start + few]


def final_attn_kernel(r, h, go):
    for n, message in enumerate(r.attn):
        h.attn[r.at[0] ^ n] = message[...].astype(F32)
    step = D // 8
    for layer in range(LAYERS):
        lanes = slice(SHARE * layer, SHARE * (layer + 1))
        start = 0
        for made, size in ((r.q, step // 4), (r.o, step // 4), (r.rel, step // 4), (r.kv, step // 2)):
            blocks = [h.attn[s, start : start + size, lanes] for s in range(4)]
            made[layer] = jnp.concatenate(blocks, axis=0).T
            start += size


def final_ffn(at, ffn):
    return run(
        final_ffn_kernel,
        "final_ffn",
        dict(at=(at, HERE), ffn=(ffn, NEAR)),
        dict(
            fin=((LAYERS, SHARE, FF // 8), F32, SMALL),
            fout=((LAYERS, D // 8, FF // 4), F32, SMALL),
        ),
        dict(got=((4, FF // 16, 2 * SHARE), F32)),
    )


def final_attn(at, attn):
    half = ((LAYERS, SHARE, SHARE // 2), F32, SMALL)
    return run(
        final_attn_kernel,
        "final_attn",
        dict(at=(at, HERE), attn=(attn, NEAR)),
        dict(q=half, kv=((LAYERS, SHARE, SHARE), F32, SMALL), o=half, rel=half),
        dict(attn=((4, ROWS_ATTN + 8, 2 * SHARE), F32)),
    )


def split_kernel(r, h, go):
    chip = r.at[1]
    for part, got in enumerate(r.got):
        n = got.shape[1]
        rows = pl.ds(n * part, n)
        for m, p in enumerate((chip, chip ^ 2)):
            r.keep[m, rows, :] = add(r.kept[p, rows, :], got[p])
        place, put = n * part, 0
        while place >= r.send[put].shape[1]:
            place, put = place - r.send[put].shape[1], put + 1
        for m, p in enumerate((chip ^ 1, chip ^ 3)):
            r.send[put][m, pl.ds(place, n), :] = add(r.kept[p, rows, :], got[p])


def fold_kernel(start, r, h, go):
    rows = pl.ds(start, r.got.shape[1])
    r.own[...], r.far[...] = [add(r.keep[m, rows, :], r.got[m]) for m in range(2)]


def sum_kernel(r, h, go):
    r.total[...] = add(r.own[...], r.got[...])


def shared_attn_kernel(r, h, go):
    total = [own[...].astype(F32) + got[...].astype(F32) for own, got in zip(r.own, r.got)]
    total = jnp.concatenate(total, axis=0)
    layers = [total[ROWS_ATTN * n : ROWS_ATTN * (n + 1)] for n in range(LAYERS)]
    for t in range(4):
        at = slice(SHARE * t, SHARE * (t + 1))
        rows = jnp.concatenate([m[:, at] for m in layers], axis=1)
        h.parts[t] = jnp.concatenate([rows, jnp.zeros((8, 2 * SHARE), F32)], axis=0).astype(BF)
    for n, part in enumerate(r.parts):
        part[...] = h.parts[r.at[0] ^ n]
    vectors = total[LAYERS * ROWS_ATTN : LAYERS * ROWS_ATTN + 8]
    r.vectors[...] = jnp.concatenate([vectors[:, : 2 * SHARE], vectors[:, 2 * SHARE :]], axis=0)


def shared_kernel(r, h, go):
    few = FF // 32
    for layer, total in enumerate((add(r.own[...], r.got[...]), r.later[...])):
        rows = slice(few * layer, few * (layer + 1))
        for t in range(4):
            at = slice(SHARE * t, SHARE * (t + 1))
            h.parts[t, rows, :SHARE], h.parts[t, rows, SHARE:] = total[:few, at], total[few:, at]
    for n, part in enumerate(r.parts):
        part[...] = h.parts[r.at[0] ^ n]


def split_pieces(at, made, cuts=(), after=()):
    got = [swapped(a, DP, 1) for a in made.given]
    shape = (2,) + made.kept.shape[1:]
    ins = dict(at=(at, HERE), kept=(made.kept, NEAR), got=(got, NEAR))
    parts = [(2, n, shape[2]) for n in cuts or shape[1:2]]
    return run(
        split_kernel, "split_pieces", ins, dict(keep=(shape, BF, NEAR), send=(parts, BF, NEAR)), {},
        after=after,
    )


def fold_pieces(split, part=0, after=()):
    got = swapped(split.send[part], DP, 2)
    start = sum(a.shape[1] for a in split.send[:part])
    ins = dict(keep=(split.keep, NEAR), got=(got, NEAR))
    shape = got.shape[1:]
    folded = run(
        functools.partial(fold_kernel, start), "fold_pieces", ins,
        dict(own=(shape, BF, NEAR), far=(shape, BF, NEAR)), {}, after=after,
    )
    return folded.own, swapped(folded.far, DP, 4)


def sum_pieces(folded, after=()):
    own, got = folded
    ins = dict(own=(own, NEAR), got=(got, NEAR))
    return run(
        sum_kernel, "sum_pieces", ins, dict(total=(got.shape, BF, NEAR)), {}, after=after
    ).total


def shared_attn(at, folded, after=()):
    ins = dict(
        at=(at, HERE), own=([f[0] for f in folded], NEAR), got=([f[1] for f in folded], NEAR)
    )
    shape = (ROWS_ATTN + 8, 2 * SHARE)
    return run(
        shared_attn_kernel, "shared_attn", ins,
        dict(parts=([shape] * 4, BF, NEAR), vectors=((16, 2 * SHARE), F32, NEAR)),
        dict(parts=((4,) + shape, BF)), after=after,
    )


def shared_pieces(at, folded, later, after=()):
    own, got = folded
    ins = dict(
        at=(at, HERE), own=(own, NEAR), got=(got, NEAR), later=(later, NEAR)
    )
    shape = (FF // 16, 2 * SHARE)
    return run(
        shared_kernel, "shared_pieces", ins,
        dict(parts=([shape] * 4, BF, NEAR)),
        dict(parts=((4,) + shape, BF)), after=after,
    ).parts


def swapped(x, axis, k):
    return lax.ppermute(x, axis, [(i, i ^ k) for i in range(lax.axis_size(axis))])


def from_all(x):
    return [x] + [swapped(x, SECTION, k) for k in (1, 2, 3)]


def messages(parts):
    return [parts[0]] + [swapped(parts[k], SECTION, k) for k in (1, 2, 3)]


def on_device(
    content_in,
    query_in,
    memory,
    doc_lengths,
    perm_rank,
    segment_ids,
    w_query,
    w_keyval,
    w_out,
    w_rel,
    head_bias,
    seg_embed,
    attn_gain,
    attn_shift,
    ffn_in,
    ffn_in_bias,
    ffn_out,
    ffn_out_bias,
    ffn_gain,
    ffn_shift,
    cot_content,
    cot_query,
):
    ORDER.clear()
    dp = lax.axis_size(DP)
    fast = dp == 8
    at = None
    table = position_table()
    marks = dict(
        at=(at, HERE),
        lengths=(doc_lengths.reshape(1, -1), SMALL),
        ranks=(perm_rank, SMALL),
        segments=(segment_ids, SMALL),
    )
    attn_v = dict(
        bias=(head_bias.transpose(1, 0, 2), SMALL),
        seg=(seg_embed, SMALL),
        again=(attn_gain, SMALL),
        ashift=(attn_shift, SMALL),
    )
    ffn_v = dict(
        fbin=(ffn_in_bias, SMALL),
        fbout=(ffn_out_bias, SMALL),
        fgain=(ffn_gain, SMALL),
        fshift=(ffn_shift, SMALL),
    )
    matrices = dict(
        wq=w_query, wkv=w_keyval, wr=w_rel, wo=w_out, win=ffn_in, wout=ffn_out,
    )
    near = {n: (a, NEAR) for n, a in matrices.items()}

    def of(which, *names):
        return {n: which[n] for n in which if n in names}

    first = run(
        forward_first_kernel,
        "forward_first",
        dict(
            **marks,
            content=(content_in, FAR),
            query=(query_in, FAR),
            memory=(memory, FAR),
            table=(table, FAR),
            **{n: (a, FAR) for n, a in matrices.items()},
            **attn_v,
            **ffn_v,
        ),
        dict(
            acts=((2 * ROWS, D), BF, NEAR),
            half=((HALF, D), BF, NEAR),
            pre0=((ROWS, FF), F32, FAR),
            fsum0=((ROWS, D), F32, FAR),
            **{n: (*s, FAR) for n, s in SAVED.items()},
        ),
        dict(**FORWARD_SCRATCH, table=((WIDE, D), BF), **WEIGHTS, **SAVED),
        copies=24,
        flops=2_400_000_000,
        moved=16_000_000,
    )
    marks, attn_v, ffn_v = (
        {n: (a, NEAR if place is SMALL else place) for n, (a, place) in group.items()}
        for group in (marks, attn_v, ffn_v)
    )
    other = swapped(first.half, SECTION, 1)
    acts0 = from_all(first.acts)
    second = run(
        forward_second_kernel,
        "forward_second",
        dict(
            **marks,
            acts0=(first.acts, NEAR),
            other=(other, NEAR),
            memory=(memory, FAR),
            table=(table, NEAR),
            cotc=(cot_content, FAR),
            cotq=(cot_query, FAR),
            **near,
            **attn_v,
            **ffn_v,
        ),
        dict(
            acts=((2 * ROWS, D), BF, NEAR),
            out=((ROWS, D), BF, NEAR),
            gy=((ROWS, D), BF, NEAR),
            fvec=((8, D), F32, NEAR),
            **{n: (*s, NEAR) for n, s in SAVED.items()},
        ),
        dict(**FORWARD_SCRATCH, grad=((ROWS, D), BF)),
        copies=4,
        flops=3_600_000_000,
        moved=16_000_000,
    )
    acts1 = from_all(second.acts)

    def attn_backward(layer, saved, gy, fvec, after=(), **extra):
        ins = dict(
            **marks,
            gy=(gy, NEAR),
            fvec=(fvec, NEAR),
            **{n: (saved.__dict__[n], FAR if layer == 0 else NEAR) for n in SAVED},
            **{n: near[n] for n in list(WEIGHTS)[:4] if n != list(WEIGHTS)[2]},
            **attn_v,
            **{n: (a, NEAR) for n, a in extra.items()},
        )
        scratch = dict(
            vec=((16, D), F32),
            turned=((D, 2 * ROWS), F32),
            gkv=((2 * D, KEYS), BF),
            grel=((D, WIDE), F32),
        )
        rows = FIRST[0] if layer else FIRST[0] + 16
        outs = dict(first=([(rows, FIRST[1])] * 4, BF, NEAR))
        if layer == 0:
            outs.update(second=([SECOND] * 4, BF, NEAR))
            scratch.update(SAVED, second=((D, 2 * WIDE), BF), parts=((4, 16, 2 * SHARE), BF))
        else:
            outs.update(
                second=((D, WIDE), BF, NEAR),
                gx=((ROWS, D), F32, NEAR),
                send=((HALF, D), BF, NEAR),
                vec=((16, D), F32, NEAR),
            )
        return run(
            functools.partial(attn_backward_kernel, layer), "attn_backward", ins, outs, scratch,
            copies=10, flops=1000, moved=1000, after=after,
        )

    def inputs_of(layer):
        if layer == 0:
            return dict(content=(content_in, NEAR), query=(query_in, NEAR))
        return dict(before=(acts0, NEAR))

    def grads_of(shape, plain, cuts=2):
        if fast:
            parts = [(4, shape[0] // cuts, shape[1])] * cuts
            return dict(kept=((4,) + shape, BF, NEAR), given=(parts, BF, NEAR))
        return dict(grads=(plain, BF, SMALL))

    def shares_of(layer):
        return run(
            functools.partial(shares_kernel, layer),
            "shares",
            dict(at=marks["at"], **of(near, "win", "wout"), **of(ffn_v, "fbin")),
            dict(
                inner=((D, D), BF, NEAR),
                outer=((D, D), BF, NEAR),
                bias=((1, D), F32, NEAR),
            ),
            {},
        )

    def ffn_weights(layer, shares, acts, lows, after=()):
        ins = dict(
            at=marks["at"],
            **inputs_of(layer),
            **of(near, "wo"),
            **of(attn_v, "again", "ashift"),
            inner=(shares.inner, NEAR),
            outer=(shares.outer, NEAR),
            bias=(shares.bias, NEAR),
            acts=(acts, NEAR),
            low=(lows, NEAR),
        )
        shape = (ROWS_FFN, D)
        tall = ((4 * ROWS, D), BF)
        return run(
            functools.partial(ffn_weights_kernel, layer, fast),
            "ffn_weights",
            ins,
            grads_of(shape, [(D, D), (D, D)]),
            dict(x=tall, y=tall, low=tall, lowt=((D, 4 * ROWS), BF), pieces=((8,) + shape, BF)),
            flops=1000,
            moved=1000,
            after=after,
        )

    def attn_weights(notes, earlier, after=()):
        ins = dict(
            at=marks["at"],
            content=(content_in, NEAR),
            query=(query_in, NEAR),
            before=(acts0, NEAR),
            memory=(memory, NEAR),
            table=(table, NEAR),
            acts0=(acts0, NEAR),
            acts1=(acts1, NEAR),
            first=(notes, NEAR),
            earlier=(earlier, NEAR),
        )
        shape = (2 * ROWS_ATTN + 2 * ROWS_VEC, D)
        outs = grads_of(shape, [(SHARE, D), (SHARE, D), (SHARE, D), (2 * SHARE, D)] * 2, 4)
        if not fast:
            outs.update(vectors=((2 * ROWS_VEC, 2 * SHARE), F32, SMALL))
        return run(
            functools.partial(attn_weights_kernel, fast),
            "attn_weights",
            ins,
            outs,
            dict(
                x=((4 * ROWS, D), BF),
                joined=((2, KEYS, D), BF),
                grads=((LAYERS, 5 * SHARE, D), F32),
                pieces=((8,) + shape, BF),
            ),
            flops=10**12,
            moved=10**9,
            after=after,
        )

    back1 = attn_backward(1, second, second.gy, second.fvec, acts0[1:], out=second.out)
    received = swapped(back1.send, SECTION, 1)
    parts1 = messages(back1.first)
    shares1, shares0 = shares_of(1), shares_of(0)
    fgrads1 = ffn_weights(1, shares1, acts1, acts1)
    third = run(
        ffn_backward_kernel,
        "ffn_backward",
        dict(
            gx=(back1.gx, NEAR),
            other=(received, NEAR),
            fsum0=(first.fsum0, FAR),
            pre0=(first.pre0, FAR),
            **of(near, "win", "wout"),
            **of(ffn_v, "fgain"),
        ),
        dict(
            low=((ROWS, D), BF, NEAR), gy=((ROWS, D), BF, NEAR), fvec=((8, D), F32, NEAR)
        ),
        dict(fsum=((ROWS, D), F32), pre=((ROWS, FF), F32)),
        copies=4,
        flops=10**12,
        moved=10**9,
    )
    lows0 = from_all(third.low)
    if fast:
        split_f1 = split_pieces(at, fgrads1, after=parts1[1:])
    back0 = attn_backward(
        0, first, third.gy, third.fvec, later=back1.second, vectors=back1.vec
    )
    parts0 = messages(back0.first)
    rows_out = back0.second
    fgrads0 = ffn_weights(0, shares0, acts0, lows0)
    if fast:
        fold_f1 = fold_pieces(split_f1)
        split_f0 = split_pieces(at, fgrads0)
    agrads = attn_weights(parts0, parts1)
    if fast:
        sum_f1 = sum_pieces(fold_f1)
        fold_f0 = fold_pieces(split_f0)
        split_a = split_pieces(at, agrads, (192, 64))
        folded = [fold_pieces(split_a, 0)]
        rows_all = messages(rows_out)
        ffn = messages(shared_pieces(at, fold_f0, sum_f1, rows_all[1:]))
        folded.append(fold_pieces(split_a, 1))
        made = final_ffn(at, ffn)
        fin, fout = made.fin, made.fout
        shared_a = shared_attn(at, folded)
        attn_all = messages(shared_a.parts)
        outs = gather_rows(at, rows_all, shared_a.vectors)
        made = final_attn(at, attn_all)
        wq, wkv, wo, wr = made.q, made.kv, made.o, made.rel
        fout = fout.transpose(0, 2, 1)
    else:
        outs = gather_rows(at, messages(rows_out), lax.psum(agrads.vectors, DP))
        section = lax.axis_index(SECTION)

        def owned(rows):
            part = rows.reshape((dp, -1) + rows.shape[1:])
            part = lax.psum_scatter(part, DP, scatter_dimension=0, tiled=False)
            part = lax.psum(part, SECTION)
            width = part.shape[1] // 4
            return lax.dynamic_slice_in_dim(part, section * width, width, 1).astype(F32).T

        def at_share(share, count, axis=0):
            cut = share.reshape(share.shape[:axis] + (count, 1, -1) + share.shape[axis + 1 :])
            full = jnp.zeros(cut.shape[: axis + 1] + (4,) + cut.shape[axis + 2 :], BF)
            full = lax.dynamic_update_slice_in_dim(full, cut, section, axis + 1)
            return full.reshape(share.shape[:axis] + (-1,) + share.shape[axis + 1 :])

        def plain(fgrads, agrads):
            parts = [at_share(a, 8) for a in agrads]
            parts += [at_share(fgrads[0], 8), at_share(fgrads[1], 8, 1)]
            q, o, rel, kv, fin, fout = [owned(a) for a in parts]
            return q, kv, o, rel, fin, fout

        pairs = zip(plain(fgrads0.grads, agrads.grads[:4]), plain(fgrads1.grads, agrads.grads[4:]))
        wq, wkv, wo, wr, fin, fout = [jnp.stack(p) for p in pairs]
    return (
        outs[0].T,
        outs[1].T,
        outs[2].T,
        outs[3].T,
        outs[4].transpose(0, 2, 1),
        wq,
        wkv,
        wo,
        wr,
        outs[5].transpose(1, 0, 2),
        outs[6],
        outs[7],
        outs[8],
        fin,
        outs[9],
        fout,
        outs[10],
        outs[11],
        outs[12],
    )


def solution(mesh):
    in_specs = (
        P(DP, None),
        P(DP, None),
        P(None, DP, None),
        P(DP),
        P(DP, None),
        P(DP, None),
    ) + (P(),) * 14 + (P(DP, None), P(DP, None))
    weight, vector = P(None, SECTION, DP), P(None, SECTION)
    out_specs = (
        P(DP, SECTION),
        P(DP, SECTION),
        P(DP, SECTION),
        P(DP, SECTION),
        P(None, DP, SECTION),
        weight,
        weight,
        weight,
        weight,
        P(None, None, SECTION),
        P(None, None, SECTION),
        vector,
        vector,
        weight,
        vector,
        weight,
        vector,
        vector,
        vector,
    )
    return jax.shard_map(
        on_device, mesh=mesh, in_specs=in_specs, out_specs=out_specs, check_vma=False
    )
```

```python
import functools
import math

import jax
import jax.numpy as jnp
import numpy as np
from jax import lax
from jax.experimental import pallas as pl
from jax.experimental.pallas import tpu as pltpu
from jax.sharding import PartitionSpec as P

D = 768
HEADS = 12
HEAD = 64
FF = 3072
S = 128
M = 64
LAYERS = 2
HALF = S // 2
KEYS = M + S
TABLE = M + 2 * S - 1
WIDE = 256
ROWS = 2 * HALF
PAIRS = HEADS // 2
SHARE = D // 4
SCALE = HEAD**-0.5
NEGATIVE = -1e30
EPSILON = 1e-05
SECTION, DP = "section", "dp"
BF = jnp.bfloat16
F32 = jnp.float32
GELU_C = math.sqrt(2.0 / math.pi)
MEG = 1 << 20

FIRST = (SHARE, 7 * 128)
SECOND = (SHARE, 2 * WIDE)
ROWS_ATTN = 120
ROWS_VEC = 8
ROWS_FFN = FF // 16


def position_table():
    distance = (M + S - 1 - np.arange(TABLE)).astype(np.float32)
    inverse = np.exp(np.arange(0, D, 2).astype(np.float32) * np.float32(-math.log(10000.0) / D))
    angles = distance[:, None] * inverse[None, :].astype(np.float32)
    table = np.concatenate([np.sin(angles), np.cos(angles)], axis=1)
    table = np.concatenate([table, np.zeros((1, D), np.float32)], axis=0)
    return jnp.asarray(table, jnp.float32).astype(BF)


def dot_nn(a, b):
    return lax.dot_general(a, b, (((1,), (0,)), ((), ())), preferred_element_type=F32)


def dot_nt(a, b):
    return lax.dot_general(a, b, (((1,), (1,)), ((), ())), preferred_element_type=F32)


def norm_parts(values):
    centre = values - jnp.mean(values, axis=-1, keepdims=True)
    spread = jnp.mean(centre * centre, axis=-1, keepdims=True)
    root = lax.rsqrt(spread + EPSILON)
    return centre * root, root


def norm_back(values, gain, grad):
    normal, root = norm_parts(values)
    scaled = grad * gain
    grad_gain = jnp.sum(grad * normal, axis=0, keepdims=True)
    grad_shift = jnp.sum(grad, axis=0, keepdims=True)
    first = jnp.mean(scaled, axis=-1, keepdims=True)
    second = jnp.mean(scaled * normal, axis=-1, keepdims=True)
    return root * (scaled - first - normal * second), grad_gain, grad_shift


def gelu(v):
    return 0.5 * v * (1.0 + jnp.tanh(GELU_C * (v + 0.044715 * (v * v * v))))


def gelu_both(v):
    square = v * v
    bend = jnp.tanh(GELU_C * (v + 0.044715 * (square * v)))
    half = 0.5 * (1.0 + bend)
    slope = half + 0.5 * v * (1.0 - bend * bend) * (GELU_C * (1.0 + 3 * 0.044715 * square))
    return v * half, slope


def low_lanes():
    return lax.broadcasted_iota(jnp.int32, (1, 2 * HEAD), 1) < HEAD


def two_heads(pair):
    low = low_lanes()
    zero = jnp.zeros_like(pair)
    return jnp.concatenate([jnp.where(low, pair, zero), jnp.where(low, zero, pair)], axis=0)


def one_pair(stacked):
    half = stacked.shape[0] // 2
    return jnp.where(low_lanes(), stacked[:half], stacked[half:])


def in_two(values):
    high = values.astype(BF)
    return jnp.concatenate([high, (values - high.astype(F32)).astype(BF)], axis=1)


def skewed_scores(wide):
    parts = [
        pltpu.roll(wide[HALF * b : HALF * (b + 1)], WIDE - HALF + 1, 1, stride=1, stride_axis=0)
        for b in range(4)
    ]
    return jnp.concatenate(parts, axis=0)[:, :KEYS]


def unskewed_scores(scores):
    rows, wide = 4 * HALF, WIDE // 2
    shift = HALF - 1 - lax.broadcasted_iota(jnp.int32, (rows, wide), 0) % HALF
    lane = lax.broadcasted_iota(jnp.int32, (rows, wide), 1)
    source = (lane - shift) & (wide - 1)
    wrapped = lane < shift
    rest = jnp.concatenate([scores[:, wide:], jnp.zeros((rows, WIDE - KEYS), F32)], axis=1)
    first, second = (
        jnp.take_along_axis(a, source, axis=1, mode=lax.GatherScatterMode.PROMISE_IN_BOUNDS)
        for a in (scores[:, :wide], rest)
    )
    return jnp.concatenate(
        [jnp.where(wrapped, 0.0, first), jnp.where(wrapped, first, second)], axis=1
    )


def sight(at_ref, lengths_ref, ranks_ref, segments_ref):
    seq, half = at_ref[0] // 2, at_ref[0] % 2
    ranks = ranks_ref[pl.ds(seq, 1), :]
    segments = segments_ref[pl.ds(seq, 1), :]
    place = lax.broadcasted_iota(jnp.int32, (1, S), 1)
    lengths = lengths_ref[...].astype(F32)
    own = lax.broadcasted_iota(jnp.int32, lengths.shape, 1) == seq
    length = jnp.sum(jnp.where(own, lengths, 0.0), axis=-1, keepdims=True)
    live = jnp.where(place.astype(F32) < length, ranks, 2 * S)
    key_rank = jnp.concatenate([jnp.full((1, M), -1, jnp.int32), live], axis=1)
    key_segment = jnp.concatenate([jnp.zeros((1, M), jnp.int32), segments], axis=1)
    row = lax.broadcasted_iota(jnp.int32, (HALF, S), 0) + half * HALF
    column = lax.broadcasted_iota(jnp.int32, (HALF, S), 1)

    def upright(values):
        wide = jnp.where(row == column, values.astype(F32), 0.0)
        return jnp.sum(wide, axis=-1, keepdims=True).astype(jnp.int32)

    own_rank, own_segment = upright(ranks), upright(segments)
    reach = jnp.concatenate([own_rank, own_rank - 1], axis=0)
    hidden = jnp.where(key_rank <= reach, 0.0, 1.0)
    differs = jnp.where(jnp.concatenate([own_segment] * 2, axis=0) != key_segment, 1.0, 0.0)
    return [jnp.concatenate([a] * 2, axis=0) > 0.0 for a in (hidden, differs)]


class Mover:
    def __init__(self, semaphores):
        self.semaphores, self.count, self.open = semaphores, 0, []

    def __call__(self, source, target):
        copy = pltpu.make_async_copy(source, target, self.semaphores.at[self.count])
        self.count += 1
        copy.start()
        self.open.append(copy)
        return copy

    def wait(self, *copies):
        for copy in copies:
            if any(copy is other for other in self.open):
                self.open = [other for other in self.open if other is not copy]
                copy.wait()

    def finish(self):
        self.wait(*list(self.open))


class Bag:
    def __init__(self, names, values):
        self.__dict__.update(zip(names, values))


class Place:
    def __init__(self, seen, space):
        self.spec, self.space = pl.BlockSpec(memory_space=seen), space

    def operand(self, array):
        if self.space is None:
            return array
        return pltpu.with_memory_space_constraint(array, self.space)

    def result(self, shape, kind):
        return jax.ShapeDtypeStruct(shape, kind) if self.space is None else self.space(shape, kind)


SCALARS = Place(pltpu.SMEM, pltpu.HBM)
SMALL = Place(pltpu.VMEM, pltpu.HBM)
HERE = None
FAR = Place(pl.ANY, pltpu.HBM)
NEAR = Place(pltpu.VMEM, pltpu.VMEM)
TOKEN = pl.BlockSpec(memory_space=pl.ANY)
SPARE = 4 * MEG


def padded_bytes(shape, kind):
    *front, rows, columns = shape
    return math.prod(front) * -(-rows // 16) * 16 * -(-columns // 128) * 128 * jnp.dtype(kind).itemsize


def params(limit=8 * MEG):
    return pltpu.CompilerParams(vmem_limit_bytes=limit)


def cost(flops, moved):
    return pl.CostEstimate(flops=flops, bytes_accessed=moved, transcendentals=0)


ORDER = []


def position():
    index = lax.axis_index(DP)
    return [lax.axis_index(SECTION), index // 2, index % 2]


def run(kernel, name, ins, outs, scratch, copies=1, flops=1000, moved=1000, after=()):
    after = [place.operand(a) for a, place in ORDER[-1:]] + list(after)
    ins = {n: value for n, value in ins.items() if value[1] is not HERE}
    arrays, counts, specs, held_bytes = [], [], [], 0
    for value, place in ins.values():
        many = isinstance(value, (list, tuple))
        counts.append(len(value) if many else 0)
        for a in value if many else [value]:
            arrays.append(place.operand(a))
            specs.append(place.spec)
            held_bytes += padded_bytes(a.shape, a.dtype) if place is SMALL else 0
    shapes, out_specs = [], []
    for shape, kind, place in outs.values():
        many = isinstance(shape, list)
        counts.append(len(shape) if many else 0)
        for one in shape if many else [shape]:
            shapes.append(place.result(one, kind))
            out_specs.append(place.spec)
            held_bytes += 2 * padded_bytes(one, kind) if place is SMALL else 0
    held_bytes += sum(padded_bytes(*s) for s in scratch.values())

    def grouped(refs, counts):
        refs = list(refs)
        taken = []
        for count in counts:
            taken.append([refs.pop(0) for _ in range(count)] if count else refs.pop(0))
        return taken

    def body(*refs):
        refs = refs[: len(arrays)] + refs[len(arrays) + len(after) :]
        split = len(arrays) + len(shapes)
        go = Mover(refs[-1])
        named = Bag([*ins, *outs], grouped(refs[:split], counts))
        named.at = position()
        kernel(named, Bag(scratch, refs[split:-1]), go)
        go.finish()

    results = pl.pallas_call(
        body,
        in_specs=specs + [TOKEN] * len(after),
        out_specs=out_specs,
        out_shape=shapes,
        scratch_shapes=[pltpu.VMEM(*s) for s in scratch.values()]
        + [pltpu.SemaphoreType.DMA((copies,))],
        compiler_params=params(held_bytes + SPARE),
        cost_estimate=cost(flops, moved),
        name=name,
    )(*arrays, *after)
    ORDER.append((results[0], next(iter(outs.values()))[2]))
    return Bag(outs, grouped(results, counts[len(ins) :]))


def aligned(start, multiple, size=None):
    return pl.ds(pl.multiple_of(start, multiple), size or multiple)


SAVED = dict(
    summed=((ROWS, D), F32),
    qc=((ROWS, D), BF),
    qp=((ROWS, D), BF),
    qs=((ROWS, D), F32),
    kv=((KEYS, 2 * D), BF),
    rel=((WIDE, D), BF),
    mix=((ROWS, D), F32),
    prob=((PAIRS, 2 * ROWS, KEYS), F32),
)
FF_STEPS = 4
FF_BLOCK = FF // FF_STEPS


def attn_forward_body(layer, r, h, saved, w, go, ready):
    mine = slice(layer, layer + 1)
    go.wait(*ready)
    projected = dot_nn(h.x[...], w.wq[...])
    saved.qc[...] = ((projected + r.bias[0, mine, :]) * SCALE).astype(BF)
    saved.qp[...] = ((projected + r.bias[1, mine, :]) * SCALE).astype(BF)
    saved.qs[...] = (projected + r.bias[2, mine, :]) * SCALE
    saved.kv[...] = dot_nn(h.joined[...], w.wkv[...]).astype(BF)
    half = r.at[0] % 2
    rows = h.table[...] if layer == 0 else r.table[aligned(HALF * (1 - half), HALF, WIDE), :]
    saved.rel[...] = dot_nn(rows, w.wr[...]).astype(BF)
    hidden, differs = sight(r.at, r.lengths, r.ranks, r.segments)
    ones = jnp.ones((WIDE, KEYS), BF)
    beside = jnp.ones((KEYS, 2 * HEAD), BF)
    for p in range(PAIRS):
        at = slice(2 * HEAD * p, 2 * HEAD * (p + 1))
        later = slice(D + 2 * HEAD * p, D + 2 * HEAD * (p + 1))
        content = dot_nt(two_heads(saved.qc[:, at]), saved.kv[:, at])
        wide = dot_nt(two_heads(saved.qp[:, at]), saved.rel[:, at])
        segment = saved.qs[:, at]
        same = dot_nn(in_two(two_heads(segment * r.seg[layer, 0:1, at])), ones)
        other = dot_nn(in_two(two_heads(segment * r.seg[layer, 1:2, at])), ones)
        raw = content + skewed_scores(wide) + jnp.where(differs, other, same)
        scores = jnp.where(hidden, NEGATIVE, raw)
        exponent = jnp.exp(scores - jnp.max(scores, axis=-1, keepdims=True))
        values = jnp.concatenate([saved.kv[:, later], beside], axis=1)
        mixed = dot_nn(exponent.astype(BF), values)
        share = 1.0 / mixed[:, 2 * HEAD :]
        saved.prob[p] = exponent * jnp.concatenate([share, share[:, : KEYS - 2 * HEAD]], axis=1)
        attended = one_pair(mixed[:, : 2 * HEAD] * share)
        saved.mix[:, at] = attended
        h.att[:, at] = attended.astype(BF)
    summed = dot_nn(h.att[...], w.wo[...]) + h.x[...].astype(F32)
    saved.summed[...] = summed
    h.y[...] = (norm_parts(summed)[0] * r.again[mine, :] + r.ashift[mine, :]).astype(BF)


def ffn_forward_body(layer, r, h, w, go, ready=()):
    mine = slice(layer, layer + 1)
    y = h.y[...]
    go.wait(*ready)
    total = None
    for c in range(FF_STEPS):
        at = slice(FF_BLOCK * c, FF_BLOCK * (c + 1))
        pre = dot_nn(y, w.win[:, at]) + r.fbin[mine, at]
        h.pre[:, at] = pre
        part = dot_nn(gelu(pre).astype(BF), w.wout[at, :])
        total = part if total is None else total + part
    summed = total + r.fbout[mine, :] + y.astype(F32)
    h.fsum[...] = summed
    return (norm_parts(summed)[0] * r.fgain[mine, :] + r.fshift[mine, :]).astype(BF)


def ffn_backward_body(layer, grad, r, h, w):
    gsum, ggain, gshift = norm_back(h.fsum[...], r.fgain[layer : layer + 1, :], grad)
    low = gsum.astype(BF)
    gbias = jnp.sum(gsum, axis=0, keepdims=True)
    vectors = [ggain, gshift, gbias]
    total = gsum
    for c in range(FF_STEPS):
        at = slice(FF_BLOCK * c, FF_BLOCK * (c + 1))
        slope = gelu_both(h.pre[:, at])[1]
        gpre = (dot_nt(low, w.wout[at, :]) * slope).astype(BF)
        vectors.append(jnp.sum(gpre.astype(F32), axis=0, keepdims=True))
        total = total + dot_nt(gpre, w.win[:, at])
    vectors = jnp.concatenate(vectors + [jnp.zeros((1, D), F32)], axis=0)
    return total.astype(BF), low, vectors


def near_weights(layer, r):
    names = [n for n in WEIGHTS if n in r.__dict__]
    return Bag(names, [r.__dict__[n].at[layer] for n in names])


WEIGHTS = dict(
    wq=((D, D), BF), wkv=((D, 2 * D), BF), wr=((D, D), BF), wo=((D, D), BF), win=((D, FF), BF),
    wout=((FF, D), BF),
)
FORWARD_SCRATCH = dict(
    x=((ROWS, D), BF),
    joined=((KEYS, D), BF),
    att=((ROWS, D), BF),
    y=((ROWS, D), BF),
    pre=((ROWS, FF), F32),
    fsum=((ROWS, D), F32),
)


def forward_first_kernel(r, h, go):
    section = r.at[0]
    seq, half = section // 2, section % 2
    own = aligned(section * HALF, HALF)
    ready = [
        go(r.content.at[own], h.x.at[pl.ds(0, HALF)]),
        go(r.query.at[own], h.x.at[pl.ds(HALF, HALF)]),
        go(r.memory.at[0, aligned(seq * M, M)], h.joined.at[pl.ds(0, M)]),
        go(r.content.at[aligned(seq * S, S)], h.joined.at[pl.ds(M, S)]),
        go(r.table.at[aligned(HALF * (1 - half), HALF, WIDE)], h.table),
        go(r.wq.at[0], h.wq),
        go(r.wkv.at[0], h.wkv),
        go(r.wr.at[0], h.wr),
        go(r.wo.at[0], h.wo),
    ]
    later = [go(r.win.at[0], h.win), go(r.wout.at[0], h.wout)]
    attn_forward_body(0, r, h, h, h, go, ready)
    for n in SAVED:
        go(h.__dict__[n], r.__dict__[n])
    r.acts[:ROWS, :] = h.att[...]
    x = ffn_forward_body(0, r, h, h, go, later)
    go(h.pre, r.pre0)
    go(h.fsum, r.fsum0)
    r.acts[ROWS:, :] = x
    r.half[...] = x[:HALF]


def forward_second_kernel(r, h, go):
    section = r.at[0]
    seq, half = section // 2, section % 2
    own = aligned(section * HALF, HALF)
    w = near_weights(1, r)
    ready = [
        go(r.memory.at[1, aligned(seq * M, M)], h.joined.at[pl.ds(0, M)]),
        go(r.cotc.at[own], h.grad.at[pl.ds(0, HALF)]),
        go(r.cotq.at[own], h.grad.at[pl.ds(HALF, HALF)]),
    ]
    h.x[...] = r.acts0[ROWS:, :]
    h.joined[aligned(M + HALF * half, HALF), :] = r.acts0[ROWS : ROWS + HALF, :]
    h.joined[aligned(M + HALF * (1 - half), HALF), :] = r.other[...]
    attn_forward_body(1, r, h, r, w, go, ready)
    r.acts[:ROWS, :] = h.att[...]
    r.out[...] = ffn_forward_body(1, r, h, w, go)
    gy, low, vectors = ffn_backward_body(1, h.grad[...].astype(F32), r, h, w)
    r.acts[ROWS:, :] = low
    r.gy[...] = gy
    r.fvec[...] = vectors


def ffn_backward_kernel(r, h, go):
    go(r.fsum0, h.fsum)
    go(r.pre0, h.pre)
    w = near_weights(0, r)
    gx = r.gx
    grad = jnp.concatenate([gx[:HALF, :] + r.other[...].astype(F32), gx[HALF:, :]], axis=0)
    go.finish()
    gy, low, vectors = ffn_backward_body(0, grad.astype(BF).astype(F32), r, h, w)
    r.low[...] = low
    r.gy[...] = gy
    r.fvec[...] = vectors


def attn_backward_kernel(layer, r, h, go):
    section = r.at[0]
    half = section % 2
    mine = slice(layer, layer + 1)
    w = near_weights(layer, r)
    if layer == 0:
        loads = [go(r.__dict__[n], h.__dict__[n]) for n in SAVED]
        go.wait(loads[0])
    k = h if layer == 0 else r
    gsum, ggain, gshift = norm_back(k.summed[...], r.again[mine, :], r.gy[...].astype(F32))
    low = gsum.astype(BF)
    h.vec[0:1, :] = ggain
    h.vec[1:2, :] = gshift
    h.vec[7:15, :] = r.fvec[...]
    h.vec[15:16, :] = jnp.zeros((1, D), F32)
    g_attended = dot_nt(low, w.wo[...]).astype(BF)
    go.finish()
    differs = sight(r.at, r.lengths, r.ranks, r.segments)[1]
    lowest = low_lanes()
    ones = jnp.ones((WIDE, KEYS), BF)
    for p in range(PAIRS):
        at = slice(2 * HEAD * p, 2 * HEAD * (p + 1))
        later = slice(D + 2 * HEAD * p, D + 2 * HEAD * (p + 1))
        prob = k.prob[p]
        ga = two_heads(g_attended[:, at])
        gprob = dot_nt(ga, k.kv[:, later])
        h.gkv[later, :] = dot_nn(ga.T, prob.astype(BF)).astype(BF)
        centre = dot_nn(in_two(two_heads(g_attended[:, at].astype(F32) * k.mix[:, at])), ones)
        gscores = (prob * (gprob - centre)).astype(BF)
        gqc = one_pair(dot_nn(gscores, k.kv[:, at]))
        h.gkv[at, :] = dot_nn(two_heads(k.qc[:, at]).T, gscores).astype(BF)
        gwhole = gscores.astype(F32)
        gwide = unskewed_scores(gwhole).astype(BF)
        gqp = one_pair(dot_nn(gwide, k.rel[:, at]))
        h.grel[at, :] = dot_nn(two_heads(k.qp[:, at]).T, gwide)
        other_part = jnp.where(differs, gwhole, 0.0)
        other = jnp.sum(other_part, axis=-1, keepdims=True)
        same = jnp.sum(gwhole - other_part, axis=-1, keepdims=True)
        same_pair = jnp.where(lowest, same[:ROWS], same[ROWS:])
        other_pair = jnp.where(lowest, other[:ROWS], other[ROWS:])
        gqs = same_pair * r.seg[layer, 0:1, at] + other_pair * r.seg[layer, 1:2, at]
        segment = k.qs[:, at]
        h.vec[2:3, at] = jnp.sum(gqc, axis=0, keepdims=True) * SCALE
        h.vec[3:4, at] = jnp.sum(gqp, axis=0, keepdims=True) * SCALE
        h.vec[4:5, at] = jnp.sum(gqs, axis=0, keepdims=True) * SCALE
        h.vec[5:6, at] = jnp.sum(same_pair * segment, axis=0, keepdims=True)
        h.vec[6:7, at] = jnp.sum(other_pair * segment, axis=0, keepdims=True)
        h.turned[at, :ROWS] = low[:, at].astype(F32).T
        h.turned[at, ROWS:] = ((gqc + gqp + gqs) * SCALE).T
    few, step = KEYS - 128, D // 8
    for n, message in enumerate(r.first):
        d = section ^ n

        def chosen(ref, size, multiple):
            starts = [4 * size * e + size * d for e in range(8)]
            return jnp.concatenate([ref[aligned(m, multiple, size), :] for m in starts], axis=0)

        message[:SHARE, :256] = chosen(h.turned, step // 4, 8).astype(BF)
        message[:SHARE, 256:512] = chosen(h.grel, step // 4, 8).astype(BF)
        keyval = chosen(h.gkv, step // 2, 16)
        for j in range(2):
            rows = keyval[SHARE * j : SHARE * (j + 1)]
            message[:SHARE, 512 + 128 * j : 640 + 128 * j] = rows[:, :128]
            message[:SHARE, 768 + few * j : 768 + few * (j + 1)] = rows[:, 128:]
    joined = dot_nn(w.wkv[...], h.gkv[...])
    one, two = joined[:, M : M + HALF], joined[:, M + HALF :]
    first_half = jnp.zeros((1, 1), jnp.int32) + half == 0
    own, partner = jnp.where(first_half, one, two), jnp.where(first_half, two, one)
    gx = dot_nn(w.wq[...], h.turned[:, ROWS:].astype(BF)) + gsum.T
    gx = jnp.concatenate([gx[:, :HALF] + own, gx[:, HALF:]], axis=1)
    if layer > 0:
        r.send[...] = partner.T.astype(BF)
        r.gx[...] = gx.T
        r.second[:, : 2 * HALF] = r.out[...].T
        r.second[:, 2 * HALF :] = jnp.concatenate([partner, joined[:, :M]], axis=1).astype(BF)
        r.vec[...] = h.vec[...]
    else:
        h.second[:, : 2 * HALF] = gx.astype(BF)
        h.second[:, 2 * HALF : WIDE] = jnp.concatenate([partner, joined[:, :M]], axis=1).astype(BF)
        h.second[:, WIDE:] = r.later[...]
        for d in range(4):
            at = slice(SHARE * d, SHARE * (d + 1))
            for n, vec in enumerate((h.vec, r.vectors)):
                place = slice(SHARE * n, SHARE * (n + 1))
                wide = vec[10 + d : 11 + d, :]
                rows = [vec[:10, at]] + [wide[:, SHARE * j : SHARE * (j + 1)] for j in range(4)]
                rows = jnp.concatenate(rows + [jnp.zeros((2, SHARE), F32)], axis=0)
                h.parts[d, :, place] = rows.astype(BF)
        for n, message in enumerate(r.second):
            message[...] = h.second[aligned(SHARE * (section ^ n), SHARE), :]
        for n, message in enumerate(r.first):
            message[SHARE:, : 2 * SHARE] = h.parts[section ^ n]


def gathered_x(layer, r, h):
    for n in range(4):
        if layer == 0:
            rows = aligned((r.at[0] ^ n) * HALF, HALF)
            h.x[ROWS * n : ROWS * n + HALF, :] = r.content[rows, :]
            h.x[ROWS * n + HALF : ROWS * (n + 1), :] = r.query[rows, :]
        else:
            h.x[ROWS * n : ROWS * (n + 1), :] = r.before[n][ROWS:, :]


def put_halves(r, h):
    core = r.at[2]
    for j in range(4):
        r.kept[j] = h.pieces[2 * j + core]
        for part, given in enumerate(r.given):
            n = given.shape[1]
            given[j] = h.pieces[2 * j + 1 - core, n * part : n * (part + 1), :]


def shares_kernel(layer, r, h, go):
    wide, few = FF // 8, FF // 32
    for t in range(4):

        @pl.when(r.at[0] == t)
        def _():
            for d in range(8):
                at = slice(few * d, few * (d + 1))
                held = slice(wide * d + few * t, wide * d + few * (t + 1))
                r.bias[:, at] = r.fbin[layer : layer + 1, held]
                r.inner[:, at] = r.win[layer, :, held]
                r.outer[at, :] = r.wout[layer, held, :]


def ffn_weights_kernel(layer, fast, r, h, go):
    mine = slice(layer, layer + 1)
    gathered_x(layer, r, h)
    attended = jnp.concatenate([a[:ROWS, :] for a in r.acts], axis=0)
    summed = dot_nn(attended, r.wo[layer]) + h.x[...].astype(F32)
    y = norm_parts(summed)[0] * r.again[mine, :] + r.ashift[mine, :]
    h.y[...] = y.astype(BF)
    for n, low in enumerate(r.low):
        rows = low[low.shape[0] - ROWS :, :]
        h.low[ROWS * n : ROWS * (n + 1), :] = rows
        h.lowt[:, ROWS * n : ROWS * (n + 1)] = rows.T
    width, few = FF // 8, FF // 32
    for t in range(2):
        at = slice(width * t, width * (t + 1))
        pre = dot_nn(h.y[...], r.inner[:, at]) + r.bias[:, at]
        active, slope = gelu_both(pre)
        gpre = (dot_nt(h.low[...], r.outer[at, :]) * slope).astype(BF)
        grad_in = dot_nn(gpre.T, h.y[...]).astype(BF)
        grad_out = dot_nn(h.lowt[...], active.astype(BF)).astype(BF)
        if fast:
            for d in range(4):
                h.pieces[4 * t + d, :few, :] = grad_in[few * d : few * (d + 1), :]
            for d in range(8):
                h.pieces[d, few:, at] = grad_out[few * d : few * (d + 1), :]
        else:
            r.grads[0][at, :] = grad_in
            r.grads[1][:, at] = grad_out
    if fast:
        put_halves(r, h)


def attn_weights_kernel(fast, r, h, go):
    parts = []
    for layer in range(LAYERS):
        grads = attn_grads(layer, r, h)
        if fast:
            for n, grad in enumerate(grads):
                h.grads[layer, SHARE * n : SHARE * n + grad.shape[0], :] = grad
        else:
            for n, grad in enumerate(grads):
                r.grads[4 * layer + n][...] = grad.astype(BF)
    vectors = None
    for f in r.first:
        part = f[SHARE : SHARE + 16, : 2 * SHARE].astype(F32)
        vectors = part if vectors is None else vectors + part
    if not fast:
        r.vectors[...] = vectors
        return
    vectors = jnp.concatenate([vectors[:8], vectors[8:]], axis=1)
    step = D // 8
    for d in range(8):
        rows = []
        for layer in range(LAYERS):
            for n in range(4):
                size = step // 2 if n == 3 else step // 4
                start = SHARE * n + size * d
                rows.append(h.grads[layer, start : start + size, :])
        rows = jnp.concatenate(rows + [vectors, jnp.zeros_like(vectors)], axis=0)
        h.pieces[d] = rows.astype(BF)
    put_halves(r, h)


def attn_grads(layer, r, h):
    section = r.at[0]
    half = section % 2
    first = [f.at[pl.ds(0, SHARE)] for f in (r.first, r.earlier)[layer]]
    gathered_x(layer, r, h)
    for pair in range(2):
        rows = aligned((section ^ (2 * pair)) // 2 * M, M)
        h.joined[pair, :M, :] = r.memory[layer, rows, :]
        for n in (2 * pair, 2 * pair + 1):
            place = half ^ (n & 1)
            h.joined[pair, aligned(M + HALF * place, HALF), :] = h.x[ROWS * n : ROWS * n + HALF, :]
    low = jnp.concatenate([f[:, :128] for f in first], axis=1)
    proj = jnp.concatenate([f[:, 128:256] for f in first], axis=1)
    grad_q = dot_nn(proj, h.x[...])
    attended = jnp.concatenate([a[:ROWS, :] for a in (r.acts0, r.acts1)[layer]], axis=0)
    grad_o = dot_nn(low, attended)
    few = KEYS - 128
    grad_kv = grad_rel = None
    for pair in range(2):
        both = add(first[2 * pair][:, 512:], first[2 * pair + 1][:, 512:])
        both = jnp.concatenate(
            [
                jnp.concatenate([both[:, :128], both[:, 256 : 256 + few]], axis=1),
                jnp.concatenate([both[:, 128:256], both[:, 256 + few :]], axis=1),
            ],
            axis=0,
        )
        part = dot_nn(both, h.joined[pair])
        grad_kv = part if grad_kv is None else grad_kv + part
    for n in range(2):
        place = half ^ n
        total = add(first[n][:, 256:512], first[n + 2][:, 256:512])
        rows = r.table[aligned(HALF * (1 - place), HALF, WIDE), :]
        part = dot_nn(total, rows)
        grad_rel = part if grad_rel is None else grad_rel + part
    return grad_q, grad_o, grad_rel, grad_kv


def add(a, b):
    return (a.astype(F32) + b.astype(F32)).astype(BF)


def whole(shape):
    return pl.BlockSpec(shape, lambda i: (0,) * len(shape))


def gather_kernel(*refs):
    section = position()[0]
    start = refs[0].shape[1] - 2 * WIDE
    early = [r.at[:, pl.ds(start, WIDE)] for r in refs[:4]]
    late = [r.at[:, pl.ds(start + WIDE, WIDE)] for r in refs[:4]]
    small_ref = refs[4]
    outc_ref, outq_ref, gradc_ref, gradq_ref, mem_ref = refs[5:10]
    bias_ref, seg_ref, again_ref, ashift_ref, inb_ref, outb_ref, fgain_ref, fshift_ref = refs[10:18]

    def in_order(blocks):
        odd = jnp.zeros((1, 1), jnp.int32) + section % 2 == 1
        high = jnp.zeros((1, 1), jnp.int32) + section // 2 == 1
        a, b, c, d = blocks
        a, b, c, d = (
            jnp.where(odd, b, a), jnp.where(odd, a, b), jnp.where(odd, d, c), jnp.where(odd, c, d)
        )
        left, right = jnp.concatenate([a, b], axis=1), jnp.concatenate([c, d], axis=1)
        return jnp.concatenate([jnp.where(high, right, left), jnp.where(high, left, right)], axis=1)

    def blocks(four, start):
        return [f[:, start : start + HALF].astype(F32) for f in four]

    outc_ref[...] = in_order(blocks(late, 0)).astype(BF)
    outq_ref[...] = in_order(blocks(late, HALF)).astype(BF)
    own, passed = blocks(early, 0), blocks(early, 2 * HALF)
    gradc_ref[...] = in_order([own[k] + passed[k ^ 1] for k in range(4)])
    gradq_ref[...] = in_order(blocks(early, HALF))
    high = jnp.zeros((1, 1), jnp.int32) + section // 2 == 1
    for layer, four in ((0, early), (1, late)):
        a, b, c, d = blocks(four, 3 * HALF)
        one, two = a + b, c + d
        mem_ref[layer] = jnp.concatenate(
            [jnp.where(high, two, one), jnp.where(high, one, two)], axis=1
        )
    for layer in range(LAYERS):
        mine = slice(layer, layer + 1)

        held = slice(SHARE * layer, SHARE * (layer + 1))

        def vector(row):
            return small_ref[row : row + 1, held].astype(F32)

        for j in range(3):
            bias_ref[j, mine, :] = vector(2 + j)
        for j in range(2):
            seg_ref[layer, j : j + 1, :] = vector(5 + j)
        again_ref[mine, :] = vector(0)
        ashift_ref[mine, :] = vector(1)
        fgain_ref[mine, :] = vector(7)
        fshift_ref[mine, :] = vector(8)
        outb_ref[mine, :] = vector(9)
        for j in range(4):
            inb_ref[mine, SHARE * j : SHARE * (j + 1)] = vector(10 + j)


def gather_rows(at, rows_out, small):
    rows = 4 * HALF
    vector = ((LAYERS, SHARE), F32)
    shapes = [
        ((SHARE, rows), BF),
        ((SHARE, rows), BF),
        ((SHARE, rows), F32),
        ((SHARE, rows), F32),
        ((LAYERS, SHARE, 2 * M), F32),
        ((3, LAYERS, SHARE), F32),
        ((LAYERS, 2, SHARE), F32),
        vector,
        vector,
        ((LAYERS, FF // 4), F32),
        vector,
        vector,
        vector,
    ]
    return pl.pallas_call(
        gather_kernel,
        grid=(1,),
        in_specs=[whole(a.shape) for a in (*rows_out, small)],
        out_specs=[whole(s) for s, _ in shapes],
        out_shape=[jax.ShapeDtypeStruct(s, t) for s, t in shapes],
        compiler_params=params(),
        cost_estimate=cost(1_000_000, 2_000_000),
        name="gather_rows",
    )(*rows_out, small)


def final_ffn_kernel(r, h, go):
    few = FF // 32
    for n, message in enumerate(r.ffn):
        h.got[r.at[0] ^ n] = message[...].astype(F32)
    for layer in range(LAYERS):
        rows_at = slice(few * layer, few * (layer + 1))
        for s in range(4):
            held = slice(few * s, few * (s + 1))
            r.fin[layer, :, held] = h.got[s, rows_at, :SHARE].T
            for e in range(2):
                place = slice(FF // 8 * e + few * s, FF // 8 * e + few * (s + 1))
                start = SHARE + few * e
                r.fout[layer, :, place] = h.got[s, rows_at, start : start + few]


def final_attn_kernel(r, h, go):
    for n, message in enumerate(r.attn):
        h.attn[r.at[0] ^ n] = message[...].astype(F32)
    step = D // 8
    for layer in range(LAYERS):
        lanes = slice(SHARE * layer, SHARE * (layer + 1))
        start = 0
        for made, size in ((r.q, step // 4), (r.o, step // 4), (r.rel, step // 4), (r.kv, step // 2)):
            blocks = [h.attn[s, start : start + size, lanes] for s in range(4)]
            made[layer] = jnp.concatenate(blocks, axis=0).T
            start += size


def final_ffn(at, ffn):
    return run(
        final_ffn_kernel,
        "final_ffn",
        dict(at=(at, HERE), ffn=(ffn, NEAR)),
        dict(
            fin=((LAYERS, SHARE, FF // 8), F32, SMALL),
            fout=((LAYERS, D // 8, FF // 4), F32, SMALL),
        ),
        dict(got=((4, FF // 16, 2 * SHARE), F32)),
    )


def final_attn(at, attn):
    half = ((LAYERS, SHARE, SHARE // 2), F32, SMALL)
    return run(
        final_attn_kernel,
        "final_attn",
        dict(at=(at, HERE), attn=(attn, NEAR)),
        dict(q=half, kv=((LAYERS, SHARE, SHARE), F32, SMALL), o=half, rel=half),
        dict(attn=((4, ROWS_ATTN + 8, 2 * SHARE), F32)),
    )


def split_kernel(r, h, go):
    chip = r.at[1]
    for part, got in enumerate(r.got):
        n = got.shape[1]
        rows = pl.ds(n * part, n)
        for m, p in enumerate((chip, chip ^ 2)):
            r.keep[m, rows, :] = add(r.kept[p, rows, :], got[p])
        place, put = n * part, 0
        while place >= r.send[put].shape[1]:
            place, put = place - r.send[put].shape[1], put + 1
        for m, p in enumerate((chip ^ 1, chip ^ 3)):
            r.send[put][m, pl.ds(place, n), :] = add(r.kept[p, rows, :], got[p])


def fold_kernel(start, also, r, h, go):
    rows = pl.ds(start, r.got.shape[1])
    r.own[...], r.far[...] = [add(r.keep[m, rows, :], r.got[m]) for m in range(2)]
    if also:
        r.total[...] = add(*[a[...] for a in r.also])


def shared_attn_kernel(r, h, go):
    total = [own[...].astype(F32) + got[...].astype(F32) for own, got in zip(r.own, r.got)]
    total = jnp.concatenate(total, axis=0)
    layers = [total[ROWS_ATTN * n : ROWS_ATTN * (n + 1)] for n in range(LAYERS)]
    for t in range(4):
        at = slice(SHARE * t, SHARE * (t + 1))
        rows = jnp.concatenate([m[:, at] for m in layers], axis=1)
        h.parts[t] = jnp.concatenate([rows, jnp.zeros((8, 2 * SHARE), F32)], axis=0).astype(BF)
    for n, part in enumerate(r.parts):
        part[...] = h.parts[r.at[0] ^ n]
    vectors = total[LAYERS * ROWS_ATTN : LAYERS * ROWS_ATTN + 8]
    r.vectors[...] = jnp.concatenate([vectors[:, : 2 * SHARE], vectors[:, 2 * SHARE :]], axis=0)


def shared_kernel(r, h, go):
    few = FF // 32
    for layer, total in enumerate((add(r.own[...], r.got[...]), r.later[...])):
        rows = slice(few * layer, few * (layer + 1))
        for t in range(4):
            at = slice(SHARE * t, SHARE * (t + 1))
            h.parts[t, rows, :SHARE], h.parts[t, rows, SHARE:] = total[:few, at], total[few:, at]
    for n, part in enumerate(r.parts):
        part[...] = h.parts[r.at[0] ^ n]


def split_pieces(at, made, cuts=(), after=()):
    got = [swapped(a, DP, 1) for a in made.given]
    shape = (2,) + made.kept.shape[1:]
    ins = dict(at=(at, HERE), kept=(made.kept, NEAR), got=(got, NEAR))
    parts = [(2, n, shape[2]) for n in cuts or shape[1:2]]
    return run(
        split_kernel, "split_pieces", ins, dict(keep=(shape, BF, NEAR), send=(parts, BF, NEAR)), {},
        after=after,
    )


def fold_pieces(split, part=0, also=()):
    got = swapped(split.send[part], DP, 2)
    start = sum(a.shape[1] for a in split.send[:part])
    ins = dict(keep=(split.keep, NEAR), got=(got, NEAR))
    shape = got.shape[1:]
    outs = dict(own=(shape, BF, NEAR), far=(shape, BF, NEAR))
    if also:
        ins.update(also=(also, NEAR))
        outs.update(total=(also[0].shape, BF, NEAR))
    kernel = functools.partial(fold_kernel, start, bool(also))
    folded = run(kernel, "fold_pieces", ins, outs, {})
    pieces = (folded.own, swapped(folded.far, DP, 4))
    return (pieces, folded.total) if also else pieces


def shared_attn(at, folded, after=()):
    ins = dict(
        at=(at, HERE), own=([f[0] for f in folded], NEAR), got=([f[1] for f in folded], NEAR)
    )
    shape = (ROWS_ATTN + 8, 2 * SHARE)
    return run(
        shared_attn_kernel, "shared_attn", ins,
        dict(parts=([shape] * 4, BF, NEAR), vectors=((16, 2 * SHARE), F32, NEAR)),
        dict(parts=((4,) + shape, BF)), after=after,
    )


def shared_pieces(at, folded, later, after=()):
    own, got = folded
    ins = dict(
        at=(at, HERE), own=(own, NEAR), got=(got, NEAR), later=(later, NEAR)
    )
    shape = (FF // 16, 2 * SHARE)
    return run(
        shared_kernel, "shared_pieces", ins,
        dict(parts=([shape] * 4, BF, NEAR)),
        dict(parts=((4,) + shape, BF)), after=after,
    ).parts


def swapped(x, axis, k):
    return lax.ppermute(x, axis, [(i, i ^ k) for i in range(lax.axis_size(axis))])


def from_all(x):
    return [x] + [swapped(x, SECTION, k) for k in (1, 2, 3)]


def messages(parts):
    return [parts[0]] + [swapped(parts[k], SECTION, k) for k in (1, 2, 3)]


def on_device(
    content_in,
    query_in,
    memory,
    doc_lengths,
    perm_rank,
    segment_ids,
    w_query,
    w_keyval,
    w_out,
    w_rel,
    head_bias,
    seg_embed,
    attn_gain,
    attn_shift,
    ffn_in,
    ffn_in_bias,
    ffn_out,
    ffn_out_bias,
    ffn_gain,
    ffn_shift,
    cot_content,
    cot_query,
):
    ORDER.clear()
    dp = lax.axis_size(DP)
    fast = dp == 8
    at = None
    table = position_table()
    marks = dict(
        at=(at, HERE),
        lengths=(doc_lengths.reshape(1, -1), SMALL),
        ranks=(perm_rank, SMALL),
        segments=(segment_ids, SMALL),
    )
    attn_v = dict(
        bias=(head_bias.transpose(1, 0, 2), SMALL),
        seg=(seg_embed, SMALL),
        again=(attn_gain, SMALL),
        ashift=(attn_shift, SMALL),
    )
    ffn_v = dict(
        fbin=(ffn_in_bias, SMALL),
        fbout=(ffn_out_bias, SMALL),
        fgain=(ffn_gain, SMALL),
        fshift=(ffn_shift, SMALL),
    )
    matrices = dict(
        wq=w_query, wkv=w_keyval, wr=w_rel, wo=w_out, win=ffn_in, wout=ffn_out,
    )
    near = {n: (a, NEAR) for n, a in matrices.items()}

    def of(which, *names):
        return {n: which[n] for n in which if n in names}

    first = run(
        forward_first_kernel,
        "forward_first",
        dict(
            **marks,
            content=(content_in, FAR),
            query=(query_in, FAR),
            memory=(memory, FAR),
            table=(table, FAR),
            **{n: (a, FAR) for n, a in matrices.items()},
            **attn_v,
            **ffn_v,
        ),
        dict(
            acts=((2 * ROWS, D), BF, NEAR),
            half=((HALF, D), BF, NEAR),
            pre0=((ROWS, FF), F32, FAR),
            fsum0=((ROWS, D), F32, FAR),
            **{n: (*s, FAR) for n, s in SAVED.items()},
        ),
        dict(**FORWARD_SCRATCH, table=((WIDE, D), BF), **WEIGHTS, **SAVED),
        copies=24,
        flops=2_400_000_000,
        moved=16_000_000,
    )
    marks, attn_v, ffn_v = (
        {n: (a, NEAR if place is SMALL else place) for n, (a, place) in group.items()}
        for group in (marks, attn_v, ffn_v)
    )
    other = swapped(first.half, SECTION, 1)
    acts0 = from_all(first.acts)
    second = run(
        forward_second_kernel,
        "forward_second",
        dict(
            **marks,
            acts0=(first.acts, NEAR),
            other=(other, NEAR),
            memory=(memory, FAR),
            table=(table, NEAR),
            cotc=(cot_content, FAR),
            cotq=(cot_query, FAR),
            **near,
            **attn_v,
            **ffn_v,
        ),
        dict(
            acts=((2 * ROWS, D), BF, NEAR),
            out=((ROWS, D), BF, NEAR),
            gy=((ROWS, D), BF, NEAR),
            fvec=((8, D), F32, NEAR),
            **{n: (*s, NEAR) for n, s in SAVED.items()},
        ),
        dict(**FORWARD_SCRATCH, grad=((ROWS, D), BF)),
        copies=4,
        flops=3_600_000_000,
        moved=16_000_000,
    )
    acts1 = from_all(second.acts)

    def attn_backward(layer, saved, gy, fvec, after=(), **extra):
        ins = dict(
            **marks,
            gy=(gy, NEAR),
            fvec=(fvec, NEAR),
            **{n: (saved.__dict__[n], FAR if layer == 0 else NEAR) for n in SAVED},
            **{n: near[n] for n in list(WEIGHTS)[:4] if n != list(WEIGHTS)[2]},
            **attn_v,
            **{n: (a, NEAR) for n, a in extra.items()},
        )
        scratch = dict(
            vec=((16, D), F32),
            turned=((D, 2 * ROWS), F32),
            gkv=((2 * D, KEYS), BF),
            grel=((D, WIDE), F32),
        )
        rows = FIRST[0] if layer else FIRST[0] + 16
        outs = dict(first=([(rows, FIRST[1])] * 4, BF, NEAR))
        if layer == 0:
            outs.update(second=([SECOND] * 4, BF, NEAR))
            scratch.update(SAVED, second=((D, 2 * WIDE), BF), parts=((4, 16, 2 * SHARE), BF))
        else:
            outs.update(
                second=((D, WIDE), BF, NEAR),
                gx=((ROWS, D), F32, NEAR),
                send=((HALF, D), BF, NEAR),
                vec=((16, D), F32, NEAR),
            )
        return run(
            functools.partial(attn_backward_kernel, layer), "attn_backward", ins, outs, scratch,
            copies=10, flops=1000, moved=1000, after=after,
        )

    def inputs_of(layer):
        if layer == 0:
            return dict(content=(content_in, NEAR), query=(query_in, NEAR))
        return dict(before=(acts0, NEAR))

    def grads_of(shape, plain, cuts=2):
        if fast:
            parts = [(4, shape[0] // cuts, shape[1])] * cuts
            return dict(kept=((4,) + shape, BF, NEAR), given=(parts, BF, NEAR))
        return dict(grads=(plain, BF, SMALL))

    def shares_of(layer):
        return run(
            functools.partial(shares_kernel, layer),
            "shares",
            dict(at=marks["at"], **of(near, "win", "wout"), **of(ffn_v, "fbin")),
            dict(
                inner=((D, D), BF, NEAR),
                outer=((D, D), BF, NEAR),
                bias=((1, D), F32, NEAR),
            ),
            {},
        )

    def ffn_weights(layer, shares, acts, lows, after=()):
        ins = dict(
            at=marks["at"],
            **inputs_of(layer),
            **of(near, "wo"),
            **of(attn_v, "again", "ashift"),
            inner=(shares.inner, NEAR),
            outer=(shares.outer, NEAR),
            bias=(shares.bias, NEAR),
            acts=(acts, NEAR),
            low=(lows, NEAR),
        )
        shape = (ROWS_FFN, D)
        tall = ((4 * ROWS, D), BF)
        return run(
            functools.partial(ffn_weights_kernel, layer, fast),
            "ffn_weights",
            ins,
            grads_of(shape, [(D, D), (D, D)]),
            dict(x=tall, y=tall, low=tall, lowt=((D, 4 * ROWS), BF), pieces=((8,) + shape, BF)),
            flops=1000,
            moved=1000,
            after=after,
        )

    def attn_weights(notes, earlier, after=()):
        ins = dict(
            at=marks["at"],
            content=(content_in, NEAR),
            query=(query_in, NEAR),
            before=(acts0, NEAR),
            memory=(memory, NEAR),
            table=(table, NEAR),
            acts0=(acts0, NEAR),
            acts1=(acts1, NEAR),
            first=(notes, NEAR),
            earlier=(earlier, NEAR),
        )
        shape = (2 * ROWS_ATTN + 2 * ROWS_VEC, D)
        outs = grads_of(shape, [(SHARE, D), (SHARE, D), (SHARE, D), (2 * SHARE, D)] * 2, 4)
        if not fast:
            outs.update(vectors=((2 * ROWS_VEC, 2 * SHARE), F32, SMALL))
        return run(
            functools.partial(attn_weights_kernel, fast),
            "attn_weights",
            ins,
            outs,
            dict(
                x=((4 * ROWS, D), BF),
                joined=((2, KEYS, D), BF),
                grads=((LAYERS, 5 * SHARE, D), F32),
                pieces=((8,) + shape, BF),
            ),
            flops=10**12,
            moved=10**9,
            after=after,
        )

    back1 = attn_backward(1, second, second.gy, second.fvec, acts0[1:], out=second.out)
    received = swapped(back1.send, SECTION, 1)
    parts1 = messages(back1.first)
    shares1, shares0 = shares_of(1), shares_of(0)
    fgrads1 = ffn_weights(1, shares1, acts1, acts1)
    third = run(
        ffn_backward_kernel,
        "ffn_backward",
        dict(
            gx=(back1.gx, NEAR),
            other=(received, NEAR),
            fsum0=(first.fsum0, FAR),
            pre0=(first.pre0, FAR),
            **of(near, "win", "wout"),
            **of(ffn_v, "fgain"),
        ),
        dict(
            low=((ROWS, D), BF, NEAR), gy=((ROWS, D), BF, NEAR), fvec=((8, D), F32, NEAR)
        ),
        dict(fsum=((ROWS, D), F32), pre=((ROWS, FF), F32)),
        copies=4,
        flops=10**12,
        moved=10**9,
    )
    lows0 = from_all(third.low)
    if fast:
        split_f1 = split_pieces(at, fgrads1, after=parts1[1:])
    back0 = attn_backward(
        0, first, third.gy, third.fvec, later=back1.second, vectors=back1.vec
    )
    parts0 = messages(back0.first)
    rows_out = back0.second
    fgrads0 = ffn_weights(0, shares0, acts0, lows0)
    if fast:
        fold_f1 = fold_pieces(split_f1)
        split_f0 = split_pieces(at, fgrads0)
    agrads = attn_weights(parts0, parts1)
    if fast:
        fold_f0, sum_f1 = fold_pieces(split_f0, also=fold_f1)
        split_a = split_pieces(at, agrads, (192, 64))
        folded = [fold_pieces(split_a, 0)]
        rows_all = messages(rows_out)
        ffn = messages(shared_pieces(at, fold_f0, sum_f1, rows_all[1:]))
        folded.append(fold_pieces(split_a, 1))
        made = final_ffn(at, ffn)
        fin, fout = made.fin, made.fout
        shared_a = shared_attn(at, folded)
        attn_all = messages(shared_a.parts)
        outs = gather_rows(at, rows_all, shared_a.vectors)
        made = final_attn(at, attn_all)
        wq, wkv, wo, wr = made.q, made.kv, made.o, made.rel
        fout = fout.transpose(0, 2, 1)
    else:
        outs = gather_rows(at, messages(rows_out), lax.psum(agrads.vectors, DP))
        section = lax.axis_index(SECTION)

        def owned(rows):
            part = rows.reshape((dp, -1) + rows.shape[1:])
            part = lax.psum_scatter(part, DP, scatter_dimension=0, tiled=False)
            part = lax.psum(part, SECTION)
            width = part.shape[1] // 4
            return lax.dynamic_slice_in_dim(part, section * width, width, 1).astype(F32).T

        def at_share(share, count, axis=0):
            cut = share.reshape(share.shape[:axis] + (count, 1, -1) + share.shape[axis + 1 :])
            full = jnp.zeros(cut.shape[: axis + 1] + (4,) + cut.shape[axis + 2 :], BF)
            full = lax.dynamic_update_slice_in_dim(full, cut, section, axis + 1)
            return full.reshape(share.shape[:axis] + (-1,) + share.shape[axis + 1 :])

        def plain(fgrads, agrads):
            parts = [at_share(a, 8) for a in agrads]
            parts += [at_share(fgrads[0], 8), at_share(fgrads[1], 8, 1)]
            q, o, rel, kv, fin, fout = [owned(a) for a in parts]
            return q, kv, o, rel, fin, fout

        pairs = zip(plain(fgrads0.grads, agrads.grads[:4]), plain(fgrads1.grads, agrads.grads[4:]))
        wq, wkv, wo, wr, fin, fout = [jnp.stack(p) for p in pairs]
    return (
        outs[0].T,
        outs[1].T,
        outs[2].T,
        outs[3].T,
        outs[4].transpose(0, 2, 1),
        wq,
        wkv,
        wo,
        wr,
        outs[5].transpose(1, 0, 2),
        outs[6],
        outs[7],
        outs[8],
        fin,
        outs[9],
        fout,
        outs[10],
        outs[11],
        outs[12],
    )


def solution(mesh):
    in_specs = (
        P(DP, None),
        P(DP, None),
        P(None, DP, None),
        P(DP),
        P(DP, None),
        P(DP, None),
    ) + (P(),) * 14 + (P(DP, None), P(DP, None))
    weight, vector = P(None, SECTION, DP), P(None, SECTION)
    out_specs = (
        P(DP, SECTION),
        P(DP, SECTION),
        P(DP, SECTION),
        P(DP, SECTION),
        P(None, DP, SECTION),
        weight,
        weight,
        weight,
        weight,
        P(None, None, SECTION),
        P(None, None, SECTION),
        vector,
        vector,
        weight,
        vector,
        weight,
        vector,
        vector,
        vector,
    )
    return jax.shard_map(
        on_device, mesh=mesh, in_specs=in_specs, out_specs=out_specs, check_vma=False
    )
```
